32 devices in a mesh: rep: 4 (over y, core), shard: 8 (over z, x).
Axes of the slice: x: 2, y: 2, z: 4, core: 2. Of those that a mesh axis runs over, the one named last changes fastest.
Arguments:
- tokens: bfloat16 [8192, 768], P(('rep', 'shard')), may hold values from -6 to 6
- cotangent: bfloat16 [8192, 768], P(('rep', 'shard')), may hold values from -6 to 6
- segments: int32 [8192], P(('rep', 'shard')), may hold values from 1 to 24, as said below
- qkv_weight: float32 [768, 2304], P('shard'), may hold values from -0.21875 to 0.21875
- out_weight: float32 [768, 768], P('shard'), may hold values from -0.875 to 0.875
- up_weight: float32 [768, 3072], P('shard'), may hold values from -0.21875 to 0.21875
- down_weight: float32 [3072, 768], P('shard'), may hold values from -0.109375 to 0.109375
- small_weights: float32 [12, 768], P(None, 'shard'), may hold values from -1.2 to 1.6
- qkv_first: float32 [768, 2304], P('shard'), may hold values from -64 to 64
- out_first: float32 [768, 768], P('shard'), may hold values from -16 to 16
- up_first: float32 [768, 3072], P('shard'), may hold values from -16 to 16
- down_first: float32 [3072, 768], P('shard'), may hold values from -40 to 40
- small_first: float32 [12, 768], P(None, 'shard'), may hold values from -40 to 40
- qkv_second: float32 [768, 2304], P('shard'), may hold values from 245.76 to 3276.8
- out_second: float32 [768, 768], P('shard'), may hold values from 16.384 to 204.8
- up_second: float32 [768, 3072], P('shard'), may hold values from 24.576 to 294.912
- down_second: float32 [3072, 768], P('shard'), may hold values from 106.496 to 1392.64
- small_second: float32 [12, 768], P(None, 'shard'), may hold values from 122.88 to 1638.4
Outputs:
- mixed: bfloat16 [8192, 768], P(('rep', 'shard'))
- input_grad: float32 [8192, 768], P(('rep', 'shard'))
- qkv_next: float32 [768, 2304], P('shard')
- out_next: float32 [768, 768], P('shard')
- up_next: float32 [768, 3072], P('shard')
- down_next: float32 [3072, 768], P('shard')
- small_next: float32 [12, 768], P(None, 'shard')
- qkv_first_next: float32 [768, 2304], P('shard')
- out_first_next: float32 [768, 768], P('shard')
- up_first_next: float32 [768, 3072], P('shard')
- down_first_next: float32 [3072, 768], P('shard')
- small_first_next: float32 [12, 768], P(None, 'shard')
- qkv_second_next: float32 [768, 2304], P('shard')
- out_second_next: float32 [768, 768], P('shard')
- up_second_next: float32 [768, 3072], P('shard')
- down_second_next: float32 [3072, 768], P('shard')
- small_second_next: float32 [12, 768], P(None, 'shard')
The draws below stay inside these ranges and needn't reach their ends.
Inputs may be any that keep to these rules, and one draw needn't show every extreme that they name: `segments`: rows are laid out as in the attention step: piece r of sequence s starts at row r * 2048 + s * 256. Along each sequence's positions the numbers never fall, and no two sequences share one; a document is a run of one number and holds at least 128 tokens; in every draw some sequence is a single document.
All inputs are finite; a program needn't handle non-finite values.
Results may differ from the reference program's by a relative error of at most 0.022.
Values may be sent and summed in bfloat16 or wider, within the bound.
No kernel may reach another device: no remote copies, remote signals or barrier semaphores. Data moves between devices by JAX's collectives and lax.ppermute only.
A program may use at most 192 MiB of HBM per device.

```python
import math
import jax
import jax.numpy as jnp
from jax import lax

HEAD_DIM = 64
D = 768
FF = 3072
SPAN = 4
STEP_NUM = 10
SEQ = 1024
TOKENS = 8192


def draw_small_weights(key, part):
    key = jax.random.fold_in(key, 11)
    gain_key, bias_key = jax.random.split(key)
    gains = jnp.exp(jax.random.uniform(gain_key, (12, D), jnp.float32, math.log(0.6), math.log(1.6)))
    biases = 0.3 * jnp.clip(jax.random.normal(bias_key, (12, D), jnp.float32), -4.0, 4.0)
    row_index = jnp.arange(12)[:, None]
    is_gain = (row_index == 0) | (row_index == 5)
    return jnp.where(is_gain, gains, biases).astype(jnp.float32)


def draw_segments(key, part):
    key = jax.random.fold_in(key, 23)
    sequences = TOKENS // SEQ
    subkeys = jax.random.split(key, 5)
    first_on = jax.random.randint(subkeys[0], (sequences,), 0, 2)
    second_on = jax.random.randint(subkeys[1], (sequences,), 0, 2)
    first_cut = jax.random.randint(subkeys[2], (sequences,), SEQ // 4, SEQ // 2)
    second_cut = jax.random.randint(subkeys[3], (sequences,), 5 * SEQ // 8, 7 * SEQ // 8)
    single_doc = jax.random.randint(subkeys[4], (), 0, sequences - 1)
    seq_index = jnp.arange(sequences)
    is_final = seq_index == sequences - 1
    first_on = jnp.where(is_final, 1, jnp.where(seq_index == single_doc, 0, first_on))
    second_on = jnp.where(is_final, 1, jnp.where(seq_index == single_doc, 0, second_on))
    places = jnp.arange(SEQ)
    passed = first_on[:, None] * (places[None, :] >= first_cut[:, None]).astype(jnp.int32)
    passed = passed + second_on[:, None] * (places[None, :] >= second_cut[:, None]).astype(jnp.int32)
    numbers = (seq_index[:, None] * 3 + passed + 1).astype(jnp.int32)
    laid_out = jnp.swapaxes(numbers.reshape(sequences, SPAN, SEQ // SPAN), 0, 1)
    return laid_out.reshape(TOKENS).astype(jnp.int32)


def steps_of(rng, dims, cuts, least, largest):
    def one(axis_at, parts):
        draws = jax.random.uniform(jax.random.fold_in(jax.random.fold_in(rng, 6), axis_at), (parts,), jnp.float32, least / len(cuts), largest / len(cuts))
        return jnp.repeat(jnp.exp(draws), dims[axis_at] // parts).reshape((-1,) + (1,) * (len(dims) - axis_at - 1))

    loudness = one(*cuts[0])
    for cut in cuts[1:]:
        loudness = loudness * one(*cut)
    return loudness


def noise(rng, dims, scale, bound, cuts=(), dtype=jnp.bfloat16):
    result = scale * jax.random.normal(rng, dims, jnp.float32)
    if cuts:
        result = result * steps_of(rng, dims, cuts, -0.22, 0.18)
    return jnp.clip(result, -bound, bound).astype(dtype)


def setup_inputs(seed: int = 0) -> dict:
    streams_of = jax.random.split(jax.random.key(seed), 19)
    tokens = noise(streams_of[0], (TOKENS, D), 1.0, 6.0, ((0, 32),))
    cotangent = noise(streams_of[1], (TOKENS, D), 1.0, 6.0, ((0, 32),))
    segments = draw_segments(jax.random.fold_in(streams_of[18], 71), 0)
    qkv_weight = noise(streams_of[3], (D, 3 * D), D ** -0.5, 0.21875, ((0, 8),), jnp.float32)
    out_weight = noise(streams_of[4], (D, D), (D // 16) ** -0.5, 0.875, ((0, 8),), jnp.float32)
    up_weight = noise(streams_of[5], (D, FF), D ** -0.5, 0.21875, ((0, 8),), jnp.float32)
    down_weight = noise(streams_of[6], (FF, D), FF ** -0.5, 0.109375, ((0, 8),), jnp.float32)
    small_weights = draw_small_weights(jax.random.fold_in(streams_of[18], 71), 0)
    qkv_first = noise(streams_of[8], (D, 3 * D), (0.11 * TOKENS ** 0.5), 64.0, ((0, 8),), jnp.float32)
    out_first = noise(streams_of[9], (D, D), (0.028 * TOKENS ** 0.5), 16.0, ((0, 8),), jnp.float32)
    up_first = noise(streams_of[10], (D, FF), (0.033 * TOKENS ** 0.5), 16.0, ((0, 8),), jnp.float32)
    down_first = noise(streams_of[11], (FF, D), (0.072 * TOKENS ** 0.5), 40.0, ((0, 8),), jnp.float32)
    small_first = noise(streams_of[12], (12, D), (0.077 * TOKENS ** 0.5), 40.0, ((1, 8),), jnp.float32)
    qkv_second = jnp.clip(jnp.exp(math.log(3276.8) - 2.5902672 * jax.random.uniform(streams_of[13], (D, 3 * D), jnp.float32) ** steps_of(streams_of[13], (D, 3 * D), ((0, 8),), -0.2, 0.2)), 245.76, 3276.8)
    out_second = jnp.clip(jnp.exp(math.log(204.8) - 2.5257286 * jax.random.uniform(streams_of[14], (D, D), jnp.float32) ** steps_of(streams_of[14], (D, D), ((0, 8),), -0.2, 0.2)), 16.384, 204.8)
    up_second = jnp.clip(jnp.exp(math.log(294.912) - 2.4849066 * jax.random.uniform(streams_of[15], (D, FF), jnp.float32) ** steps_of(streams_of[15], (D, FF), ((0, 8),), -0.2, 0.2)), 24.576, 294.912)
    down_second = jnp.clip(jnp.exp(math.log(1392.64) - 2.5708491 * jax.random.uniform(streams_of[16], (FF, D), jnp.float32) ** steps_of(streams_of[16], (FF, D), ((0, 8),), -0.2, 0.2)), 106.496, 1392.64)
    small_second = jnp.clip(jnp.exp(math.log(1638.4) - 2.5902672 * jax.random.uniform(streams_of[17], (12, D), jnp.float32) ** steps_of(streams_of[17], (12, D), ((1, 8),), -0.2, 0.2)), 122.88, 1638.4)
    return {"tokens": tokens, "cotangent": cotangent, "segments": segments, "qkv_weight": qkv_weight, "out_weight": out_weight, "up_weight": up_weight, "down_weight": down_weight, "small_weights": small_weights, "qkv_first": qkv_first, "out_first": out_first, "up_first": up_first, "down_first": down_first, "small_first": small_first, "qkv_second": qkv_second, "out_second": out_second, "up_second": up_second, "down_second": down_second, "small_second": small_second}


NORM_EPS = 1e-05
BETA_ONE = 0.9
BETA_TWO = 0.95
ADAM_EPS = 1e-08
DECAY = 0.1
RATE_MATRIX = 0.05
RATE_SMALL = 0.3
MASKED = -1e+30

@jax.custom_vjp
def low(v):
    return lax.optimization_barrier(v.astype(jnp.bfloat16)).astype(jnp.float32)

@jax.custom_vjp
def low_back(v):
    return v

def low_keep(v):
    return (low(v), None)

def low_pass(kept, grad):
    return (grad,)

def back_keep(v):
    return (v, None)

def back_low(kept, grad):
    return (low(grad),)
low.defvjp(low_keep, low_pass)
low_back.defvjp(back_keep, back_low)

def product(left_side, right_side):
    return jnp.dot(left_side, right_side, precision=lax.Precision.HIGHEST, preferred_element_type=jnp.float32)

def layer_norm(values, gain_row, bias_row):
    center = lax.optimization_barrier(jnp.mean(values, axis=-1, keepdims=True))
    centered = values - center
    variance = lax.optimization_barrier(jnp.mean(centered * centered, axis=-1, keepdims=True))
    return centered * lax.rsqrt(variance + NORM_EPS) * gain_row + bias_row

def unpack(packed):
    return (packed[0], packed[1], packed[2], packed[3], packed[4], packed[5], packed[6], packed[7], packed[8:].reshape(-1))

def attend(pieces):
    query_part, key_part, value_part, seg_ids = pieces
    scores = low_back(jnp.einsum('qhd,khd->hqk', query_part, key_part, precision=lax.Precision.HIGHEST))
    places = jnp.arange(seg_ids.shape[0])
    allowed = (seg_ids[:, None] == seg_ids[None, :]) & (places[None, :] <= places[:, None])
    attn_probs = jax.nn.softmax(jnp.where(allowed[None], scores, MASKED), axis=-1)
    return jnp.einsum('hqk,khd->qhd', low(attn_probs), value_part, precision=lax.Precision.HIGHEST)

def forward(inputs, seg_ids, qkv_weight, out_weight, up_weight, down_weight, small_weights):
    row_count = inputs.shape[0]
    model_width = inputs.shape[1]
    head_count = model_width // HEAD_DIM
    gain_one, bias_one, query_bias, value_bias, out_bias, gain_two, bias_two, down_bias, up_bias = unpack(low(small_weights))
    normed = low(layer_norm(inputs, gain_one, bias_one))
    joined_bias = jnp.concatenate([query_bias, jnp.zeros_like(query_bias), value_bias])
    projected = low_back(product(normed, low(qkv_weight)) + joined_bias)
    queries = low(projected[:, :model_width] * HEAD_DIM ** (-0.5))
    key_rows = low(projected[:, model_width:2 * model_width])
    value_rows = low(projected[:, 2 * model_width:])

    def per_seq(values):
        return values.reshape(seg_ids.shape[0], seg_ids.shape[1], head_count, HEAD_DIM)
    mixed_heads = lax.map(jax.checkpoint(attend), (per_seq(queries), per_seq(key_rows), per_seq(value_rows), seg_ids))
    attended = low(low_back(mixed_heads.reshape(row_count, model_width)))
    residual = inputs + low_back(product(attended, low(out_weight)) + out_bias)
    hidden = low(layer_norm(residual, gain_two, bias_two))
    pre_act = low_back(product(hidden, low(up_weight)) + up_bias)
    activated = low(jax.nn.gelu(pre_act, approximate=False))
    return residual + low_back(product(activated, low(down_weight)) + down_bias)

def adam_update(master, gradient, moment_one, moment_two, step_rate):
    first_new = BETA_ONE * moment_one + (1.0 - BETA_ONE) * gradient
    second_new = BETA_TWO * moment_two + (1.0 - BETA_TWO) * gradient * gradient
    fix_one = 1.0 - BETA_ONE ** STEP_NUM
    fix_two = 1.0 - BETA_TWO ** STEP_NUM
    step_dir = first_new / fix_one / (jnp.sqrt(second_new / fix_two) + ADAM_EPS)
    return (master - step_rate * (step_dir + DECAY * master), first_new, second_new)

def to_sequences(values, width):
    sequences = TOKENS // SEQ
    return jnp.swapaxes(values.reshape(SPAN, sequences, SEQ // SPAN, width), 0, 1).reshape(TOKENS, width)

def from_sequences(values, width):
    sequences = TOKENS // SEQ
    return jnp.swapaxes(values.reshape(sequences, SPAN, SEQ // SPAN, width), 0, 1).reshape(TOKENS, width)

def reference(tokens, cotangent, segments, qkv_weight, out_weight, up_weight, down_weight, small_weights, qkv_first, out_first, up_first, down_first, small_first, qkv_second, out_second, up_second, down_second, small_second):
    sequences = TOKENS // SEQ
    group_seqs = math.gcd(sequences, max(1, 4096 // SEQ))
    turn_count = sequences // group_seqs
    inputs = to_sequences(tokens.astype(jnp.float32), D).reshape(turn_count, group_seqs * SEQ, D)
    grads_in = to_sequences(cotangent.astype(jnp.float32), D).reshape(turn_count, group_seqs * SEQ, D)
    seg_all = to_sequences(segments.reshape(TOKENS, 1), 1).reshape(turn_count, group_seqs, SEQ)
    params = (qkv_weight, out_weight, up_weight, down_weight, small_weights)

    def one_turn(totals, scan_item):
        block_in, block_grad, block_ids = scan_item

        def apply_layer(values, w_qkv, w_out, w_up, w_down, w_small):
            return forward(values, block_ids, w_qkv, w_out, w_up, w_down, w_small)
        output, pull_back = jax.vjp(apply_layer, block_in, qkv_weight, out_weight, up_weight, down_weight, small_weights)
        gradients = pull_back(block_grad)
        totals = jax.tree.map(jnp.add, totals, tuple(gradients[1:]))
        return (totals, (output, gradients[0]))
    zero_sums = jax.tree.map(jnp.zeros_like, params)
    totals, (outputs, input_grads) = lax.scan(one_turn, zero_sums, (inputs, grads_in, seg_all))
    mixed = from_sequences(outputs.reshape(TOKENS, D), D).astype(jnp.bfloat16)
    input_grad = from_sequences(input_grads.reshape(TOKENS, D), D)
    qkv_res = adam_update(qkv_weight, totals[0], qkv_first, qkv_second, RATE_MATRIX)
    out_res = adam_update(out_weight, totals[1], out_first, out_second, RATE_MATRIX)
    up_res = adam_update(up_weight, totals[2], up_first, up_second, RATE_MATRIX)
    down_res = adam_update(down_weight, totals[3], down_first, down_second, RATE_MATRIX)
    small_res = adam_update(small_weights, totals[4], small_first, small_second, RATE_SMALL)
    return (mixed, input_grad, qkv_res[0], out_res[0], up_res[0], down_res[0], small_res[0], qkv_res[1], out_res[1], up_res[1], down_res[1], small_res[1], qkv_res[2], out_res[2], up_res[2], down_res[2], small_res[2])
```

```python
import jax
import jax.numpy as jnp
from jax import lax
from jax.experimental import pallas as pl
from jax.experimental.pallas import tpu as pltpu
from jax.sharding import PartitionSpec as P

HEAD_DIM = 64
SPAN = 4
STEP_NUM = 10


NORM_EPS = 1e-05
BETA_ONE = 0.9
BETA_TWO = 0.95
ADAM_EPS = 1e-08
DECAY = 0.1
RATE_MATRIX = 0.05
RATE_SMALL = 0.3
MASKED = -1e30
BLOCK = 256
F32 = jnp.float32
BF16 = jnp.bfloat16


def swapped(block, bit):
    return lax.ppermute(block, "rep", [(i, i ^ bit) for i in range(SPAN)])


def rep_gather(block):
    rep = lax.axis_index("rep")
    far = swapped(block, 2)
    near = swapped(block, 1)
    cross = swapped(far, 1)
    odd = (rep & 1) == 1
    high = (rep & 2) == 2
    low_pair = (jnp.where(odd, near, block), jnp.where(odd, block, near))
    high_pair = (jnp.where(odd, cross, far), jnp.where(odd, far, cross))
    return (
        jnp.where(high, high_pair[0], low_pair[0]),
        jnp.where(high, high_pair[1], low_pair[1]),
        jnp.where(high, low_pair[0], high_pair[0]),
        jnp.where(high, low_pair[1], high_pair[1]),
    )


def rep_scatter(partial):
    rep = lax.axis_index("rep")
    rows = partial.shape[0] // SPAN

    def piece(index):
        return lax.dynamic_slice_in_dim(partial, index * rows, rows, 0)

    near_send = jnp.concatenate([piece(rep ^ 3), piece(rep ^ 1)], axis=0).astype(BF16)
    near = swapped(near_send, 1).astype(F32)
    far_send = (piece(rep ^ 2) + near[:rows]).astype(BF16)
    return piece(rep) + near[rows:] + swapped(far_send, 2).astype(F32)


def norm_parts(values):
    center = jnp.mean(values, axis=-1, keepdims=True)
    centered = values - center
    variance = jnp.mean(centered * centered, axis=-1, keepdims=True)
    inverse = lax.rsqrt(variance + NORM_EPS)
    return centered * inverse, inverse


def norm_back(normalized, inverse, gain, grad):
    scaled = grad * gain
    mean_one = jnp.mean(scaled, axis=-1, keepdims=True)
    mean_two = jnp.mean(scaled * normalized, axis=-1, keepdims=True)
    return inverse * (scaled - mean_one - normalized * mean_two)


def contract_rows(left_side, right_side):
    return lax.dot_general(
        left_side, right_side, (((0,), (0,)), ((), ())), preferred_element_type=F32
    )


def contract_cols(left_side, right_side):
    return lax.dot_general(
        left_side, right_side, (((1,), (1,)), ((), ())), preferred_element_type=F32
    )


def adam_update(master, gradient, moment_one, moment_two, step_rate):
    first_new = BETA_ONE * moment_one + (1.0 - BETA_ONE) * gradient
    second_new = BETA_TWO * moment_two + (1.0 - BETA_TWO) * gradient * gradient
    fix_one = 1.0 - BETA_ONE**STEP_NUM
    fix_two = 1.0 - BETA_TWO**STEP_NUM
    step_dir = first_new / fix_one / (jnp.sqrt(second_new / fix_two) + ADAM_EPS)
    return (master - step_rate * (step_dir + DECAY * master), first_new, second_new)


def mask_bias(seg_col_ref, seg_row_ref, start, keys):
    same = seg_col_ref[:keys, :] == seg_row_ref[:, start : start + BLOCK]
    key_at = lax.broadcasted_iota(jnp.int32, (keys, BLOCK), 0)
    query_at = lax.broadcasted_iota(jnp.int32, (keys, BLOCK), 1) + start
    return jnp.where(same & (key_at <= query_at), 0.0, MASKED)


def head_lanes(shape, head):
    lane = lax.broadcasted_iota(jnp.int32, shape, 1)
    return (lane >= head * HEAD_DIM) & (lane < (head + 1) * HEAD_DIM)


def attend_kernel(q_ref, k_ref, v_ref, seg_col_ref, seg_row_ref, out_ref, lse_ref):
    total, width = q_ref.shape
    heads = width // HEAD_DIM
    value_t = v_ref[...].T
    lse_ref[...] = jnp.zeros_like(lse_ref)
    for start in range(0, total, BLOCK):
        keys = start + BLOCK
        bias = mask_bias(seg_col_ref, seg_row_ref, start, keys)
        query = q_ref[start : start + BLOCK, :]
        pieces = []
        for head in range(heads):
            masked = jnp.where(head_lanes(query.shape, head), query, 0)
            scores = contract_cols(k_ref[:keys, :], masked) + bias
            peak = jnp.max(scores, axis=0, keepdims=True)
            exponent = jnp.exp(scores - peak)
            row_total = jnp.sum(exponent, axis=0, keepdims=True)
            mixed = jnp.dot(
                value_t[head * HEAD_DIM : (head + 1) * HEAD_DIM, :keys],
                exponent.astype(BF16),
                preferred_element_type=F32,
            )
            pieces.append(mixed / row_total)
            lse_ref[head : head + 1, start : start + BLOCK] = peak + jnp.log(row_total)
        out_ref[start : start + BLOCK, :] = jnp.concatenate(pieces, axis=0).T.astype(BF16)


def attend_back_kernel(
    q_ref, k_ref, v_ref, do_ref, lse_ref, seg_col_ref, seg_row_ref, grad_ref, dk_ref, dv_ref
):
    total, width = q_ref.shape
    heads = width // HEAD_DIM
    key_t = k_ref[...].T
    dk_ref[...] = jnp.zeros_like(dk_ref)
    dv_ref[...] = jnp.zeros_like(dv_ref)
    for start in range(0, total, BLOCK):
        keys = start + BLOCK
        bias = mask_bias(seg_col_ref, seg_row_ref, start, keys)
        query = q_ref[start : start + BLOCK, :]
        grad = do_ref[start : start + BLOCK, :]
        pieces = []
        dk = dk_ref[:keys, :]
        dv = dv_ref[:keys, :]
        for head in range(heads):
            lanes = head_lanes(query.shape, head)
            query_h = jnp.where(lanes, query, 0)
            grad_h = jnp.where(lanes, grad, 0)
            scores = contract_cols(k_ref[:keys, :], query_h) + bias
            probs = jnp.exp(scores - lse_ref[head : head + 1, start : start + BLOCK])
            prob_grad = contract_cols(v_ref[:keys, :], grad_h)
            inner = jnp.sum(prob_grad * probs, axis=0, keepdims=True)
            score_grad = (probs * (prob_grad - inner)).astype(BF16)
            dv = dv + jnp.dot(probs.astype(BF16), grad_h, preferred_element_type=F32)
            dk = dk + jnp.dot(score_grad, query_h, preferred_element_type=F32)
            pieces.append(
                jnp.dot(
                    key_t[head * HEAD_DIM : (head + 1) * HEAD_DIM, :keys],
                    score_grad,
                    preferred_element_type=F32,
                )
            )
        dk_ref[:keys, :] = dk
        dv_ref[:keys, :] = dv
        dq = jnp.concatenate(pieces, axis=0).T * HEAD_DIM ** (-0.5)
        grad_ref[start : start + BLOCK, :width] = dq.astype(BF16)
    grad_ref[:, width : 2 * width] = dk_ref[...].astype(BF16)
    grad_ref[:, 2 * width :] = dv_ref[...].astype(BF16)


def whole_specs(count):
    return [pl.BlockSpec(memory_space=pltpu.VMEM) for _ in range(count)]


def attend(query, key, value, seg_col, seg_row):
    total, width = query.shape
    return pl.pallas_call(
        attend_kernel,
        out_shape=(
            jax.ShapeDtypeStruct((total, width), BF16),
            jax.ShapeDtypeStruct((8, total), F32),
        ),
        in_specs=whole_specs(5),
        out_specs=tuple(whole_specs(2)),
        compiler_params=pltpu.CompilerParams(vmem_limit_bytes=48 * 2**20),
        cost_estimate=pl.CostEstimate(
            flops=2 * 2 * total * total * width,
            bytes_accessed=8 * total * width,
            transcendentals=total * total * width // HEAD_DIM // 2,
        ),
    )(query, key, value, seg_col, seg_row)


def attend_back(query, key, value, grad, lse, seg_col, seg_row):
    total, width = query.shape
    return pl.pallas_call(
        attend_back_kernel,
        out_shape=jax.ShapeDtypeStruct((total, 3 * width), BF16),
        in_specs=whole_specs(7),
        out_specs=whole_specs(1)[0],
        scratch_shapes=[pltpu.VMEM((total, width), F32), pltpu.VMEM((total, width), F32)],
        compiler_params=pltpu.CompilerParams(vmem_limit_bytes=48 * 2**20),
        cost_estimate=pl.CostEstimate(
            flops=5 * 2 * total * total * width,
            bytes_accessed=14 * total * width,
            transcendentals=total * total * width // HEAD_DIM // 2,
        ),
    )(query, key, value, grad, lse, seg_col, seg_row)


def local(
    tokens,
    cotangent,
    segments,
    qkv_weight,
    out_weight,
    up_weight,
    down_weight,
    small_weights,
    qkv_first,
    out_first,
    up_first,
    down_first,
    small_first,
    qkv_second,
    out_second,
    up_second,
    down_second,
    small_second,
):
    rep = lax.axis_index("rep")
    shard = lax.axis_index("shard")
    shards = lax.axis_size("shard")
    tok_rows, width = tokens.shape
    part = width // SPAN
    owned = qkv_weight.shape[0]
    ff = up_weight.shape[1]
    unit_rows = down_weight.shape[0]
    units = unit_rows // SPAN
    score_scale = HEAD_DIM ** (-0.5)

    def rep_part(block, size, axis):
        return lax.dynamic_slice_in_dim(block, rep * size, size, axis)

    low_small = small_weights.astype(BF16).T
    low_qkv = rep_part(qkv_weight.astype(BF16).reshape(owned, 3, SPAN, part), 1, 2)
    low_qkv = low_qkv.reshape(owned, 3 * part)
    pad = 64 - low_small.shape[1]
    first_send = jnp.concatenate([low_qkv, jnp.pad(low_small, ((0, 0), (0, pad)))], axis=1)
    low_out = out_weight.astype(BF16)
    low_up = rep_part(up_weight.astype(BF16).reshape(owned, shards, SPAN, units), 1, 2)
    low_up = low_up.reshape(owned, ff // SPAN)
    low_down = rep_part(down_weight, units, 0).astype(BF16)
    first_full = lax.all_gather(first_send, "shard", axis=0, tiled=True)
    out_full = lax.all_gather(low_out, "shard", axis=0, tiled=True)
    up_part = lax.all_gather(low_up, "shard", axis=0, tiled=True)
    down_part = lax.all_gather(low_down, "shard", axis=0, tiled=True)
    qkv_part = first_full[:, : 3 * part]
    small_full = first_full[:, 3 * part : 3 * part + 12].T.astype(F32)
    gain_one, bias_one, query_bias, value_bias, out_bias, gain_two, bias_two, down_bias = (
        small_full[:8]
    )
    up_bias = rep_part(small_full[8:].reshape(shards, SPAN, units), 1, 1).reshape(-1)

    seg_rows = -(-tok_rows // width)
    seg_block = jnp.pad(segments.astype(BF16), (0, seg_rows * width - tok_rows))
    seg_block = jnp.pad(seg_block.reshape(seg_rows, width), ((0, 16 - seg_rows), (0, 0)))
    with_seg = rep_gather(jnp.concatenate([tokens, seg_block], axis=0))
    all_tokens = jnp.concatenate([block[:tok_rows] for block in with_seg], axis=0)
    all_segs = jnp.concatenate(
        [block[tok_rows : tok_rows + seg_rows].reshape(-1)[:tok_rows] for block in with_seg]
    ).astype(jnp.int32)
    seg_col, seg_row = all_segs[:, None], all_segs[None, :]
    all_cot = jnp.concatenate(rep_gather(cotangent), axis=0)

    inputs = all_tokens.astype(F32)
    norm_one, inverse_one = norm_parts(inputs)
    hidden_one = (norm_one * gain_one + bias_one).astype(BF16)
    query_bias_part = rep_part(query_bias, part, 0)
    value_bias_part = rep_part(value_bias, part, 0)
    joined_bias = jnp.concatenate(
        [query_bias_part, jnp.zeros_like(query_bias_part), value_bias_part]
    )
    projected = jnp.dot(hidden_one, qkv_part, preferred_element_type=F32) + joined_bias
    queries = (projected[:, :part] * score_scale).astype(BF16)
    keys = projected[:, part : 2 * part].astype(BF16)
    values = projected[:, 2 * part :].astype(BF16)
    attended_part, log_total = attend(queries, keys, values, seg_col, seg_row)
    attended = jnp.concatenate(rep_gather(attended_part), axis=1)
    residual = inputs + (jnp.dot(attended, out_full, preferred_element_type=F32) + out_bias)
    norm_two, inverse_two = norm_parts(residual)
    hidden_two = (norm_two * gain_two + bias_two).astype(BF16)
    pre_act = jnp.dot(hidden_two, up_part, preferred_element_type=F32) + up_bias
    cdf = 0.5 * (1.0 + lax.erf(pre_act * (0.5**0.5)))
    act_low = (pre_act * cdf).astype(BF16)
    slope = cdf + pre_act * (jnp.exp(-0.5 * pre_act * pre_act) * 0.3989422804014327)
    pre_low = (contract_cols(all_cot, down_part) * slope).astype(BF16)
    hidden_two_grad = rep_scatter(contract_cols(pre_low, up_part))
    mixed_sum = rep_scatter(jnp.dot(act_low, down_part, preferred_element_type=F32))
    residual_own = rep_part(residual, tok_rows, 0)
    mixed = (residual_own + (mixed_sum + down_bias)).astype(BF16)
    down_grad = contract_rows(act_low, all_cot)
    up_grad = contract_rows(hidden_two, pre_low)
    up_bias_grad = jnp.sum(pre_low.astype(F32), axis=0)

    norm_two_own = rep_part(norm_two, tok_rows, 0)
    grad_own = cotangent.astype(F32)
    gain_two_grad = jnp.sum(hidden_two_grad * norm_two_own, axis=0)
    bias_two_grad = jnp.sum(hidden_two_grad, axis=0)
    resid_grad = grad_own + norm_back(
        norm_two_own, rep_part(inverse_two, tok_rows, 0), gain_two, hidden_two_grad
    )
    branch_own = resid_grad.astype(BF16)
    out_bias_grad = jnp.sum(branch_own.astype(F32), axis=0)
    branch_low = jnp.concatenate(rep_gather(branch_own), axis=0)
    out_grad = contract_rows(attended, rep_part(branch_low, part, 1))
    attended_grad = contract_cols(branch_low, rep_part(out_full, part, 0)).astype(BF16)
    proj_low = attend_back(queries, keys, values, attended_grad, log_total, seg_col, seg_row)
    proj_sums = jnp.sum(proj_low.astype(F32), axis=0)
    qkv_grad = contract_rows(hidden_one, proj_low)
    hidden_one_part = contract_cols(proj_low, qkv_part)
    gain_one_grad = jnp.sum(hidden_one_part * norm_one, axis=0)
    bias_one_grad = jnp.sum(hidden_one_part, axis=0)
    hidden_one_grad = rep_scatter(hidden_one_part)
    input_grad = resid_grad + norm_back(
        rep_part(norm_one, tok_rows, 0),
        rep_part(inverse_one, tok_rows, 0),
        gain_one,
        hidden_one_grad,
    )

    def placed(values_part, size, parts_before):
        blank = jnp.zeros((parts_before, SPAN, size), F32)
        return lax.dynamic_update_slice(
            blank, values_part.reshape(parts_before, 1, size), (0, rep, 0)
        ).reshape(-1)

    vector_grads = jnp.stack(
        [
            gain_one_grad,
            bias_one_grad,
            placed(proj_sums[:part], part, 1),
            placed(proj_sums[2 * part :], part, 1),
            out_bias_grad,
            gain_two_grad,
            bias_two_grad,
            jnp.sum(grad_own, axis=0),
        ]
    )
    small_grad = jnp.concatenate(
        [vector_grads, placed(up_bias_grad, units, shards).reshape(-1, width)], axis=0
    )
    small_sum = lax.psum(small_grad, ("rep", "shard"))
    small_own = lax.dynamic_slice_in_dim(
        small_sum, shard * small_weights.shape[1], small_weights.shape[1], 1
    )

    def owned_sum(gradient):
        low = gradient.astype(BF16)
        return rep_gather(lax.psum_scatter(low, "shard", scatter_dimension=0, tiled=True))

    down_own = jnp.concatenate(owned_sum(down_grad), axis=0).astype(F32)
    up_own = jnp.stack([g.reshape(owned, shards, units) for g in owned_sum(up_grad)], axis=2)
    up_own = up_own.reshape(owned, ff).astype(F32)
    out_own = jnp.concatenate(owned_sum(out_grad), axis=1).astype(F32)
    qkv_own = jnp.stack([g.reshape(owned, 3, part) for g in owned_sum(qkv_grad)], axis=2)
    qkv_own = qkv_own.reshape(owned, 3 * width).astype(F32)
    qkv_res = adam_update(qkv_weight, qkv_own, qkv_first, qkv_second, RATE_MATRIX)
    out_res = adam_update(out_weight, out_own, out_first, out_second, RATE_MATRIX)
    up_res = adam_update(up_weight, up_own, up_first, up_second, RATE_MATRIX)
    down_res = adam_update(down_weight, down_own, down_first, down_second, RATE_MATRIX)
    small_res = adam_update(small_weights, small_own, small_first, small_second, RATE_SMALL)
    return (
        mixed,
        input_grad,
        qkv_res[0],
        out_res[0],
        up_res[0],
        down_res[0],
        small_res[0],
        qkv_res[1],
        out_res[1],
        up_res[1],
        down_res[1],
        small_res[1],
        qkv_res[2],
        out_res[2],
        up_res[2],
        down_res[2],
        small_res[2],
    )


def solution(mesh):
    tokens_spec = P(("rep", "shard"), None)
    rows = P("shard", None)
    columns = P(None, "shard")
    weights = (rows, rows, rows, rows, columns)
    return jax.shard_map(
        local,
        mesh=mesh,
        in_specs=(tokens_spec, tokens_spec, P(("rep", "shard"))) + weights * 3,
        out_specs=(tokens_spec, tokens_spec) + weights * 3,
        check_vma=False,
    )
```

```python
import jax
import jax.numpy as jnp
from jax import lax
from jax.experimental import pallas as pl
from jax.experimental.pallas import tpu as pltpu
from jax.sharding import PartitionSpec as P

HEAD_DIM = 64
SPAN = 4
STEP_NUM = 10


NORM_EPS = 1e-05
BETA_ONE = 0.9
BETA_TWO = 0.95
ADAM_EPS = 1e-08
DECAY = 0.1
RATE_MATRIX = 0.05
RATE_SMALL = 0.3
MASKED = -1e30
BLOCK = 256
FEW = 8
F32 = jnp.float32
BF16 = jnp.bfloat16


def swapped(block, bit):
    return lax.ppermute(block, "rep", [(i, i ^ bit) for i in range(SPAN)])


def rep_gather(block):
    rep = lax.axis_index("rep")
    far = swapped(block, 2)
    near = swapped(block, 1)
    cross = swapped(far, 1)
    odd = (rep & 1) == 1
    high = (rep & 2) == 2
    low_pair = (jnp.where(odd, near, block), jnp.where(odd, block, near))
    high_pair = (jnp.where(odd, cross, far), jnp.where(odd, far, cross))
    return (
        jnp.where(high, high_pair[0], low_pair[0]),
        jnp.where(high, high_pair[1], low_pair[1]),
        jnp.where(high, low_pair[0], high_pair[0]),
        jnp.where(high, low_pair[1], high_pair[1]),
    )


def rep_scatter(partial):
    rep = lax.axis_index("rep")
    rows = partial.shape[0] // SPAN

    def piece(index):
        return lax.dynamic_slice_in_dim(partial, index * rows, rows, 0)

    near_send = jnp.concatenate([piece(rep ^ 3), piece(rep ^ 1)], axis=0).astype(BF16)
    near = swapped(near_send, 1).astype(F32)
    far_send = (piece(rep ^ 2) + near[:rows]).astype(BF16)
    return piece(rep) + near[rows:] + swapped(far_send, 2).astype(F32)


def swap_low(block):
    return lax.ppermute(block, "shard", [(i, i ^ 1) for i in range(lax.axis_size("shard"))])


def shard_gather(block):
    shards = lax.axis_size("shard")
    if shards > FEW:
        return lax.all_gather(block, "shard", axis=0, tiled=True), block
    shard = lax.axis_index("shard")
    high, low = shard // 2, shard % 2
    count = shards // 2
    ring = [0] + list(range(1, count, 2)) + list(range(count - 2, 0, -2))
    route = []
    for place, here in enumerate(ring):
        there = ring[(place + 1) % count]
        route += [(2 * here, 2 * there), (2 * here + 1, 2 * there + 1)]
    full = jnp.zeros((shards,) + block.shape, block.dtype)
    for step in range(count):
        source = [0] * count
        for place, here in enumerate(ring):
            source[here] = ring[place - step]
        index = jnp.array(source, jnp.int32)[high]
        other = swap_low(block)
        full = lax.dynamic_update_index_in_dim(full, block, 2 * index + low, 0)
        full = lax.dynamic_update_index_in_dim(full, other, 2 * index + 1 - low, 0)
        if step < count - 1:
            block = lax.ppermute(block, "shard", route)
    return full.reshape((-1,) + block.shape[1:]), block


def shard_scatter(partial):
    shards = lax.axis_size("shard")
    if shards > FEW:
        low = partial.astype(BF16)
        return lax.psum_scatter(low, "shard", scatter_dimension=0, tiled=True).astype(F32)
    shard = lax.axis_index("shard")
    high, low = shard // 2, shard % 2
    count = shards // 2
    blocks = partial.reshape(count, 2, partial.shape[0] // shards, partial.shape[1])
    sent = lax.dynamic_index_in_dim(blocks, 1 - low, 1, keepdims=False).astype(BF16)
    halves = lax.dynamic_index_in_dim(blocks, low, 1, keepdims=False)
    halves = halves + swap_low(sent).astype(F32)
    total = lax.dynamic_index_in_dim(halves, high, 0, keepdims=False)
    for bits in range(1, count):
        sent = lax.dynamic_index_in_dim(halves, high ^ bits, 0, keepdims=False).astype(BF16)
        route = [(i, i ^ (2 * bits)) for i in range(shards)]
        total = total + lax.ppermute(sent, "shard", route).astype(F32)
    return total


def after(block, other):
    return lax.optimization_barrier((block, other))[0]


def norm_parts(values):
    center = jnp.mean(values, axis=-1, keepdims=True)
    centered = values - center
    variance = jnp.mean(centered * centered, axis=-1, keepdims=True)
    inverse = lax.rsqrt(variance + NORM_EPS)
    return centered * inverse, inverse


def norm_back(normalized, inverse, gain, grad):
    scaled = grad * gain
    mean_one = jnp.mean(scaled, axis=-1, keepdims=True)
    mean_two = jnp.mean(scaled * normalized, axis=-1, keepdims=True)
    return inverse * (scaled - mean_one - normalized * mean_two)


def contract_rows(left_side, right_side):
    return lax.dot_general(
        left_side, right_side, (((0,), (0,)), ((), ())), preferred_element_type=F32
    )


def contract_cols(left_side, right_side):
    return lax.dot_general(
        left_side, right_side, (((1,), (1,)), ((), ())), preferred_element_type=F32
    )


def adam_update(master, gradient, moment_one, moment_two, step_rate):
    first_new = BETA_ONE * moment_one + (1.0 - BETA_ONE) * gradient
    second_new = BETA_TWO * moment_two + (1.0 - BETA_TWO) * gradient * gradient
    fix_one = 1.0 - BETA_ONE**STEP_NUM
    fix_two = 1.0 - BETA_TWO**STEP_NUM
    step_dir = first_new / fix_one / (jnp.sqrt(second_new / fix_two) + ADAM_EPS)
    return (master - step_rate * (step_dir + DECAY * master), first_new, second_new)


def mask_bias(seg_col_ref, seg_row_ref, start, keys):
    same = seg_col_ref[:keys, :] == seg_row_ref[:, start : start + BLOCK]
    key_at = lax.broadcasted_iota(jnp.int32, (keys, BLOCK), 0)
    query_at = lax.broadcasted_iota(jnp.int32, (keys, BLOCK), 1) + start
    return jnp.where(same & (key_at <= query_at), 0.0, MASKED)


def head_lanes(shape, head):
    lane = lax.broadcasted_iota(jnp.int32, shape, 1)
    return (lane >= head * HEAD_DIM) & (lane < (head + 1) * HEAD_DIM)


def attend_kernel(q_ref, k_ref, v_ref, seg_col_ref, seg_row_ref, out_ref, lse_ref):
    total, width = q_ref.shape
    heads = width // HEAD_DIM
    value_t = v_ref[...].T
    lse_ref[...] = jnp.zeros_like(lse_ref)
    for start in range(0, total, BLOCK):
        keys = start + BLOCK
        bias = mask_bias(seg_col_ref, seg_row_ref, start, keys)
        query = q_ref[start : start + BLOCK, :]
        pieces = []
        for head in range(heads):
            masked = jnp.where(head_lanes(query.shape, head), query, 0)
            scores = contract_cols(k_ref[:keys, :], masked) + bias
            peak = jnp.max(scores, axis=0, keepdims=True)
            exponent = jnp.exp(scores - peak)
            row_total = jnp.sum(exponent, axis=0, keepdims=True)
            mixed = jnp.dot(
                value_t[head * HEAD_DIM : (head + 1) * HEAD_DIM, :keys],
                exponent.astype(BF16),
                preferred_element_type=F32,
            )
            pieces.append(mixed / row_total)
            lse_ref[head : head + 1, start : start + BLOCK] = peak + jnp.log(row_total)
        out_ref[start : start + BLOCK, :] = jnp.concatenate(pieces, axis=0).T.astype(BF16)


def attend_back_kernel(
    q_ref, k_ref, v_ref, do_ref, lse_ref, seg_col_ref, seg_row_ref, grad_ref, dk_ref, dv_ref
):
    total, width = q_ref.shape
    heads = width // HEAD_DIM
    key_t = k_ref[...].T
    dk_ref[...] = jnp.zeros_like(dk_ref)
    dv_ref[...] = jnp.zeros_like(dv_ref)
    for start in range(0, total, BLOCK):
        keys = start + BLOCK
        bias = mask_bias(seg_col_ref, seg_row_ref, start, keys)
        query = q_ref[start : start + BLOCK, :]
        grad = do_ref[start : start + BLOCK, :]
        pieces = []
        dk = dk_ref[:keys, :]
        dv = dv_ref[:keys, :]
        for head in range(heads):
            lanes = head_lanes(query.shape, head)
            query_h = jnp.where(lanes, query, 0)
            grad_h = jnp.where(lanes, grad, 0)
            scores = contract_cols(k_ref[:keys, :], query_h) + bias
            probs = jnp.exp(scores - lse_ref[head : head + 1, start : start + BLOCK])
            prob_grad = contract_cols(v_ref[:keys, :], grad_h)
            inner = jnp.sum(prob_grad * probs, axis=0, keepdims=True)
            score_grad = (probs * (prob_grad - inner)).astype(BF16)
            dv = dv + jnp.dot(probs.astype(BF16), grad_h, preferred_element_type=F32)
            dk = dk + jnp.dot(score_grad, query_h, preferred_element_type=F32)
            pieces.append(
                jnp.dot(
                    key_t[head * HEAD_DIM : (head + 1) * HEAD_DIM, :keys],
                    score_grad,
                    preferred_element_type=F32,
                )
            )
        dk_ref[:keys, :] = dk
        dv_ref[:keys, :] = dv
        dq = jnp.concatenate(pieces, axis=0).T * HEAD_DIM ** (-0.5)
        grad_ref[start : start + BLOCK, :width] = dq.astype(BF16)
    grad_ref[:, width : 2 * width] = dk_ref[...].astype(BF16)
    grad_ref[:, 2 * width :] = dv_ref[...].astype(BF16)


def whole_specs(count):
    return [pl.BlockSpec(memory_space=pltpu.VMEM) for _ in range(count)]


def attend(query, key, value, seg_col, seg_row):
    total, width = query.shape
    return pl.pallas_call(
        attend_kernel,
        out_shape=(
            jax.ShapeDtypeStruct((total, width), BF16),
            jax.ShapeDtypeStruct((8, total), F32),
        ),
        in_specs=whole_specs(5),
        out_specs=tuple(whole_specs(2)),
        compiler_params=pltpu.CompilerParams(vmem_limit_bytes=48 * 2**20),
        cost_estimate=pl.CostEstimate(
            flops=2 * 2 * total * total * width,
            bytes_accessed=8 * total * width,
            transcendentals=total * total * width // HEAD_DIM // 2,
        ),
    )(query, key, value, seg_col, seg_row)


def attend_back(query, key, value, grad, lse, seg_col, seg_row):
    total, width = query.shape
    return pl.pallas_call(
        attend_back_kernel,
        out_shape=jax.ShapeDtypeStruct((total, 3 * width), BF16),
        in_specs=whole_specs(7),
        out_specs=whole_specs(1)[0],
        scratch_shapes=[pltpu.VMEM((total, width), F32), pltpu.VMEM((total, width), F32)],
        compiler_params=pltpu.CompilerParams(vmem_limit_bytes=48 * 2**20),
        cost_estimate=pl.CostEstimate(
            flops=5 * 2 * total * total * width,
            bytes_accessed=14 * total * width,
            transcendentals=total * total * width // HEAD_DIM // 2,
        ),
    )(query, key, value, grad, lse, seg_col, seg_row)


def local(
    tokens,
    cotangent,
    segments,
    qkv_weight,
    out_weight,
    up_weight,
    down_weight,
    small_weights,
    qkv_first,
    out_first,
    up_first,
    down_first,
    small_first,
    qkv_second,
    out_second,
    up_second,
    down_second,
    small_second,
):
    rep = lax.axis_index("rep")
    shards = lax.axis_size("shard")
    tok_rows, width = tokens.shape
    part = width // SPAN
    owned = qkv_weight.shape[0]
    ff = up_weight.shape[1]
    unit_rows = down_weight.shape[0]
    units = unit_rows // SPAN
    score_scale = HEAD_DIM ** (-0.5)

    def rep_part(block, size, axis):
        return lax.dynamic_slice_in_dim(block, rep * size, size, axis)

    low_small = small_weights.astype(BF16).T
    low_qkv = rep_part(qkv_weight.astype(BF16).reshape(owned, 3, SPAN, part), 1, 2)
    low_qkv = low_qkv.reshape(owned, 3 * part)
    pad = 64 - low_small.shape[1]
    first_send = jnp.concatenate([low_qkv, jnp.pad(low_small, ((0, 0), (0, pad)))], axis=1)
    low_out = out_weight.astype(BF16)
    low_up = rep_part(up_weight.astype(BF16).reshape(owned, shards, SPAN, units), 1, 2)
    low_up = low_up.reshape(owned, ff // SPAN)
    low_down = rep_part(down_weight, units, 0).astype(BF16)
    first_full, last = shard_gather(first_send)
    second_send = after(jnp.concatenate([low_out, low_up], axis=1), last)
    second_full, last = shard_gather(second_send)
    out_full, up_part = second_full[:, :width], second_full[:, width:]
    down_part, _ = shard_gather(after(low_down, last))
    qkv_part = first_full[:, : 3 * part]
    small_full = first_full[:, 3 * part : 3 * part + 12].T.astype(F32)
    gain_one, bias_one, query_bias, value_bias, out_bias, gain_two, bias_two, down_bias = (
        small_full[:8]
    )
    up_bias = rep_part(small_full[8:].reshape(shards, SPAN, units), 1, 1).reshape(-1)

    seg_rows = -(-tok_rows // width)
    seg_block = jnp.pad(segments.astype(BF16), (0, seg_rows * width - tok_rows))
    seg_block = jnp.pad(seg_block.reshape(seg_rows, width), ((0, 16 - seg_rows), (0, 0)))
    with_seg = rep_gather(jnp.concatenate([tokens, seg_block], axis=0))
    all_tokens = jnp.concatenate([block[:tok_rows] for block in with_seg], axis=0)
    all_segs = jnp.concatenate(
        [block[tok_rows : tok_rows + seg_rows].reshape(-1)[:tok_rows] for block in with_seg]
    ).astype(jnp.int32)
    seg_col, seg_row = all_segs[:, None], all_segs[None, :]
    all_cot = jnp.concatenate(rep_gather(cotangent), axis=0)

    inputs = all_tokens.astype(F32)
    norm_one, inverse_one = norm_parts(inputs)
    hidden_one = (norm_one * gain_one + bias_one).astype(BF16)
    query_bias_part = rep_part(query_bias, part, 0)
    value_bias_part = rep_part(value_bias, part, 0)
    joined_bias = jnp.concatenate(
        [query_bias_part, jnp.zeros_like(query_bias_part), value_bias_part]
    )
    projected = jnp.dot(hidden_one, qkv_part, preferred_element_type=F32) + joined_bias
    queries = (projected[:, :part] * score_scale).astype(BF16)
    keys = projected[:, part : 2 * part].astype(BF16)
    values = projected[:, 2 * part :].astype(BF16)
    attended_part, log_total = attend(queries, keys, values, seg_col, seg_row)
    attended = jnp.concatenate(rep_gather(attended_part), axis=1)
    residual = inputs + (jnp.dot(attended, out_full, preferred_element_type=F32) + out_bias)
    norm_two, inverse_two = norm_parts(residual)
    hidden_two = (norm_two * gain_two + bias_two).astype(BF16)
    pre_act = jnp.dot(hidden_two, up_part, preferred_element_type=F32) + up_bias
    cdf = 0.5 * (1.0 + lax.erf(pre_act * (0.5**0.5)))
    act_low = (pre_act * cdf).astype(BF16)
    slope = cdf + pre_act * (jnp.exp(-0.5 * pre_act * pre_act) * 0.3989422804014327)
    pre_low = (contract_cols(all_cot, down_part) * slope).astype(BF16)
    hidden_two_grad = rep_scatter(contract_cols(pre_low, up_part))
    mixed_part = jnp.dot(act_low, down_part, preferred_element_type=F32)
    residual_own = rep_part(residual, tok_rows, 0)
    down_grad = contract_rows(act_low, all_cot)
    up_grad = contract_rows(hidden_two, pre_low)
    up_bias_grad = jnp.sum(pre_low.astype(F32), axis=0)

    norm_two_own = rep_part(norm_two, tok_rows, 0)
    grad_own = cotangent.astype(F32)
    gain_two_grad = jnp.sum(hidden_two_grad * norm_two_own, axis=0)
    bias_two_grad = jnp.sum(hidden_two_grad, axis=0)
    resid_grad = grad_own + norm_back(
        norm_two_own, rep_part(inverse_two, tok_rows, 0), gain_two, hidden_two_grad
    )
    branch_own = resid_grad.astype(BF16)
    out_bias_grad = jnp.sum(branch_own.astype(F32), axis=0)
    branch_low = jnp.concatenate(rep_gather(branch_own), axis=0)
    mixed_sum = rep_scatter(after(mixed_part, branch_low))
    mixed = (residual_own + (mixed_sum + down_bias)).astype(BF16)
    out_grad = contract_rows(attended, rep_part(branch_low, part, 1))
    attended_grad = contract_cols(branch_low, rep_part(out_full, part, 0)).astype(BF16)
    proj_low = attend_back(queries, keys, values, attended_grad, log_total, seg_col, seg_row)
    proj_sums = jnp.sum(proj_low.astype(F32), axis=0)
    qkv_grad = contract_rows(hidden_one, proj_low)
    hidden_one_part = contract_cols(proj_low, qkv_part)
    gain_one_grad = jnp.sum(hidden_one_part * norm_one, axis=0)
    bias_one_grad = jnp.sum(hidden_one_part, axis=0)
    hidden_one_grad = rep_scatter(hidden_one_part)
    input_grad = resid_grad + norm_back(
        rep_part(norm_one, tok_rows, 0),
        rep_part(inverse_one, tok_rows, 0),
        gain_one,
        hidden_one_grad,
    )

    def placed(values_part, size, parts_before):
        blank = jnp.zeros((parts_before, SPAN, size), F32)
        return lax.dynamic_update_slice(
            blank, values_part.reshape(parts_before, 1, size), (0, rep, 0)
        ).reshape(-1)

    vector_grads = jnp.stack(
        [
            gain_one_grad,
            bias_one_grad,
            placed(proj_sums[:part], part, 1),
            placed(proj_sums[2 * part :], part, 1),
            out_bias_grad,
            gain_two_grad,
            bias_two_grad,
            jnp.sum(grad_own, axis=0),
        ]
    )
    small_grad = jnp.concatenate(
        [vector_grads, placed(up_bias_grad, units, shards).reshape(-1, width)], axis=0
    )

    def owned_sum(gradient):
        return rep_gather(shard_scatter(gradient).astype(BF16))

    down_own = jnp.concatenate(owned_sum(down_grad), axis=0).astype(F32)
    up_own = jnp.stack([g.reshape(owned, shards, units) for g in owned_sum(up_grad)], axis=2)
    up_own = up_own.reshape(owned, ff).astype(F32)
    out_own = jnp.concatenate(owned_sum(out_grad), axis=1).astype(F32)
    small_send = jnp.pad(small_grad.T, ((0, 0), (0, pad)))
    last_own = owned_sum(jnp.concatenate([qkv_grad, small_send], axis=1))
    qkv_own = [g[:, : 3 * part].reshape(owned, 3, part) for g in last_own]
    qkv_own = jnp.stack(qkv_own, axis=2).reshape(owned, 3 * width).astype(F32)
    small_own = sum(g[:, 3 * part : 3 * part + 12].astype(F32) for g in last_own).T
    qkv_res = adam_update(qkv_weight, qkv_own, qkv_first, qkv_second, RATE_MATRIX)
    out_res = adam_update(out_weight, out_own, out_first, out_second, RATE_MATRIX)
    up_res = adam_update(up_weight, up_own, up_first, up_second, RATE_MATRIX)
    down_res = adam_update(down_weight, down_own, down_first, down_second, RATE_MATRIX)
    small_res = adam_update(small_weights, small_own, small_first, small_second, RATE_SMALL)
    return (
        mixed,
        input_grad,
        qkv_res[0],
        out_res[0],
        up_res[0],
        down_res[0],
        small_res[0],
        qkv_res[1],
        out_res[1],
        up_res[1],
        down_res[1],
        small_res[1],
        qkv_res[2],
        out_res[2],
        up_res[2],
        down_res[2],
        small_res[2],
    )


def solution(mesh):
    tokens_spec = P(("rep", "shard"), None)
    rows = P("shard", None)
    columns = P(None, "shard")
    weights = (rows, rows, rows, rows, columns)
    return jax.shard_map(
        local,
        mesh=mesh,
        in_specs=(tokens_spec, tokens_spec, P(("rep", "shard"))) + weights * 3,
        out_specs=(tokens_spec, tokens_spec) + weights * 3,
        check_vma=False,
    )
```

```python
import jax
import jax.numpy as jnp
from jax import lax
from jax.experimental import pallas as pl
from jax.experimental.pallas import tpu as pltpu
from jax.sharding import PartitionSpec as P

HEAD_DIM = 64
SPAN = 4
STEP_NUM = 10


NORM_EPS = 1e-05
BETA_ONE = 0.9
BETA_TWO = 0.95
ADAM_EPS = 1e-08
DECAY = 0.1
RATE_MATRIX = 0.05
RATE_SMALL = 0.3
MASKED = -1e30
BLOCK = 256
FEW = 8
F32 = jnp.float32
BF16 = jnp.bfloat16


def swapped(block, bit):
    return lax.ppermute(block, "rep", [(i, i ^ bit) for i in range(SPAN)])


def rep_blocks(block):
    far = swapped(block, 2)
    near = swapped(block, 1)
    return (block, near, far, swapped(far, 1))


def swap_shard(block, bits):
    return lax.ppermute(block, "shard", [(i, i ^ bits) for i in range(lax.axis_size("shard"))])


def after(block, other):
    return lax.optimization_barrier((block, other))[0]


class Pieces:
    def __init__(self, arrays, codes, rows):
        self.arrays, self.codes, self.rows = arrays, codes, rows

    def place(self, shard, refs, store):
        if self.codes is None:
            store(0, refs[0], 0, refs[0].shape[0])
            return
        for ref, codes in zip(refs, self.codes):
            for index, code in enumerate(codes):
                start = pl.multiple_of((shard ^ code) * self.rows, self.rows)
                store(start, ref, index * self.rows, self.rows)


def shard_gather(block):
    shards = lax.axis_size("shard")
    if shards != FEW:
        full = lax.all_gather(block, "shard", axis=0, tiled=True)
        return Pieces([full], None, block.shape[0]), block
    one = swap_shard(block, 2)
    two = swap_shard(block, 4)
    three = swap_shard(block, 6)
    pair = swap_shard(jnp.concatenate([block, one], axis=0), 1)
    other = swap_shard(jnp.concatenate([two, three], axis=0), 1)
    codes = [[0], [2], [4], [6], [1, 3], [5, 7]]
    return Pieces([block, one, two, three, pair, other], codes, block.shape[0]), three


def shard_scatter(partial):
    shards = lax.axis_size("shard")
    if shards != FEW:
        total = lax.psum_scatter(partial, "shard", scatter_dimension=0, tiled=True)
        return total
    shard = lax.axis_index("shard")
    high, low = shard // 2, shard % 2
    count = shards // 2
    blocks = partial.reshape(count, 2, partial.shape[0] // shards, partial.shape[1])
    sent = lax.dynamic_index_in_dim(blocks, 1 - low, 1, keepdims=False)
    halves = lax.dynamic_index_in_dim(blocks, low, 1, keepdims=False).astype(F32)
    halves = (halves + swap_shard(sent, 1).astype(F32)).astype(BF16)
    total = lax.dynamic_index_in_dim(halves, high, 0, keepdims=False).astype(F32)
    for bits in range(1, count):
        sent = lax.dynamic_index_in_dim(halves, high ^ bits, 0, keepdims=False)
        total = total + swap_shard(sent, 2 * bits).astype(F32)
    return total.astype(BF16)


def norm_parts(values):
    center = jnp.mean(values, axis=-1, keepdims=True)
    centered = values - center
    variance = jnp.mean(centered * centered, axis=-1, keepdims=True)
    inverse = lax.rsqrt(variance + NORM_EPS)
    return centered * inverse, inverse


def norm_back(normalized, inverse, gain, grad):
    scaled = grad * gain
    mean_one = jnp.mean(scaled, axis=-1, keepdims=True)
    mean_two = jnp.mean(scaled * normalized, axis=-1, keepdims=True)
    return inverse * (scaled - mean_one - normalized * mean_two)


def contract_rows(left_side, right_side):
    return lax.dot_general(
        left_side, right_side, (((0,), (0,)), ((), ())), preferred_element_type=F32
    )


def contract_cols(left_side, right_side):
    return lax.dot_general(
        left_side, right_side, (((1,), (1,)), ((), ())), preferred_element_type=F32
    )


def adam_update(master, gradient, moment_one, moment_two, step_rate):
    first_new = BETA_ONE * moment_one + (1.0 - BETA_ONE) * gradient
    second_new = BETA_TWO * moment_two + (1.0 - BETA_TWO) * gradient * gradient
    fix_one = 1.0 - BETA_ONE**STEP_NUM
    fix_two = 1.0 - BETA_TWO**STEP_NUM
    step_dir = first_new / fix_one / (jnp.sqrt(second_new / fix_two) + ADAM_EPS)
    return (master - step_rate * (step_dir + DECAY * master), first_new, second_new)


def dot(left_side, right_side):
    return jnp.dot(left_side, right_side, preferred_element_type=F32)


def chosen(values, index):
    result = values[0]
    for at in range(1, len(values)):
        result = jnp.where(index == at, values[at], result)
    return result


def mask_bias(seg_col_ref, seg_row_ref, start, keys):
    same = seg_col_ref[:keys, 0:1] == seg_row_ref[0:1, start : start + BLOCK]
    key_at = lax.broadcasted_iota(jnp.int32, (keys, BLOCK), 0)
    query_at = lax.broadcasted_iota(jnp.int32, (keys, BLOCK), 1) + start
    return jnp.where(same & (key_at <= query_at), 0.0, MASKED)


def head_lanes(shape, head):
    lane = lax.broadcasted_iota(jnp.int32, shape, 1)
    return (lane >= head * HEAD_DIM) & (lane < (head + 1) * HEAD_DIM)


def attend(q_ref, k_ref, v_ref, seg_col_ref, seg_row_ref, out_ref, lse_ref):
    total, width = q_ref.shape
    heads = width // HEAD_DIM
    value_t = v_ref[...].T
    lse_ref[...] = jnp.zeros_like(lse_ref)
    for start in range(0, total, BLOCK):
        keys = start + BLOCK
        bias = mask_bias(seg_col_ref, seg_row_ref, start, keys)
        query = q_ref[start : start + BLOCK, :]
        pieces = []
        for head in range(heads):
            masked = jnp.where(head_lanes(query.shape, head), query, 0)
            scores = contract_cols(k_ref[:keys, :], masked) + bias
            peak = jnp.max(scores, axis=0, keepdims=True)
            exponent = jnp.exp(scores - peak)
            row_total = jnp.sum(exponent, axis=0, keepdims=True)
            mixed = dot(
                value_t[head * HEAD_DIM : (head + 1) * HEAD_DIM, :keys], exponent.astype(BF16)
            )
            pieces.append(mixed / row_total)
            lse_ref[head : head + 1, start : start + BLOCK] = peak + jnp.log(row_total)
        out_ref[start : start + BLOCK, :] = jnp.concatenate(pieces, axis=0).T.astype(BF16)


def attend_back(
    q_ref, k_ref, v_ref, do_ref, lse_ref, seg_col_ref, seg_row_ref, grad_ref, dk_ref, dv_ref
):
    total, width = q_ref.shape
    heads = width // HEAD_DIM
    key_t = k_ref[...].T
    dk_ref[...] = jnp.zeros_like(dk_ref)
    dv_ref[...] = jnp.zeros_like(dv_ref)
    for start in range(0, total, BLOCK):
        keys = start + BLOCK
        bias = mask_bias(seg_col_ref, seg_row_ref, start, keys)
        query = q_ref[start : start + BLOCK, :]
        grad = do_ref[start : start + BLOCK, :]
        pieces = []
        dk = dk_ref[:keys, :]
        dv = dv_ref[:keys, :]
        for head in range(heads):
            lanes = head_lanes(query.shape, head)
            query_h = jnp.where(lanes, query, 0)
            grad_h = jnp.where(lanes, grad, 0)
            scores = contract_cols(k_ref[:keys, :], query_h) + bias
            probs = jnp.exp(scores - lse_ref[head : head + 1, start : start + BLOCK])
            prob_grad = contract_cols(v_ref[:keys, :], grad_h)
            inner = jnp.sum(prob_grad * probs, axis=0, keepdims=True)
            score_grad = (probs * (prob_grad - inner)).astype(BF16)
            dv = dv + dot(probs.astype(BF16), grad_h)
            dk = dk + dot(score_grad, query_h)
            pieces.append(
                dot(key_t[head * HEAD_DIM : (head + 1) * HEAD_DIM, :keys], score_grad)
            )
        dk_ref[:keys, :] = dk
        dv_ref[:keys, :] = dv
        dq = jnp.concatenate(pieces, axis=0).T * HEAD_DIM ** (-0.5)
        grad_ref[start : start + BLOCK, :width] = dq.astype(BF16)
    grad_ref[:, width : 2 * width] = dk_ref[...].astype(BF16)
    grad_ref[:, 2 * width :] = dv_ref[...].astype(BF16)


def call(kernel, outs, scratch, flops, *operands):
    sizes = [o.size * o.dtype.itemsize for o in operands] + [
        o.size * jnp.dtype(o.dtype).itemsize for o in outs
    ]
    vmem = pl.BlockSpec(memory_space=pltpu.VMEM)
    return pl.pallas_call(
        kernel,
        out_shape=tuple(outs),
        in_specs=[pl.BlockSpec(memory_space=pltpu.SMEM)] + [vmem] * (len(operands) - 1),
        out_specs=tuple([vmem] * len(outs)),
        scratch_shapes=scratch,
        compiler_params=pltpu.CompilerParams(vmem_limit_bytes=56 * 2**20),
        cost_estimate=pl.CostEstimate(
            flops=flops, bytes_accessed=sum(sizes), transcendentals=0
        ),
    )(*operands)


def shape(*dims, dtype=BF16):
    return jax.ShapeDtypeStruct(dims, dtype)


def send_parts(value, at, near_ref, far_ref, own_ref):
    rows = value.shape[0]

    @pl.when(at == 0)
    def _():
        own_ref[...] = value

    @pl.when(at == 1)
    def _():
        near_ref[rows:, :] = value.astype(BF16)

    @pl.when(at == 2)
    def _():
        far_ref[...] = value

    @pl.when(at == 3)
    def _():
        near_ref[:rows, :] = value.astype(BF16)


def rep_sum(near_send, far_part, own):
    rows = own.shape[0]
    near = swapped(near_send, 1)
    far_send = (far_part + near[:rows].astype(F32)).astype(BF16)
    return own, near[rows:], swapped(far_send, 2)


def place_store(target, columns):
    def store(start, ref, first, rows):
        target[pl.ds(start, rows), :] = ref[first : first + rows, columns]

    return store


def first_kernel(pieces, *refs):
    place_ref, refs = refs[0], refs[1:]
    token_refs, refs = refs[:SPAN], refs[SPAN:]
    count = len(pieces.arrays)
    weight_refs, refs = refs[:count], refs[count:]
    (
        all_ref,
        hidden_ref,
        weight_ref,
        small_ref,
        q_ref,
        k_ref,
        v_ref,
        seg_col_ref,
        seg_row_ref,
        out_ref,
        lse_ref,
        small_cols,
    ) = refs
    rep, shard = place_ref[0], place_ref[1]
    total, width = all_ref.shape
    rows = total // SPAN
    part = q_ref.shape[1]
    pieces.place(shard, weight_refs, place_store(weight_ref, slice(0, 3 * part)))
    last = small_cols.shape[1]
    pieces.place(
        shard, weight_refs, place_store(small_cols, slice(3 * part + 64 - last, 3 * part + 64))
    )
    small = small_cols[...].astype(F32).T
    small = small[last - 64 : last - 48, :]
    small_ref[...] = small
    gain, bias = small[0:1, :], small[1:2, :]
    query_bias = chosen([small[2:3, r * part : (r + 1) * part] for r in range(SPAN)], rep)
    value_bias = chosen([small[3:4, r * part : (r + 1) * part] for r in range(SPAN)], rep)
    for at in range(SPAN):
        start = pl.multiple_of((rep ^ at) * rows, rows)
        block = token_refs[at][:rows, :]
        all_ref[pl.ds(start, rows), :] = block
        hidden = (norm_parts(block.astype(F32))[0] * gain + bias).astype(BF16)
        hidden_ref[pl.ds(start, rows), :] = hidden
        segs = token_refs[at][rows : rows + 16, :rows].astype(F32)
        seg_row_ref[:, pl.ds(start, rows)] = segs[:8, :]
        seg_col_ref[pl.ds(start, rows), 0:16] = segs.T
        projected = dot(hidden, weight_ref[...])
        q_ref[pl.ds(start, rows), :] = (
            (projected[:, :part] + query_bias) * HEAD_DIM ** (-0.5)
        ).astype(BF16)
        k_ref[pl.ds(start, rows), :] = projected[:, part : 2 * part].astype(BF16)
        v_ref[pl.ds(start, rows), :] = (projected[:, 2 * part :] + value_bias).astype(BF16)
    attend(q_ref, k_ref, v_ref, seg_col_ref, seg_row_ref, out_ref, lse_ref)


def second_kernel(wide, down, *refs):
    place_ref, refs = refs[0], refs[1:]
    attended_refs, refs = refs[:SPAN], refs[SPAN:]
    cot_refs, refs = refs[:SPAN], refs[SPAN:]
    wide_refs, refs = refs[: len(wide.arrays)], refs[len(wide.arrays) :]
    down_refs, refs = refs[: len(down.arrays)], refs[len(down.arrays) :]
    (
        all_ref,
        small_ref,
        up_bias_ref,
        out_weight,
        down_weight,
        cot_ref,
        hidden_ref,
        act_ref,
        pre_ref,
        residual_ref,
        near_ref,
        far_ref,
        own_ref,
        up_weight,
    ) = refs
    rep, shard = place_ref[0], place_ref[1]
    total, width = all_ref.shape
    rows = total // SPAN
    part = attended_refs[0].shape[1]
    wide.place(shard, wide_refs, place_store(out_weight, slice(0, width)))
    wide.place(shard, wide_refs, place_store(up_weight, slice(width, None)))
    down.place(shard, down_refs, place_store(down_weight, slice(None)))
    for at in range(SPAN):
        cot_ref[pl.ds(pl.multiple_of((rep ^ at) * rows, rows), rows), :] = cot_refs[at][...]
    out_bias, gain, bias = small_ref[4:5, :], small_ref[5:6, :], small_ref[6:7, :]

    @pl.loop(0, SPAN)
    def _(index):
        block = pl.ds(pl.multiple_of(index * rows, rows), rows)
        mixed = out_bias
        for at in range(SPAN):
            from_rows = pl.ds(pl.multiple_of((rep ^ at) * part, part), part)
            mixed = mixed + dot(attended_refs[at][block, :], out_weight[from_rows, :])
        residual = all_ref[block, :].astype(F32) + mixed

        @pl.when(index == rep)
        def _():
            residual_ref[...] = residual

        hidden = (norm_parts(residual)[0] * gain + bias).astype(BF16)
        hidden_ref[block, :] = hidden
        pre_act = dot(hidden, up_weight[...]) + up_bias_ref[...]
        cdf = 0.5 * (1.0 + lax.erf(pre_act * (0.5**0.5)))
        act_ref[block, :] = (pre_act * cdf).astype(BF16)
        slope = cdf + pre_act * (jnp.exp(-0.5 * pre_act * pre_act) * 0.3989422804014327)
        pre_low = (contract_cols(cot_ref[block, :], down_weight[...]) * slope).astype(BF16)
        pre_ref[block, :] = pre_low
        send_parts(contract_cols(pre_low, up_weight[...]), index ^ rep, near_ref, far_ref, own_ref)


def third_kernel(
    place_ref,
    act_ref,
    hidden_ref,
    pre_ref,
    cot_ref,
    down_weight,
    grad_ref,
    near_ref,
    far_ref,
    own_ref,
    sum_ref,
):
    rep = place_ref[0]
    total, width = cot_ref.shape
    rows = total // SPAN
    units = act_ref.shape[1]
    step = units // 3
    for first in range(0, units, step):
        grad_ref[first : first + step, :width] = contract_rows(
            act_ref[:, first : first + step], cot_ref[...]
        ).astype(BF16)
    step = width // 3
    for first in range(0, width, step):
        grad_ref[first : first + step, width:] = contract_rows(
            hidden_ref[:, first : first + step], pre_ref[...]
        ).astype(BF16)
    sum_ref[...] = jnp.broadcast_to(
        jnp.sum(pre_ref[...].astype(F32), axis=0, keepdims=True), sum_ref.shape
    )

    @pl.loop(0, SPAN)
    def _(index):
        block = pl.ds(pl.multiple_of(index * rows, rows), rows)
        send_parts(
            dot(act_ref[block, :], down_weight[...]), index ^ rep, near_ref, far_ref, own_ref
        )


def fourth_kernel(
    place_ref,
    own_ref,
    near_ref,
    far_ref,
    residual_ref,
    cotangent_ref,
    small_ref,
    resid_grad_ref,
    branch_ref,
    sums_ref,
):
    grad = own_ref[...] + near_ref[...].astype(F32) + far_ref[...].astype(F32)
    normalized, inverse = norm_parts(residual_ref[...])
    cotangent = cotangent_ref[...].astype(F32)
    resid_grad = cotangent + norm_back(normalized, inverse, small_ref[5:6, :], grad)
    branch = resid_grad.astype(BF16)
    resid_grad_ref[...] = resid_grad
    branch_ref[...] = branch
    sums_ref[...] = jnp.zeros_like(sums_ref)
    sums_ref[4:5, :] = jnp.sum(branch.astype(F32), axis=0, keepdims=True)
    sums_ref[5:6, :] = jnp.sum(grad * normalized, axis=0, keepdims=True)
    sums_ref[6:7, :] = jnp.sum(grad, axis=0, keepdims=True)
    sums_ref[7:8, :] = jnp.sum(cotangent, axis=0, keepdims=True)


def fifth_kernel(
    place_ref,
    branch_a,
    branch_b,
    branch_c,
    branch_d,
    attended_a,
    attended_b,
    attended_c,
    attended_d,
    out_weight,
    qkv_weight,
    q_ref,
    k_ref,
    v_ref,
    lse_ref,
    seg_col_ref,
    seg_row_ref,
    all_ref,
    hidden_ref,
    small_ref,
    sums_ref,
    unit_sums_ref,
    grad_ref,
    near_ref,
    far_ref,
    own_ref,
    branch_ref,
    back_ref,
    proj_ref,
    dk_ref,
    dv_ref,
    small_grads,
):
    rep = place_ref[0]
    total, width = all_ref.shape
    rows = total // SPAN
    part = q_ref.shape[1]
    own_rows = pl.ds(pl.multiple_of(rep * part, part), part)
    for at, ref in enumerate((branch_a, branch_b, branch_c, branch_d)):
        start = pl.multiple_of((rep ^ at) * rows, rows)
        branch_ref[pl.ds(start, rows), :] = ref[...]
    back_ref[...] = contract_cols(branch_ref[...], out_weight[own_rows, :]).astype(BF16)
    attend_back(
        q_ref,
        k_ref,
        v_ref,
        back_ref,
        lse_ref,
        seg_col_ref,
        seg_row_ref,
        proj_ref,
        dk_ref,
        dv_ref,
    )
    gain = small_ref[0:1, :]
    small_grads[...] = jnp.zeros_like(small_grads)
    small_grads[0:8, :] = sums_ref[...]
    small_grads[8:16, :] = unit_sums_ref[...]

    @pl.loop(0, SPAN)
    def _(index):
        block = pl.ds(pl.multiple_of(index * rows, rows), rows)
        grad = contract_cols(proj_ref[block, :], qkv_weight[...])
        normalized = norm_parts(all_ref[block, :].astype(F32))[0]
        small_grads[0:1, :] += jnp.sum(grad * normalized, axis=0, keepdims=True)
        small_grads[1:2, :] += jnp.sum(grad, axis=0, keepdims=True)
        send_parts(grad, index ^ rep, near_ref, far_ref, own_ref)

    lane = lax.broadcasted_iota(jnp.int32, (1, width), 1)
    mine = (lane >= rep * part) & (lane < (rep + 1) * part)
    for row, first in ((2, 0), (3, 2 * part)):
        column_sum = jnp.sum(
            proj_ref[:, first : first + part].astype(F32), axis=0, keepdims=True
        )
        small_grads[row : row + 1, :] = jnp.where(
            mine, jnp.concatenate([column_sum] * SPAN, axis=1), 0.0
        )
    step = width // 3
    for first in range(0, width, step):
        grad_ref[first : first + step, : 3 * part] = contract_rows(
            hidden_ref[:, first : first + step], proj_ref[...]
        ).astype(BF16)
    branch_part = chosen(
        [branch_ref[:, r * part : (r + 1) * part] for r in range(SPAN)], rep
    )
    for at, ref in enumerate((attended_a, attended_b, attended_c, attended_d)):
        from_rows = pl.ds(pl.multiple_of((rep ^ at) * part, part), part)
        grad_ref[from_rows, 3 * part : 4 * part] = contract_rows(ref[...], branch_part).astype(
            BF16
        )
    grad_ref[:, 4 * part :] = small_grads[...].T[:, :64].astype(BF16)


def sixth_kernel(
    place_ref, own_ref, near_ref, far_ref, tokens_ref, resid_grad_ref, small_ref, out_ref
):
    grad = own_ref[...] + near_ref[...].astype(F32) + far_ref[...].astype(F32)
    normalized, inverse = norm_parts(tokens_ref[...].astype(F32))
    out_ref[...] = resid_grad_ref[...] + norm_back(normalized, inverse, small_ref[0:1, :], grad)


def in_order(blocks, rep):
    odd = (rep & 1) == 1
    high = (rep & 2) == 2
    low_pair = (jnp.where(odd, blocks[1], blocks[0]), jnp.where(odd, blocks[0], blocks[1]))
    high_pair = (jnp.where(odd, blocks[3], blocks[2]), jnp.where(odd, blocks[2], blocks[3]))
    return (
        jnp.where(high, high_pair[0], low_pair[0]),
        jnp.where(high, high_pair[1], low_pair[1]),
        jnp.where(high, low_pair[0], high_pair[0]),
        jnp.where(high, low_pair[1], high_pair[1]),
    )


def local(
    tokens,
    cotangent,
    segments,
    qkv_weight,
    out_weight,
    up_weight,
    down_weight,
    small_weights,
    qkv_first,
    out_first,
    up_first,
    down_first,
    small_first,
    qkv_second,
    out_second,
    up_second,
    down_second,
    small_second,
):
    rep = lax.axis_index("rep")
    shards = lax.axis_size("shard")
    place = jnp.stack([rep, lax.axis_index("shard")]).astype(jnp.int32)
    rows, width = tokens.shape
    total = SPAN * rows
    part = width // SPAN
    owned = qkv_weight.shape[0]
    ff = up_weight.shape[1]
    ff_part = ff // SPAN
    units = down_weight.shape[0] // SPAN

    def rep_part(block, size, axis):
        return lax.dynamic_slice_in_dim(block, rep * size, size, axis)

    low_small = small_weights.astype(BF16).T
    low_qkv = rep_part(qkv_weight.astype(BF16).reshape(owned, 3, SPAN, part), 1, 2)
    low_qkv = low_qkv.reshape(owned, 3 * part)
    pad = 64 - low_small.shape[1]
    first_send = jnp.concatenate([low_qkv, jnp.pad(low_small, ((0, 0), (0, pad)))], axis=1)
    low_up = rep_part(up_weight.astype(BF16).reshape(owned, shards, SPAN, units), 1, 2)
    low_up = low_up.reshape(owned, ff_part)
    low_down = rep_part(down_weight, units, 0).astype(BF16)
    first_pieces, last = shard_gather(first_send)
    wide_send = jnp.concatenate([out_weight.astype(BF16), low_up], axis=1)
    wide_pieces, last = shard_gather(after(wide_send, last))
    down_pieces, _ = shard_gather(after(low_down, last))

    seg_block = jnp.pad(segments.astype(BF16)[None, :], ((0, 15), (0, width - rows)))
    token_blocks = rep_blocks(jnp.concatenate([tokens, seg_block], axis=0))
    cot_blocks = rep_blocks(cotangent)

    (
        all_tokens,
        hidden_one,
        qkv_part,
        small,
        queries,
        keys,
        values,
        seg_col,
        seg_row,
        attended,
        log_total,
    ) = call(
        lambda *refs: first_kernel(first_pieces, *refs),
        [
            shape(total, width),
            shape(total, width),
            shape(width, 3 * part),
            shape(16, width, dtype=F32),
            shape(total, part),
            shape(total, part),
            shape(total, part),
            shape(total, 128, dtype=F32),
            shape(8, total, dtype=F32),
            shape(total, part),
            shape(8, total, dtype=F32),
        ],
        [pltpu.VMEM((width, 128), BF16)],
        2 * total * width * 3 * part + 16 * total * total * part,
        place,
        *token_blocks,
        *first_pieces.arrays,
    )
    up_bias = rep_part(small[8:12].reshape(shards, SPAN, units), 1, 1).reshape(1, -1)
    attended_blocks = rep_blocks(attended)
    (
        out_part,
        down_part,
        all_cot,
        hidden_two,
        act_low,
        pre_low,
        residual,
        near_send,
        far_part,
        own,
    ) = call(
        lambda *refs: second_kernel(wide_pieces, down_pieces, *refs),
        [
            shape(width, width),
            shape(ff_part, width),
            shape(total, width),
            shape(total, width),
            shape(total, ff_part),
            shape(total, ff_part),
            shape(rows, width, dtype=F32),
            shape(2 * rows, width),
            shape(rows, width, dtype=F32),
            shape(rows, width, dtype=F32),
        ],
        [pltpu.VMEM((width, ff_part), BF16)],
        10 * total * width * width,
        place,
        *attended_blocks,
        *cot_blocks,
        *wide_pieces.arrays,
        *down_pieces.arrays,
        all_tokens,
        small,
        up_bias,
    )
    hidden_two_terms = rep_sum(near_send, far_part, own)
    wide_grad, near_send, far_part, own, unit_sums = call(
        third_kernel,
        [
            shape(ff_part, 2 * width),
            shape(2 * rows, width),
            shape(rows, width, dtype=F32),
            shape(rows, width, dtype=F32),
            shape(8, ff_part, dtype=F32),
        ],
        [],
        6 * total * width * width,
        place,
        act_low,
        hidden_two,
        pre_low,
        all_cot,
        down_part,
    )
    wide_own = rep_blocks(shard_scatter(wide_grad))
    resid_grad, branch, sums = call(
        fourth_kernel,
        [
            shape(rows, width, dtype=F32),
            shape(rows, width),
            shape(8, width, dtype=F32),
        ],
        [],
        10 * rows * width,
        place,
        *hidden_two_terms,
        residual,
        cotangent,
        small,
    )
    branch_blocks = rep_blocks(branch)
    mixed_terms = rep_sum(after(near_send, branch_blocks[3]), far_part, own)
    mixed = residual + (
        mixed_terms[0] + mixed_terms[1].astype(F32) + mixed_terms[2].astype(F32) + small[7]
    )
    unit_rows = lax.dynamic_update_slice(
        jnp.zeros((shards, SPAN, units), F32), unit_sums[0].reshape(shards, 1, units), (0, rep, 0)
    ).reshape(ff // width, width)
    unit_rows = jnp.pad(unit_rows, ((0, 8 - ff // width), (0, 0)))
    last_grad, near_send, far_part, own = call(
        fifth_kernel,
        [
            shape(width, 4 * part + 64),
            shape(2 * rows, width),
            shape(rows, width, dtype=F32),
            shape(rows, width, dtype=F32),
        ],
        [
            pltpu.VMEM((total, width), BF16),
            pltpu.VMEM((total, part), BF16),
            pltpu.VMEM((total, 3 * part), BF16),
            pltpu.VMEM((total, part), F32),
            pltpu.VMEM((total, part), F32),
            pltpu.VMEM((128, width), F32),
        ],
        6 * total * width * width + 40 * total * total * part,
        place,
        *branch_blocks,
        *attended_blocks,
        out_part,
        qkv_part,
        queries,
        keys,
        values,
        log_total,
        seg_col,
        seg_row,
        all_tokens,
        hidden_one,
        small,
        sums,
        unit_rows,
    )
    last_own = in_order(rep_blocks(shard_scatter(last_grad)), rep)
    hidden_one_terms = rep_sum(near_send, far_part, own)
    input_grad = call(
        sixth_kernel,
        [shape(rows, width, dtype=F32)],
        [],
        10 * rows * width,
        place,
        *hidden_one_terms,
        tokens,
        resid_grad,
        small,
    )[0]

    wide_own = in_order(wide_own, rep)
    down_own = jnp.concatenate([g[:, :width] for g in wide_own], axis=0).astype(F32)
    up_own = jnp.stack([g[:, width:].reshape(owned, shards, units) for g in wide_own], axis=2)
    up_own = up_own.reshape(owned, ff).astype(F32)
    out_own = jnp.concatenate([g[:, 3 * part : 4 * part] for g in last_own], axis=1).astype(F32)
    qkv_own = [g[:, : 3 * part].reshape(owned, 3, part) for g in last_own]
    qkv_own = jnp.stack(qkv_own, axis=2).reshape(owned, 3 * width).astype(F32)
    small_own = sum(g[:, 4 * part : 4 * part + 12].astype(F32) for g in last_own).T
    qkv_res = adam_update(qkv_weight, qkv_own, qkv_first, qkv_second, RATE_MATRIX)
    out_res = adam_update(out_weight, out_own, out_first, out_second, RATE_MATRIX)
    up_res = adam_update(up_weight, up_own, up_first, up_second, RATE_MATRIX)
    down_res = adam_update(down_weight, down_own, down_first, down_second, RATE_MATRIX)
    small_res = adam_update(small_weights, small_own, small_first, small_second, RATE_SMALL)
    return (
        mixed.astype(BF16),
        input_grad,
        qkv_res[0],
        out_res[0],
        up_res[0],
        down_res[0],
        small_res[0],
        qkv_res[1],
        out_res[1],
        up_res[1],
        down_res[1],
        small_res[1],
        qkv_res[2],
        out_res[2],
        up_res[2],
        down_res[2],
        small_res[2],
    )


def solution(mesh):
    tokens_spec = P(("rep", "shard"), None)
    rows = P("shard", None)
    columns = P(None, "shard")
    weights = (rows, rows, rows, rows, columns)
    return jax.shard_map(
        local,
        mesh=mesh,
        in_specs=(tokens_spec, tokens_spec, P(("rep", "shard"))) + weights * 3,
        out_specs=(tokens_spec, tokens_spec) + weights * 3,
        check_vma=False,
    )
```

```python
import jax
import jax.numpy as jnp
from jax import lax
from jax.experimental import pallas as pl
from jax.experimental.pallas import tpu as pltpu
from jax.sharding import PartitionSpec as P

HEAD_DIM = 64
SPAN = 4
STEP_NUM = 10


NORM_EPS = 1e-05
BETA_ONE = 0.9
BETA_TWO = 0.95
ADAM_EPS = 1e-08
DECAY = 0.1
RATE_MATRIX = 0.05
RATE_SMALL = 0.3
MASKED = -1e30
BLOCK = 256
FEW = 8
F32 = jnp.float32
BF16 = jnp.bfloat16


def swapped(block, bit):
    return lax.ppermute(block, "rep", [(i, i ^ bit) for i in range(SPAN)])


def rep_blocks(block):
    far = swapped(block, 2)
    near = swapped(block, 1)
    return (block, near, far, swapped(far, 1))


def swap_shard(block, bits):
    return lax.ppermute(block, "shard", [(i, i ^ bits) for i in range(lax.axis_size("shard"))])


def after(block, other):
    return lax.optimization_barrier((block, other))[0]


class Pieces:
    def __init__(self, arrays, codes, rows):
        self.arrays, self.codes, self.rows = arrays, codes, rows

    def place(self, shard, refs, store):
        if self.codes is None:
            store(0, refs[0], 0, refs[0].shape[0])
            return
        for ref, codes in zip(refs, self.codes):
            for index, code in enumerate(codes):
                start = pl.multiple_of((shard ^ code) * self.rows, self.rows)
                store(start, ref, index * self.rows, self.rows)


def shard_gather(block):
    shards = lax.axis_size("shard")
    if shards != FEW:
        full = lax.all_gather(block, "shard", axis=0, tiled=True)
        return Pieces([full], None, block.shape[0])
    cross = swap_shard(block, 1)
    one = swap_shard(block, 2)
    two = swap_shard(block, 4)
    three = swap_shard(block, 6)
    other = swap_shard(jnp.concatenate([one, two, three], axis=0), 1)
    codes = [[0], [1], [2], [4], [6], [3, 5, 7]]
    return Pieces([block, cross, one, two, three, other], codes, block.shape[0])


def middle_kernel(place_ref, kept_ref, received_ref, own_ref, *sent_refs):
    high = place_ref[1] // 2
    rows = own_ref.shape[0]
    for bits in range(len(sent_refs) + 1):
        block = pl.ds(pl.multiple_of((high ^ bits) * rows, rows), rows)
        value = kept_ref[block, :].astype(F32) + received_ref[block, :].astype(F32)
        if bits == 0:
            own_ref[...] = value
        else:
            sent_refs[bits - 1][...] = value.astype(BF16)


def scatter_middle(place, kept, sent):
    received = swap_shard(sent, 1)
    count = FEW // 2
    rows, columns = kept.shape[0] // count, kept.shape[1]
    own, *sends = call(
        middle_kernel,
        [shape(rows, columns, dtype=F32)] + [shape(rows, columns)] * (count - 1),
        [],
        kept.size,
        16,
        place,
        kept,
        received,
    )
    return own, [swap_shard(send, 2 * (bits + 1)) for bits, send in enumerate(sends)]


def scatter_end(own, received):
    total = own
    for block in received:
        total = total + block.astype(F32)
    return total.astype(BF16)


def split_halves(place_ref, full_ref, kept_ref, sent_ref):
    low = place_ref[1] & 1
    rows = full_ref.shape[0] // FEW
    for at in range(FEW // 2):
        target = slice(at * rows, (at + 1) * rows)
        for ref, bit in ((kept_ref, low), (sent_ref, 1 - low)):
            start = pl.multiple_of((2 * at + bit) * rows, rows)
            ref[target, :] = full_ref[pl.ds(start, rows), :]


def norm_parts(values):
    center = jnp.mean(values, axis=-1, keepdims=True)
    centered = values - center
    variance = jnp.mean(centered * centered, axis=-1, keepdims=True)
    inverse = lax.rsqrt(variance + NORM_EPS)
    return centered * inverse, inverse


def norm_back(normalized, inverse, gain, grad):
    scaled = grad * gain
    mean_one = jnp.mean(scaled, axis=-1, keepdims=True)
    mean_two = jnp.mean(scaled * normalized, axis=-1, keepdims=True)
    return inverse * (scaled - mean_one - normalized * mean_two)


def contract_rows(left_side, right_side):
    return lax.dot_general(
        left_side, right_side, (((0,), (0,)), ((), ())), preferred_element_type=F32
    )


def contract_cols(left_side, right_side):
    return lax.dot_general(
        left_side, right_side, (((1,), (1,)), ((), ())), preferred_element_type=F32
    )


def adam_update(master, gradient, moment_one, moment_two, step_rate):
    first_new = BETA_ONE * moment_one + (1.0 - BETA_ONE) * gradient
    second_new = BETA_TWO * moment_two + (1.0 - BETA_TWO) * gradient * gradient
    fix_one = 1.0 - BETA_ONE**STEP_NUM
    fix_two = 1.0 - BETA_TWO**STEP_NUM
    step_dir = first_new / fix_one / (jnp.sqrt(second_new / fix_two) + ADAM_EPS)
    return (master - step_rate * (step_dir + DECAY * master), first_new, second_new)


def dot(left_side, right_side):
    return jnp.dot(left_side, right_side, preferred_element_type=F32)


def chosen(values, index):
    result = values[0]
    for at in range(1, len(values)):
        result = jnp.where(index == at, values[at], result)
    return result


def mask_bias(seg_col_ref, seg_row_ref, start, keys):
    same = seg_col_ref[:keys, 0:1] == seg_row_ref[0:1, start : start + BLOCK]
    key_at = lax.broadcasted_iota(jnp.int32, (keys, BLOCK), 0)
    query_at = lax.broadcasted_iota(jnp.int32, (keys, BLOCK), 1) + start
    return jnp.where(same & (key_at <= query_at), 0.0, MASKED)


def head_lanes(shape, head):
    lane = lax.broadcasted_iota(jnp.int32, shape, 1)
    return (lane >= head * HEAD_DIM) & (lane < (head + 1) * HEAD_DIM)


def attend(q_ref, k_ref, v_ref, seg_col_ref, seg_row_ref, out_ref, lse_ref):
    total, width = q_ref.shape
    heads = width // HEAD_DIM
    value_t = v_ref[...].T
    lse_ref[...] = jnp.zeros_like(lse_ref)
    for start in range(0, total, BLOCK):
        keys = start + BLOCK
        bias = mask_bias(seg_col_ref, seg_row_ref, start, keys)
        query = q_ref[start : start + BLOCK, :]
        pieces = []
        for head in range(heads):
            masked = jnp.where(head_lanes(query.shape, head), query, 0)
            scores = contract_cols(k_ref[:keys, :], masked) + bias
            peak = jnp.max(scores, axis=0, keepdims=True)
            exponent = jnp.exp(scores - peak)
            row_total = jnp.sum(exponent, axis=0, keepdims=True)
            mixed = dot(
                value_t[head * HEAD_DIM : (head + 1) * HEAD_DIM, :keys], exponent.astype(BF16)
            )
            pieces.append(mixed / row_total)
            lse_ref[head : head + 1, start : start + BLOCK] = peak + jnp.log(row_total)
        out_ref[start : start + BLOCK, :] = jnp.concatenate(pieces, axis=0).T.astype(BF16)


def attend_back(
    q_ref, k_ref, v_ref, do_ref, lse_ref, seg_col_ref, seg_row_ref, grad_ref, dk_ref, dv_ref
):
    total, width = q_ref.shape
    heads = width // HEAD_DIM
    key_t = k_ref[...].T
    dk_ref[...] = jnp.zeros_like(dk_ref)
    dv_ref[...] = jnp.zeros_like(dv_ref)
    for start in range(0, total, BLOCK):
        keys = start + BLOCK
        bias = mask_bias(seg_col_ref, seg_row_ref, start, keys)
        query = q_ref[start : start + BLOCK, :]
        grad = do_ref[start : start + BLOCK, :]
        pieces = []
        dk = dk_ref[:keys, :]
        dv = dv_ref[:keys, :]
        for head in range(heads):
            lanes = head_lanes(query.shape, head)
            query_h = jnp.where(lanes, query, 0)
            grad_h = jnp.where(lanes, grad, 0)
            scores = contract_cols(k_ref[:keys, :], query_h) + bias
            probs = jnp.exp(scores - lse_ref[head : head + 1, start : start + BLOCK])
            prob_grad = contract_cols(v_ref[:keys, :], grad_h)
            inner = jnp.sum(prob_grad * probs, axis=0, keepdims=True)
            score_grad = (probs * (prob_grad - inner)).astype(BF16)
            dv = dv + dot(probs.astype(BF16), grad_h)
            dk = dk + dot(score_grad, query_h)
            pieces.append(
                dot(key_t[head * HEAD_DIM : (head + 1) * HEAD_DIM, :keys], score_grad)
            )
        dk_ref[:keys, :] = dk
        dv_ref[:keys, :] = dv
        dq = jnp.concatenate(pieces, axis=0).T * HEAD_DIM ** (-0.5)
        grad_ref[start : start + BLOCK, :width] = dq.astype(BF16)
    grad_ref[:, width : 2 * width] = dk_ref[...].astype(BF16)
    grad_ref[:, 2 * width :] = dv_ref[...].astype(BF16)


def call(kernel, outs, scratch, flops, limit, *operands):
    sizes = [o.size * o.dtype.itemsize for o in operands] + [
        o.size * jnp.dtype(o.dtype).itemsize for o in outs
    ]
    vmem = pl.BlockSpec(memory_space=pltpu.VMEM)
    return pl.pallas_call(
        kernel,
        out_shape=tuple(outs),
        in_specs=[pl.BlockSpec(memory_space=pltpu.SMEM)] + [vmem] * (len(operands) - 1),
        out_specs=tuple([vmem] * len(outs)),
        scratch_shapes=scratch,
        compiler_params=pltpu.CompilerParams(vmem_limit_bytes=limit * 2**20),
        cost_estimate=pl.CostEstimate(
            flops=flops, bytes_accessed=sum(sizes), transcendentals=0
        ),
    )(*operands)


def shape(*dims, dtype=BF16):
    return jax.ShapeDtypeStruct(dims, dtype)


def send_parts(value, at, near_ref, far_ref, own_ref):
    rows = value.shape[0]

    @pl.when(at == 0)
    def _():
        own_ref[...] = value

    @pl.when(at == 1)
    def _():
        near_ref[rows:, :] = value.astype(BF16)

    @pl.when(at == 2)
    def _():
        far_ref[...] = value

    @pl.when(at == 3)
    def _():
        near_ref[:rows, :] = value.astype(BF16)


def rep_sum(near_send, far_part):
    rows = far_part.shape[0]
    near = swapped(near_send, 1)
    far_send = (far_part + near[:rows].astype(F32)).astype(BF16)
    return near, swapped(far_send, 2), far_send


def place_store(target, columns):
    def store(start, ref, first, rows):
        target[pl.ds(start, rows), :] = ref[first : first + rows, columns]

    return store


def first_kernel(pieces, *refs):
    place_ref, refs = refs[0], refs[1:]
    token_refs, refs = refs[:SPAN], refs[SPAN:]
    count = len(pieces.arrays)
    weight_refs, refs = refs[:count], refs[count:]
    (
        all_ref,
        hidden_ref,
        weight_ref,
        small_ref,
        q_ref,
        k_ref,
        v_ref,
        seg_col_ref,
        seg_row_ref,
        out_ref,
        lse_ref,
        small_cols,
    ) = refs
    rep, shard = place_ref[0], place_ref[1]
    total, width = all_ref.shape
    rows = total // SPAN
    part = q_ref.shape[1]
    pieces.place(shard, weight_refs, place_store(weight_ref, slice(0, 3 * part)))
    last = small_cols.shape[1]
    pieces.place(
        shard, weight_refs, place_store(small_cols, slice(3 * part + 64 - last, 3 * part + 64))
    )
    small = small_cols[...].astype(F32).T
    small = small[last - 64 : last - 48, :]
    small_ref[...] = small
    gain, bias = small[0:1, :], small[1:2, :]
    query_bias = chosen([small[2:3, r * part : (r + 1) * part] for r in range(SPAN)], rep)
    value_bias = chosen([small[3:4, r * part : (r + 1) * part] for r in range(SPAN)], rep)
    for at in range(SPAN):
        start = pl.multiple_of((rep ^ at) * rows, rows)
        block = token_refs[at][:rows, :]
        all_ref[pl.ds(start, rows), :] = block
        hidden = (norm_parts(block.astype(F32))[0] * gain + bias).astype(BF16)
        hidden_ref[pl.ds(start, rows), :] = hidden
        segs = token_refs[at][rows : rows + 16, :rows].astype(F32)
        seg_row_ref[:, pl.ds(start, rows)] = segs[:8, :]
        seg_col_ref[pl.ds(start, rows), 0:16] = segs.T
        projected = dot(hidden, weight_ref[...])
        q_ref[pl.ds(start, rows), :] = (
            (projected[:, :part] + query_bias) * HEAD_DIM ** (-0.5)
        ).astype(BF16)
        k_ref[pl.ds(start, rows), :] = projected[:, part : 2 * part].astype(BF16)
        v_ref[pl.ds(start, rows), :] = (projected[:, 2 * part :] + value_bias).astype(BF16)
    attend(q_ref, k_ref, v_ref, seg_col_ref, seg_row_ref, out_ref, lse_ref)


def second_kernel(place_ref, *refs):
    attended_refs, refs = refs[:SPAN], refs[SPAN:]
    cot_refs, refs = refs[:SPAN], refs[SPAN:]
    (
        wide_ref,
        half_ref,
        all_ref,
        small_ref,
        up_bias_ref,
        out_weight,
        cot_ref,
        hidden_ref,
        act_ref,
        pre_ref,
        residual_ref,
        near_ref,
        far_ref,
        own_ref,
    ) = refs
    rep = place_ref[0]
    total, width = all_ref.shape
    rows = total // SPAN
    part = attended_refs[0].shape[1]
    half = width // 2
    units = act_ref.shape[1]
    core = rep & 1
    out_weight[:, pl.ds(pl.multiple_of(core * half, half), half)] = wide_ref[:, :half]
    out_weight[:, pl.ds(pl.multiple_of((1 - core) * half, half), half)] = half_ref[...]
    up_columns = slice(half, half + units)
    down_columns = slice(half + units, None)
    for at in range(SPAN):
        cot_ref[pl.ds(pl.multiple_of((rep ^ at) * rows, rows), rows), :] = cot_refs[at][...]
    out_bias, gain, bias = small_ref[4:5, :], small_ref[5:6, :], small_ref[6:7, :]

    @pl.loop(0, SPAN)
    def _(index):
        block = pl.ds(pl.multiple_of(index * rows, rows), rows)
        mixed = out_bias
        for at in range(SPAN):
            from_rows = pl.ds(pl.multiple_of((rep ^ at) * part, part), part)
            mixed = mixed + dot(attended_refs[at][block, :], out_weight[from_rows, :])
        residual = all_ref[block, :].astype(F32) + mixed

        @pl.when(index == rep)
        def _():
            residual_ref[...] = residual

        hidden = (norm_parts(residual)[0] * gain + bias).astype(BF16)
        hidden_ref[block, :] = hidden
        pre_act = dot(hidden, wide_ref[:, up_columns]) + up_bias_ref[...]
        cdf = 0.5 * (1.0 + lax.erf(pre_act * (0.5**0.5)))
        act_ref[block, :] = (pre_act * cdf).astype(BF16)
        slope = cdf + pre_act * (jnp.exp(-0.5 * pre_act * pre_act) * 0.3989422804014327)
        pre_low = (contract_cols(cot_ref[block, :], wide_ref[:, down_columns]) * slope).astype(BF16)
        pre_ref[block, :] = pre_low
        grad = contract_cols(pre_low, wide_ref[:, up_columns])
        send_parts(grad, index ^ rep, near_ref, far_ref, own_ref)


def third_kernel(place_ref, act_ref, hidden_ref, pre_ref, cot_ref, wide_ref, *refs):
    grad_refs, (near_ref, far_ref, own_ref, sum_ref, grad_ref) = refs[:-5], refs[-5:]
    rep = place_ref[0]
    total, width = cot_ref.shape
    rows = total // SPAN
    units = act_ref.shape[1]
    step = units // 3
    for first in range(0, units, step):
        grad_ref[first : first + step, :width] = contract_rows(
            act_ref[:, first : first + step], cot_ref[...]
        ).astype(BF16)
    step = width // 3
    for first in range(0, width, step):
        grad_ref[first : first + step, width:] = contract_rows(
            hidden_ref[:, first : first + step], pre_ref[...]
        ).astype(BF16)
    sum_ref[...] = jnp.broadcast_to(
        jnp.sum(pre_ref[...].astype(F32), axis=0, keepdims=True), sum_ref.shape
    )

    @pl.loop(0, SPAN)
    def _(index):
        block = pl.ds(pl.multiple_of(index * rows, rows), rows)
        send_parts(
            dot(act_ref[block, :], wide_ref[:, -width:]), index ^ rep, near_ref, far_ref, own_ref
        )

    if len(grad_refs) == 2:
        split_halves(place_ref, grad_ref, *grad_refs)
    else:
        grad_refs[0][...] = grad_ref[...]


def fourth_kernel(
    place_ref,
    own_ref,
    near_ref,
    far_ref,
    residual_ref,
    cotangent_ref,
    small_ref,
    resid_grad_ref,
    branch_ref,
    sums_ref,
):
    grad = own_ref[...] + near_ref[own_ref.shape[0] :, :].astype(F32) + far_ref[...].astype(F32)
    normalized, inverse = norm_parts(residual_ref[...])
    cotangent = cotangent_ref[...].astype(F32)
    resid_grad = cotangent + norm_back(normalized, inverse, small_ref[5:6, :], grad)
    branch = resid_grad.astype(BF16)
    resid_grad_ref[...] = resid_grad
    branch_ref[...] = branch
    sums_ref[...] = jnp.zeros_like(sums_ref)
    sums_ref[4:5, :] = jnp.sum(branch.astype(F32), axis=0, keepdims=True)
    sums_ref[5:6, :] = jnp.sum(grad * normalized, axis=0, keepdims=True)
    sums_ref[6:7, :] = jnp.sum(grad, axis=0, keepdims=True)
    sums_ref[7:8, :] = jnp.sum(cotangent, axis=0, keepdims=True)


def fifth_kernel(
    place_ref,
    branch_a,
    branch_b,
    branch_c,
    branch_d,
    attended_a,
    attended_b,
    attended_c,
    attended_d,
    out_weight,
    qkv_weight,
    q_ref,
    k_ref,
    v_ref,
    lse_ref,
    seg_col_ref,
    seg_row_ref,
    all_ref,
    hidden_ref,
    small_ref,
    sums_ref,
    unit_sums_ref,
    *refs,
):
    grad_refs, refs = refs[:-10], refs[-10:]
    (
        near_ref,
        far_ref,
        own_ref,
        branch_ref,
        back_ref,
        proj_ref,
        dk_ref,
        dv_ref,
        small_grads,
        grad_ref,
    ) = refs
    rep = place_ref[0]
    total, width = all_ref.shape
    rows = total // SPAN
    part = q_ref.shape[1]
    own_rows = pl.ds(pl.multiple_of(rep * part, part), part)
    for at, ref in enumerate((branch_a, branch_b, branch_c, branch_d)):
        start = pl.multiple_of((rep ^ at) * rows, rows)
        branch_ref[pl.ds(start, rows), :] = ref[...]
    back_ref[...] = contract_cols(branch_ref[...], out_weight[own_rows, :]).astype(BF16)
    attend_back(
        q_ref,
        k_ref,
        v_ref,
        back_ref,
        lse_ref,
        seg_col_ref,
        seg_row_ref,
        proj_ref,
        dk_ref,
        dv_ref,
    )
    gain = small_ref[0:1, :]
    small_grads[...] = jnp.zeros_like(small_grads)
    small_grads[0:8, :] = sums_ref[...]
    small_grads[8:16, :] = unit_sums_ref[...]

    @pl.loop(0, SPAN)
    def _(index):
        block = pl.ds(pl.multiple_of(index * rows, rows), rows)
        grad = contract_cols(proj_ref[block, :], qkv_weight[...])
        normalized = norm_parts(all_ref[block, :].astype(F32))[0]
        small_grads[0:1, :] += jnp.sum(grad * normalized, axis=0, keepdims=True)
        small_grads[1:2, :] += jnp.sum(grad, axis=0, keepdims=True)
        send_parts(grad, index ^ rep, near_ref, far_ref, own_ref)

    lane = lax.broadcasted_iota(jnp.int32, (1, width), 1)
    mine = (lane >= rep * part) & (lane < (rep + 1) * part)
    for row, first in ((2, 0), (3, 2 * part)):
        column_sum = jnp.sum(
            proj_ref[:, first : first + part].astype(F32), axis=0, keepdims=True
        )
        small_grads[row : row + 1, :] = jnp.where(
            mine, jnp.concatenate([column_sum] * SPAN, axis=1), 0.0
        )
    step = width // 3
    for first in range(0, width, step):
        grad_ref[first : first + step, : 3 * part] = contract_rows(
            hidden_ref[:, first : first + step], proj_ref[...]
        ).astype(BF16)
    branch_part = chosen(
        [branch_ref[:, r * part : (r + 1) * part] for r in range(SPAN)], rep
    )
    for at, ref in enumerate((attended_a, attended_b, attended_c, attended_d)):
        from_rows = pl.ds(pl.multiple_of((rep ^ at) * part, part), part)
        grad_ref[from_rows, 3 * part : 4 * part] = contract_rows(ref[...], branch_part).astype(
            BF16
        )
    grad_ref[:, 4 * part :] = small_grads[...].T[:, :64].astype(BF16)
    if len(grad_refs) == 2:
        split_halves(place_ref, grad_ref, *grad_refs)
    else:
        grad_refs[0][...] = grad_ref[...]


def sixth_kernel(
    place_ref, own_ref, near_ref, far_ref, tokens_ref, resid_grad_ref, small_ref, out_ref
):
    grad = own_ref[...] + near_ref[own_ref.shape[0] :, :].astype(F32) + far_ref[...].astype(F32)
    normalized, inverse = norm_parts(tokens_ref[...].astype(F32))
    out_ref[...] = resid_grad_ref[...] + norm_back(normalized, inverse, small_ref[0:1, :], grad)


def rep_order(refs, rep):
    blocks = [ref[...].astype(F32) for ref in refs]
    odd, high = (rep & 1) == 1, (rep & 2) == 2
    pairs = []
    for first in (0, 2):
        lower, upper = blocks[first], blocks[first + 1]
        pairs.append((jnp.where(odd, upper, lower), jnp.where(odd, lower, upper)))
    low = [jnp.where(high, b, a) for a, b in zip(*pairs)]
    return low + [jnp.where(high, a, b) for a, b in zip(*pairs)]


def adam_kernel(place_ref, *refs):
    blocks = rep_order(refs[:SPAN], place_ref[0])
    ins, outs = refs[SPAN : SPAN + 9], refs[SPAN + 9 :]
    part = ins[3].shape[1] // SPAN
    qkv = [b[:, c * part : (c + 1) * part] for c in range(3) for b in blocks]
    out = [b[:, 3 * part : 4 * part] for b in blocks]
    small = blocks[0][:, 4 * part :]
    for block in blocks[1:]:
        small = small + block[:, 4 * part :]
    small = jnp.concatenate([small, small], axis=1).T[:12, :]
    grads = (jnp.concatenate(qkv, axis=1), jnp.concatenate(out, axis=1), small)
    for at, (gradient, rate) in enumerate(zip(grads, (RATE_MATRIX, RATE_MATRIX, RATE_SMALL))):
        weight, first, second = (ref[...] for ref in ins[3 * at : 3 * at + 3])
        results = adam_update(weight, gradient, first, second, rate)
        for ref, value in zip(outs[3 * at : 3 * at + 3], results):
            ref[...] = value


def in_order(blocks, rep):
    odd = (rep & 1) == 1
    high = (rep & 2) == 2
    low_pair = (jnp.where(odd, blocks[1], blocks[0]), jnp.where(odd, blocks[0], blocks[1]))
    high_pair = (jnp.where(odd, blocks[3], blocks[2]), jnp.where(odd, blocks[2], blocks[3]))
    return (
        jnp.where(high, high_pair[0], low_pair[0]),
        jnp.where(high, high_pair[1], low_pair[1]),
        jnp.where(high, low_pair[0], high_pair[0]),
        jnp.where(high, low_pair[1], high_pair[1]),
    )


def local(
    tokens,
    cotangent,
    segments,
    qkv_weight,
    out_weight,
    up_weight,
    down_weight,
    small_weights,
    qkv_first,
    out_first,
    up_first,
    down_first,
    small_first,
    qkv_second,
    out_second,
    up_second,
    down_second,
    small_second,
):
    rep = lax.axis_index("rep")
    shards = lax.axis_size("shard")
    place = jnp.stack([rep, lax.axis_index("shard")]).astype(jnp.int32)
    rows, width = tokens.shape
    total = SPAN * rows
    part = width // SPAN
    owned = qkv_weight.shape[0]
    ff = up_weight.shape[1]
    ff_part = ff // SPAN
    units = down_weight.shape[0] // SPAN

    def rep_part(block, size, axis):
        return lax.dynamic_slice_in_dim(block, rep * size, size, axis)

    low_small = small_weights.astype(BF16).T
    low_qkv = rep_part(qkv_weight.astype(BF16).reshape(owned, 3, SPAN, part), 1, 2)
    low_qkv = low_qkv.reshape(owned, 3 * part)
    pad = 64 - low_small.shape[1]
    first_send = jnp.concatenate([low_qkv, jnp.pad(low_small, ((0, 0), (0, pad)))], axis=1)
    low_up = rep_part(up_weight.astype(BF16).reshape(owned, shards, SPAN, units), 1, 2)
    low_up = low_up.reshape(owned, ff_part)
    low_down = rep_part(down_weight, units, 0).astype(BF16)
    first_pieces = shard_gather(first_send)
    half = width // 2
    low_out = lax.dynamic_slice_in_dim(out_weight, (rep & 1) * half, half, 1).astype(BF16)
    wide_send = jnp.concatenate([low_out, low_up, low_down], axis=1)
    wide_full = lax.all_gather(wide_send, "shard", axis=0, tiled=True)
    other_half = swapped(wide_full[:, :half], 1)

    seg_block = jnp.pad(segments.astype(BF16)[None, :], ((0, 15), (0, width - rows)))
    token_blocks = rep_blocks(jnp.concatenate([tokens, seg_block], axis=0))
    cot_blocks = rep_blocks(cotangent)

    (
        all_tokens,
        hidden_one,
        qkv_part,
        small,
        queries,
        keys,
        values,
        seg_col,
        seg_row,
        attended,
        log_total,
    ) = call(
        lambda *refs: first_kernel(first_pieces, *refs),
        [
            shape(total, width),
            shape(total, width),
            shape(width, 3 * part),
            shape(16, width, dtype=F32),
            shape(total, part),
            shape(total, part),
            shape(total, part),
            shape(total, 128, dtype=F32),
            shape(8, total, dtype=F32),
            shape(total, part),
            shape(8, total, dtype=F32),
        ],
        [pltpu.VMEM((width, 128), BF16)],
        2 * total * width * 3 * part + 16 * total * total * part,
        24,
        place,
        *token_blocks,
        *first_pieces.arrays,
    )
    up_bias = rep_part(small[8:12].reshape(shards, SPAN, units), 1, 1).reshape(1, -1)
    attended_blocks = rep_blocks(attended)
    (
        out_part,
        all_cot,
        hidden_two,
        act_low,
        pre_low,
        residual,
        near_send,
        far_part,
        own,
    ) = call(
        second_kernel,
        [
            shape(width, width),
            shape(total, width),
            shape(total, width),
            shape(total, ff_part),
            shape(total, ff_part),
            shape(rows, width, dtype=F32),
            shape(2 * rows, width),
            shape(rows, width, dtype=F32),
            shape(rows, width, dtype=F32),
        ],
        [],
        10 * total * width * width,
        36,
        place,
        *attended_blocks,
        *cot_blocks,
        wide_full,
        other_half,
        all_tokens,
        small,
        up_bias,
    )
    few = shards == FEW
    half_rows = ff_part // 2
    near, far, far_send = rep_sum(near_send, far_part)
    hidden_two_terms = own, near, far
    *wide_grad, mixed_near, mixed_far, mixed_own, unit_sums = call(
        third_kernel,
        [shape(half_rows, 2 * width)] * 2 * few
        + [shape(ff_part, 2 * width)] * (not few)
        + [
            shape(2 * rows, width),
            shape(rows, width, dtype=F32),
            shape(rows, width, dtype=F32),
            shape(8, ff_part, dtype=F32),
        ],
        [pltpu.VMEM((ff_part, 2 * width), BF16)],
        6 * total * width * width,
        36,
        place,
        after(act_low, far_send),
        hidden_two,
        pre_low,
        all_cot,
        wide_full,
    )
    resid_grad, branch, sums = call(
        fourth_kernel,
        [
            shape(rows, width, dtype=F32),
            shape(rows, width),
            shape(8, width, dtype=F32),
        ],
        [],
        10 * rows * width,
        16,
        place,
        *hidden_two_terms,
        residual,
        cotangent,
        small,
    )
    branch_blocks = rep_blocks(branch)
    if few:
        kept = after(wide_grad[0], branch_blocks[2])
        wide_own, wide_received = scatter_middle(place, kept, wide_grad[1])
        branch_blocks = (after(branch, wide_own),) + branch_blocks[1:]
    unit_rows = lax.dynamic_update_slice(
        jnp.zeros((shards, SPAN, units), F32), unit_sums[0].reshape(shards, 1, units), (0, rep, 0)
    ).reshape(ff // width, width)
    unit_rows = jnp.pad(unit_rows, ((0, 8 - ff // width), (0, 0)))
    *last_grad, near_send, far_part, own = call(
        fifth_kernel,
        [shape(width // 2, 4 * part + 64)] * 2 * few
        + [shape(width, 4 * part + 64)] * (not few)
        + [
            shape(2 * rows, width),
            shape(rows, width, dtype=F32),
            shape(rows, width, dtype=F32),
        ],
        [
            pltpu.VMEM((total, width), BF16),
            pltpu.VMEM((total, part), BF16),
            pltpu.VMEM((total, 3 * part), BF16),
            pltpu.VMEM((total, part), F32),
            pltpu.VMEM((total, part), F32),
            pltpu.VMEM((128, width), F32),
            pltpu.VMEM((width, 4 * part + 64), BF16),
        ],
        6 * total * width * width + 40 * total * total * part,
        40,
        place,
        *branch_blocks,
        *attended_blocks,
        out_part,
        qkv_part,
        queries,
        keys,
        values,
        log_total,
        seg_col,
        seg_row,
        all_tokens,
        hidden_one,
        small,
        sums,
        unit_rows,
    )
    near, far, far_send = rep_sum(near_send, far_part)
    if few:
        last_own, last_received = scatter_middle(place, *last_grad)
        wide_blocks = rep_blocks(scatter_end(wide_own, wide_received))
    else:
        last_total, wide_total = (
            lax.psum_scatter(grad, "shard", scatter_dimension=0, tiled=True)
            for grad in (last_grad[0], wide_grad[0])
        )
        wide_blocks = rep_blocks(wide_total)
    near_mixed, far_mixed, _ = rep_sum(after(mixed_near, far_send), mixed_far)
    input_grad = call(
        sixth_kernel,
        [shape(rows, width, dtype=F32)],
        [],
        10 * rows * width,
        16,
        place,
        own,
        near,
        far,
        tokens,
        resid_grad,
        small,
    )[0]
    mixed = residual + (
        mixed_own + near_mixed[rows:].astype(F32) + far_mixed.astype(F32) + small[7]
    )
    wide_own = in_order(wide_blocks, rep)
    down_own = jnp.concatenate([g[:, :width] for g in wide_own], axis=0).astype(F32)
    up_own = jnp.stack([g[:, width:].reshape(owned, shards, units) for g in wide_own], axis=2)
    up_own = up_own.reshape(owned, ff).astype(F32)
    up_res = adam_update(up_weight, up_own, up_first, up_second, RATE_MATRIX)
    down_res = adam_update(down_weight, down_own, down_first, down_second, RATE_MATRIX)
    if few:
        last_total = scatter_end(last_own, last_received)
        results = call(
            adam_kernel,
            [shape(*ref.shape, dtype=F32) for ref in (qkv_weight, out_weight, small_weights)
             for _ in range(3)],
            [],
            20 * qkv_weight.size,
            32,
            place,
            *rep_blocks(last_total),
            qkv_weight,
            qkv_first,
            qkv_second,
            out_weight,
            out_first,
            out_second,
            small_weights,
            small_first,
            small_second,
        )
        qkv_res, out_res, small_res = results[:3], results[3:6], results[6:]
    else:
        last_own = in_order(rep_blocks(last_total), rep)
        out_own = jnp.concatenate([g[:, 3 * part : 4 * part] for g in last_own], axis=1)
        qkv_own = [g[:, : 3 * part].reshape(owned, 3, part) for g in last_own]
        qkv_own = jnp.stack(qkv_own, axis=2).reshape(owned, 3 * width).astype(F32)
        small_own = sum(g[:, 4 * part : 4 * part + 12].astype(F32) for g in last_own).T
        qkv_res = adam_update(qkv_weight, qkv_own, qkv_first, qkv_second, RATE_MATRIX)
        out_res = adam_update(
            out_weight, out_own.astype(F32), out_first, out_second, RATE_MATRIX
        )
        small_res = adam_update(
            small_weights, small_own, small_first, small_second, RATE_SMALL
        )
    return (
        mixed.astype(BF16),
        input_grad,
        qkv_res[0],
        out_res[0],
        up_res[0],
        down_res[0],
        small_res[0],
        qkv_res[1],
        out_res[1],
        up_res[1],
        down_res[1],
        small_res[1],
        qkv_res[2],
        out_res[2],
        up_res[2],
        down_res[2],
        small_res[2],
    )


def solution(mesh):
    tokens_spec = P(("rep", "shard"), None)
    rows = P("shard", None)
    columns = P(None, "shard")
    weights = (rows, rows, rows, rows, columns)
    return jax.shard_map(
        local,
        mesh=mesh,
        in_specs=(tokens_spec, tokens_spec, P(("rep", "shard"))) + weights * 3,
        out_specs=(tokens_spec, tokens_spec) + weights * 3,
        check_vma=False,
    )
```

```python
import jax
import jax.numpy as jnp
from jax import lax
from jax.experimental import pallas as pl
from jax.experimental.pallas import tpu as pltpu
from jax.sharding import PartitionSpec as P

HEAD_DIM = 64
SPAN = 4
STEP_NUM = 10


NORM_EPS = 1e-05
BETA_ONE = 0.9
BETA_TWO = 0.95
ADAM_EPS = 1e-08
DECAY = 0.1
RATE_MATRIX = 0.05
RATE_SMALL = 0.3
MASKED = -1e30
BLOCK = 256
FEW = 8
F32 = jnp.float32
BF16 = jnp.bfloat16


def swapped(block, bit):
    return lax.ppermute(block, "rep", [(i, i ^ bit) for i in range(SPAN)])


def rep_blocks(block):
    far = swapped(block, 2)
    near = swapped(block, 1)
    return (block, near, far, swapped(far, 1))


def swap_shard(block, bits):
    return lax.ppermute(block, "shard", [(i, i ^ bits) for i in range(lax.axis_size("shard"))])


def after(block, other):
    return lax.optimization_barrier((block, other))[0]


class Pieces:
    def __init__(self, arrays, codes, rows):
        self.arrays, self.codes, self.rows = arrays, codes, rows

    def place(self, shard, refs, store):
        if self.codes is None:
            store(0, refs[0], 0, refs[0].shape[0])
            return
        for ref, codes in zip(refs, self.codes):
            for index, code in enumerate(codes):
                start = pl.multiple_of((shard ^ code) * self.rows, self.rows)
                store(start, ref, index * self.rows, self.rows)


def shard_gather(block, gate=None):
    shards = lax.axis_size("shard")
    if shards != FEW:
        full = lax.all_gather(block, "shard", axis=0, tiled=True)
        return Pieces([full], None, block.shape[0])
    cross = swap_shard(block, 1)
    sent = block if gate is None else after(block, gate)
    one = swap_shard(sent, 2)
    two = swap_shard(sent, 4)
    three = swap_shard(sent, 6)
    other = swap_shard(jnp.concatenate([one, two, three], axis=0), 1)
    codes = [[0], [1], [2], [4], [6], [3, 5, 7]]
    return Pieces([block, cross, one, two, three, other], codes, block.shape[0])


def scatter(blocks):
    return [blocks[0]] + [swap_shard(block, code + 1) for code, block in enumerate(blocks[1:])]


def scatter_end(blocks):
    total = blocks[0].astype(F32)
    for block in blocks[1:]:
        total = total + block.astype(F32)
    return total.astype(BF16)


def emit(place_ref, full_ref, refs):
    if len(refs) == 1:
        refs[0][...] = full_ref[...]
        return
    rows = full_ref.shape[0] // len(refs)
    for code, ref in enumerate(refs):
        start = pl.multiple_of((place_ref[1] ^ code) * rows, rows)
        ref[...] = full_ref[pl.ds(start, rows), :]


def norm_parts(values):
    center = jnp.mean(values, axis=-1, keepdims=True)
    centered = values - center
    variance = jnp.mean(centered * centered, axis=-1, keepdims=True)
    inverse = lax.rsqrt(variance + NORM_EPS)
    return centered * inverse, inverse


def norm_back(normalized, inverse, gain, grad):
    scaled = grad * gain
    mean_one = jnp.mean(scaled, axis=-1, keepdims=True)
    mean_two = jnp.mean(scaled * normalized, axis=-1, keepdims=True)
    return inverse * (scaled - mean_one - normalized * mean_two)


def contract_rows(left_side, right_side):
    return lax.dot_general(
        left_side, right_side, (((0,), (0,)), ((), ())), preferred_element_type=F32
    )


def contract_cols(left_side, right_side):
    return lax.dot_general(
        left_side, right_side, (((1,), (1,)), ((), ())), preferred_element_type=F32
    )


def adam_update(master, gradient, moment_one, moment_two, step_rate):
    first_new = BETA_ONE * moment_one + (1.0 - BETA_ONE) * gradient
    second_new = BETA_TWO * moment_two + (1.0 - BETA_TWO) * gradient * gradient
    fix_one = 1.0 - BETA_ONE**STEP_NUM
    fix_two = 1.0 - BETA_TWO**STEP_NUM
    step_dir = first_new / fix_one / (jnp.sqrt(second_new / fix_two) + ADAM_EPS)
    return (master - step_rate * (step_dir + DECAY * master), first_new, second_new)


def dot(left_side, right_side):
    return jnp.dot(left_side, right_side, preferred_element_type=F32)


def chosen(values, index):
    result = values[0]
    for at in range(1, len(values)):
        result = jnp.where(index == at, values[at], result)
    return result


def mask_bias(seg_col_ref, seg_row_ref, start, keys):
    same = seg_col_ref[:keys, 0:1] == seg_row_ref[0:1, start : start + BLOCK]
    key_at = lax.broadcasted_iota(jnp.int32, (keys, BLOCK), 0)
    query_at = lax.broadcasted_iota(jnp.int32, (keys, BLOCK), 1) + start
    return jnp.where(same & (key_at <= query_at), 0.0, MASKED)


def head_lanes(shape, head):
    lane = lax.broadcasted_iota(jnp.int32, shape, 1)
    return (lane >= head * HEAD_DIM) & (lane < (head + 1) * HEAD_DIM)


def attend(q_ref, k_ref, v_ref, seg_col_ref, seg_row_ref, out_ref, lse_ref):
    total, width = q_ref.shape
    heads = width // HEAD_DIM
    value_t = v_ref[...].T
    lse_ref[...] = jnp.zeros_like(lse_ref)
    for start in range(0, total, BLOCK):
        keys = start + BLOCK
        bias = mask_bias(seg_col_ref, seg_row_ref, start, keys)
        query = q_ref[start : start + BLOCK, :]
        pieces = []
        for head in range(heads):
            masked = jnp.where(head_lanes(query.shape, head), query, 0)
            scores = contract_cols(k_ref[:keys, :], masked) + bias
            peak = jnp.max(scores, axis=0, keepdims=True)
            exponent = jnp.exp(scores - peak)
            row_total = jnp.sum(exponent, axis=0, keepdims=True)
            mixed = dot(
                value_t[head * HEAD_DIM : (head + 1) * HEAD_DIM, :keys], exponent.astype(BF16)
            )
            pieces.append(mixed / row_total)
            lse_ref[head : head + 1, start : start + BLOCK] = peak + jnp.log(row_total)
        out_ref[start : start + BLOCK, :] = jnp.concatenate(pieces, axis=0).T.astype(BF16)


def attend_back(
    q_ref, k_ref, v_ref, do_ref, lse_ref, seg_col_ref, seg_row_ref, grad_ref, dk_ref, dv_ref
):
    total, width = q_ref.shape
    heads = width // HEAD_DIM
    key_t = k_ref[...].T
    dk_ref[...] = jnp.zeros_like(dk_ref)
    dv_ref[...] = jnp.zeros_like(dv_ref)
    for start in range(0, total, BLOCK):
        keys = start + BLOCK
        bias = mask_bias(seg_col_ref, seg_row_ref, start, keys)
        query = q_ref[start : start + BLOCK, :]
        grad = do_ref[start : start + BLOCK, :]
        pieces = []
        dk = dk_ref[:keys, :]
        dv = dv_ref[:keys, :]
        for head in range(heads):
            lanes = head_lanes(query.shape, head)
            query_h = jnp.where(lanes, query, 0)
            grad_h = jnp.where(lanes, grad, 0)
            scores = contract_cols(k_ref[:keys, :], query_h) + bias
            probs = jnp.exp(scores - lse_ref[head : head + 1, start : start + BLOCK])
            prob_grad = contract_cols(v_ref[:keys, :], grad_h)
            inner = jnp.sum(prob_grad * probs, axis=0, keepdims=True)
            score_grad = (probs * (prob_grad - inner)).astype(BF16)
            dv = dv + dot(probs.astype(BF16), grad_h)
            dk = dk + dot(score_grad, query_h)
            pieces.append(
                dot(key_t[head * HEAD_DIM : (head + 1) * HEAD_DIM, :keys], score_grad)
            )
        dk_ref[:keys, :] = dk
        dv_ref[:keys, :] = dv
        dq = jnp.concatenate(pieces, axis=0).T * HEAD_DIM ** (-0.5)
        grad_ref[start : start + BLOCK, :width] = dq.astype(BF16)
    grad_ref[:, width : 2 * width] = dk_ref[...].astype(BF16)
    grad_ref[:, 2 * width :] = dv_ref[...].astype(BF16)


def call(kernel, outs, scratch, flops, limit, *operands):
    sizes = [o.size * o.dtype.itemsize for o in operands] + [
        o.size * jnp.dtype(o.dtype).itemsize for o in outs
    ]
    vmem = pl.BlockSpec(memory_space=pltpu.VMEM)
    return pl.pallas_call(
        kernel,
        out_shape=tuple(outs),
        in_specs=[pl.BlockSpec(memory_space=pltpu.SMEM)] + [vmem] * (len(operands) - 1),
        out_specs=tuple([vmem] * len(outs)),
        scratch_shapes=scratch,
        compiler_params=pltpu.CompilerParams(vmem_limit_bytes=limit * 2**20),
        cost_estimate=pl.CostEstimate(
            flops=flops, bytes_accessed=sum(sizes), transcendentals=0
        ),
    )(*operands)


def shape(*dims, dtype=BF16):
    return jax.ShapeDtypeStruct(dims, dtype)


def send_parts(value, at, near_ref, far_ref, own_ref):
    rows = value.shape[0]

    @pl.when(at == 0)
    def _():
        own_ref[...] = value

    @pl.when(at == 1)
    def _():
        near_ref[rows:, :] = value.astype(BF16)

    @pl.when(at == 2)
    def _():
        far_ref[...] = value

    @pl.when(at == 3)
    def _():
        near_ref[:rows, :] = value.astype(BF16)


def rep_sum(near_send, far_part, gate=None):
    rows = far_part.shape[0]
    near = swapped(near_send, 1)
    far_send = (far_part + near[:rows].astype(F32)).astype(BF16)
    if gate is not None:
        far_send = after(far_send, gate)
    return near, swapped(far_send, 2), far_send


def place_store(target, columns, limit=None):
    def store(start, ref, first, rows):
        target[pl.ds(start, rows), :limit] = ref[first : first + rows, columns]

    return store


def prep_kernel(
    place_ref,
    qkv_ref,
    out_ref,
    up_ref,
    down_ref,
    small_ref,
    first_ref,
    second_ref,
    third_ref,
    small_rows,
):
    rep = place_ref[0]
    owned, width = out_ref.shape
    part, half = width // SPAN, width // 2
    units = third_ref.shape[0]
    small_rows[...] = jnp.zeros_like(small_rows)
    small_rows[: small_ref.shape[0], : small_ref.shape[1]] = small_ref[...]
    for which in range(3):
        first = which * width
        options = [qkv_ref[:, first + r * part : first + (r + 1) * part] for r in range(SPAN)]
        first_ref[:, which * part : (which + 1) * part] = chosen(options, rep).astype(BF16)
    first_ref[:, 3 * part :] = small_rows[...].T[:owned, :64].astype(BF16)
    second_ref[:, :half] = out_ref[:, :half].astype(BF16)
    pieces = []
    for first in range(0, up_ref.shape[1], SPAN * units):
        options = [up_ref[:, first + r * units : first + (r + 1) * units] for r in range(SPAN)]
        pieces.append(chosen(options, rep))
    second_ref[:, half:] = jnp.concatenate(pieces, axis=1).astype(BF16)
    third_ref[:, :half] = out_ref[:, half:].astype(BF16)
    start = pl.multiple_of(rep * units, units)
    third_ref[:, half:] = down_ref[pl.ds(start, units), :].astype(BF16)


def first_kernel(pieces, *refs):
    place_ref, refs = refs[0], refs[1:]
    token_refs, refs = refs[:SPAN], refs[SPAN:]
    count = len(pieces.arrays)
    weight_refs, refs = refs[:count], refs[count:]
    (
        all_ref,
        weight_ref,
        small_ref,
        q_ref,
        k_ref,
        v_ref,
        seg_col_ref,
        seg_row_ref,
        out_ref,
        lse_ref,
        small_cols,
    ) = refs
    rep, shard = place_ref[0], place_ref[1]
    total, width = all_ref.shape
    rows = total // SPAN
    part = q_ref.shape[1]
    pieces.place(shard, weight_refs, place_store(weight_ref, slice(0, 3 * part)))
    last = small_cols.shape[1]
    pieces.place(
        shard, weight_refs, place_store(small_cols, slice(3 * part + 64 - last, 3 * part + 64))
    )
    small = small_cols[...].astype(F32).T
    small = small[last - 64 : last - 48, :]
    small_ref[...] = small
    gain, bias = small[0:1, :], small[1:2, :]
    query_bias = chosen([small[2:3, r * part : (r + 1) * part] for r in range(SPAN)], rep)
    value_bias = chosen([small[3:4, r * part : (r + 1) * part] for r in range(SPAN)], rep)
    for at in range(SPAN):
        start = pl.multiple_of((rep ^ at) * rows, rows)
        block = token_refs[at][:rows, :]
        all_ref[pl.ds(start, rows), :] = block
        hidden = (norm_parts(block.astype(F32))[0] * gain + bias).astype(BF16)
        segs = token_refs[at][rows : rows + 16, :rows].astype(F32)
        seg_row_ref[:, pl.ds(start, rows)] = segs[:8, :]
        seg_col_ref[pl.ds(start, rows), 0:16] = segs.T
        projected = dot(hidden, weight_ref[...])
        q_ref[pl.ds(start, rows), :] = (
            (projected[:, :part] + query_bias) * HEAD_DIM ** (-0.5)
        ).astype(BF16)
        k_ref[pl.ds(start, rows), :] = projected[:, part : 2 * part].astype(BF16)
        v_ref[pl.ds(start, rows), :] = (projected[:, 2 * part :] + value_bias).astype(BF16)
    attend(q_ref, k_ref, v_ref, seg_col_ref, seg_row_ref, out_ref, lse_ref)


def second_kernel(pieces, place_ref, *refs):
    attended_refs, refs = refs[:SPAN], refs[SPAN:]
    cot_refs, refs = refs[:SPAN], refs[SPAN:]
    count = len(pieces.arrays)
    piece_refs, refs = refs[:count], refs[count:]
    (
        wide_ref,
        all_ref,
        small_ref,
        up_bias_ref,
        out_weight,
        cot_ref,
        hidden_ref,
        act_ref,
        pre_ref,
        residual_ref,
        near_ref,
        far_ref,
        own_ref,
        up_weight,
    ) = refs
    rep = place_ref[0]
    total, width = all_ref.shape
    rows = total // SPAN
    part = attended_refs[0].shape[1]
    half = width // 2
    pieces.place(place_ref[1], piece_refs, place_store(up_weight, slice(half, None)))
    pieces.place(place_ref[1], piece_refs, place_store(out_weight, slice(0, half), half))
    out_weight[:, half:] = wide_ref[:, :half]
    for at in range(SPAN):
        cot_ref[pl.ds(pl.multiple_of((rep ^ at) * rows, rows), rows), :] = cot_refs[at][...]
    out_bias, gain, bias = small_ref[4:5, :], small_ref[5:6, :], small_ref[6:7, :]

    @pl.loop(0, SPAN)
    def _(index):
        block = pl.ds(pl.multiple_of(index * rows, rows), rows)
        mixed = out_bias
        for at in range(SPAN):
            from_rows = pl.ds(pl.multiple_of((rep ^ at) * part, part), part)
            mixed = mixed + dot(attended_refs[at][block, :], out_weight[from_rows, :])
        residual = all_ref[block, :].astype(F32) + mixed

        @pl.when(index == rep)
        def _():
            residual_ref[...] = residual

        hidden = (norm_parts(residual)[0] * gain + bias).astype(BF16)
        hidden_ref[block, :] = hidden
        pre_act = dot(hidden, up_weight[...]) + up_bias_ref[...]
        cdf = 0.5 * (1.0 + lax.erf(pre_act * (0.5**0.5)))
        act_ref[block, :] = (pre_act * cdf).astype(BF16)
        slope = cdf + pre_act * (jnp.exp(-0.5 * pre_act * pre_act) * 0.3989422804014327)
        pre_low = (contract_cols(cot_ref[block, :], wide_ref[:, half:]) * slope).astype(BF16)
        pre_ref[block, :] = pre_low
        grad = contract_cols(pre_low, up_weight[...])
        send_parts(grad, index ^ rep, near_ref, far_ref, own_ref)


def third_kernel(place_ref, act_ref, hidden_ref, pre_ref, cot_ref, wide_ref, *refs):
    grad_refs, (near_ref, far_ref, own_ref, sum_ref, grad_ref) = refs[:-5], refs[-5:]
    rep = place_ref[0]
    total, width = cot_ref.shape
    rows = total // SPAN
    units = act_ref.shape[1]
    step = units // 3
    for first in range(0, units, step):
        grad_ref[first : first + step, :width] = contract_rows(
            act_ref[:, first : first + step], cot_ref[...]
        ).astype(BF16)
    step = width // 3
    for first in range(0, width, step):
        grad_ref[first : first + step, width:] = contract_rows(
            hidden_ref[:, first : first + step], pre_ref[...]
        ).astype(BF16)
    sum_ref[...] = jnp.broadcast_to(
        jnp.sum(pre_ref[...].astype(F32), axis=0, keepdims=True), sum_ref.shape
    )

    @pl.loop(0, SPAN)
    def _(index):
        block = pl.ds(pl.multiple_of(index * rows, rows), rows)
        send_parts(
            dot(act_ref[block, :], wide_ref[:, -width:]), index ^ rep, near_ref, far_ref, own_ref
        )

    emit(place_ref, grad_ref, grad_refs)

def fourth_kernel(
    place_ref,
    own_ref,
    near_ref,
    far_ref,
    residual_ref,
    cotangent_ref,
    small_ref,
    resid_grad_ref,
    branch_ref,
    sums_ref,
):
    grad = own_ref[...] + near_ref[own_ref.shape[0] :, :].astype(F32) + far_ref[...].astype(F32)
    normalized, inverse = norm_parts(residual_ref[...])
    cotangent = cotangent_ref[...].astype(F32)
    resid_grad = cotangent + norm_back(normalized, inverse, small_ref[5:6, :], grad)
    branch = resid_grad.astype(BF16)
    resid_grad_ref[...] = resid_grad
    branch_ref[...] = branch
    sums_ref[...] = jnp.zeros_like(sums_ref)
    sums_ref[4:5, :] = jnp.sum(branch.astype(F32), axis=0, keepdims=True)
    sums_ref[5:6, :] = jnp.sum(grad * normalized, axis=0, keepdims=True)
    sums_ref[6:7, :] = jnp.sum(grad, axis=0, keepdims=True)
    sums_ref[7:8, :] = jnp.sum(cotangent, axis=0, keepdims=True)


def fifth_kernel(
    place_ref,
    branch_a,
    branch_b,
    branch_c,
    branch_d,
    attended_a,
    attended_b,
    attended_c,
    attended_d,
    out_weight,
    qkv_weight,
    q_ref,
    k_ref,
    v_ref,
    lse_ref,
    seg_col_ref,
    seg_row_ref,
    all_ref,
    small_ref,
    sums_ref,
    unit_sums_ref,
    *refs,
):
    grad_refs, refs = refs[:-11], refs[-11:]
    (
        near_ref,
        far_ref,
        own_ref,
        branch_ref,
        back_ref,
        proj_ref,
        dk_ref,
        dv_ref,
        small_grads,
        grad_ref,
        hidden_ref,
    ) = refs
    rep = place_ref[0]
    total, width = all_ref.shape
    rows = total // SPAN
    part = q_ref.shape[1]
    own_rows = pl.ds(pl.multiple_of(rep * part, part), part)
    for at, ref in enumerate((branch_a, branch_b, branch_c, branch_d)):
        start = pl.multiple_of((rep ^ at) * rows, rows)
        branch_ref[pl.ds(start, rows), :] = ref[...]
    back_ref[...] = contract_cols(branch_ref[...], out_weight[own_rows, :]).astype(BF16)
    attend_back(
        q_ref,
        k_ref,
        v_ref,
        back_ref,
        lse_ref,
        seg_col_ref,
        seg_row_ref,
        proj_ref,
        dk_ref,
        dv_ref,
    )
    gain = small_ref[0:1, :]
    small_grads[...] = jnp.zeros_like(small_grads)
    small_grads[0:8, :] = sums_ref[...]
    small_grads[8:16, :] = unit_sums_ref[...]

    @pl.loop(0, SPAN)
    def _(index):
        block = pl.ds(pl.multiple_of(index * rows, rows), rows)
        grad = contract_cols(proj_ref[block, :], qkv_weight[...])
        normalized = norm_parts(all_ref[block, :].astype(F32))[0]
        hidden_ref[block, :] = (normalized * gain + small_ref[1:2, :]).astype(BF16)
        small_grads[0:1, :] += jnp.sum(grad * normalized, axis=0, keepdims=True)
        small_grads[1:2, :] += jnp.sum(grad, axis=0, keepdims=True)
        send_parts(grad, index ^ rep, near_ref, far_ref, own_ref)

    lane = lax.broadcasted_iota(jnp.int32, (1, width), 1)
    mine = (lane >= rep * part) & (lane < (rep + 1) * part)
    for row, first in ((2, 0), (3, 2 * part)):
        column_sum = jnp.sum(
            proj_ref[:, first : first + part].astype(F32), axis=0, keepdims=True
        )
        small_grads[row : row + 1, :] = jnp.where(
            mine, jnp.concatenate([column_sum] * SPAN, axis=1), 0.0
        )
    step = width // 3
    for first in range(0, width, step):
        grad_ref[first : first + step, : 3 * part] = contract_rows(
            hidden_ref[:, first : first + step], proj_ref[...]
        ).astype(BF16)
    branch_part = chosen(
        [branch_ref[:, r * part : (r + 1) * part] for r in range(SPAN)], rep
    )
    for at, ref in enumerate((attended_a, attended_b, attended_c, attended_d)):
        from_rows = pl.ds(pl.multiple_of((rep ^ at) * part, part), part)
        grad_ref[from_rows, 3 * part : 4 * part] = contract_rows(ref[...], branch_part).astype(
            BF16
        )
    grad_ref[:, 4 * part :] = small_grads[...].T[:, :64].astype(BF16)
    emit(place_ref, grad_ref, grad_refs)

def sixth_kernel(
    place_ref, own_ref, near_ref, far_ref, tokens_ref, resid_grad_ref, small_ref, out_ref
):
    grad = own_ref[...] + near_ref[own_ref.shape[0] :, :].astype(F32) + far_ref[...].astype(F32)
    normalized, inverse = norm_parts(tokens_ref[...].astype(F32))
    out_ref[...] = resid_grad_ref[...] + norm_back(normalized, inverse, small_ref[0:1, :], grad)


def rep_order(refs, rep):
    blocks = [ref[...].astype(F32) for ref in refs]
    odd, high = (rep & 1) == 1, (rep & 2) == 2
    pairs = []
    for first in (0, 2):
        lower, upper = blocks[first], blocks[first + 1]
        pairs.append((jnp.where(odd, upper, lower), jnp.where(odd, lower, upper)))
    low = [jnp.where(high, b, a) for a, b in zip(*pairs)]
    return low + [jnp.where(high, a, b) for a, b in zip(*pairs)]


def adam_kernel(place_ref, *refs):
    blocks = rep_order(refs[:SPAN], place_ref[0])
    ins, outs = refs[SPAN : SPAN + 9], refs[SPAN + 9 :]
    part = ins[3].shape[1] // SPAN
    qkv = [b[:, c * part : (c + 1) * part] for c in range(3) for b in blocks]
    out = [b[:, 3 * part : 4 * part] for b in blocks]
    small = blocks[0][:, 4 * part :]
    for block in blocks[1:]:
        small = small + block[:, 4 * part :]
    small = jnp.concatenate([small, small], axis=1).T[:12, :]
    grads = (jnp.concatenate(qkv, axis=1), jnp.concatenate(out, axis=1), small)
    for at, (gradient, rate) in enumerate(zip(grads, (RATE_MATRIX, RATE_MATRIX, RATE_SMALL))):
        weight, first, second = (ref[...] for ref in ins[3 * at : 3 * at + 3])
        results = adam_update(weight, gradient, first, second, rate)
        for ref, value in zip(outs[3 * at : 3 * at + 3], results):
            ref[...] = value


def up_adam_kernel(place_ref, *refs):
    blocks = rep_order(refs[:SPAN], place_ref[0])
    weight, first, second, *outs = refs[SPAN:]
    width = weight.shape[1] // SPAN
    units = width // FEW
    pieces = [b[:, at * units : (at + 1) * units] for at in range(FEW) for b in blocks]
    results = adam_update(
        weight[...], jnp.concatenate(pieces, axis=1), first[...], second[...], RATE_MATRIX
    )
    for ref, value in zip(outs, results):
        ref[...] = value


def down_adam_kernel(place_ref, *refs):
    at = pl.program_id(0) ^ place_ref[0]
    gradient = chosen([ref[...] for ref in refs[:SPAN]], at).astype(F32)
    weight, first, second, *outs = refs[SPAN:]
    results = adam_update(weight[...], gradient, first[...], second[...], RATE_MATRIX)
    for ref, value in zip(outs, results):
        ref[...] = value


def grid_adam(kernel, steps, place, blocks, block_spec, arrays):
    rows, columns = arrays[0].shape
    spec = pl.BlockSpec((rows // steps, columns), lambda i: (i, 0))
    return pl.pallas_call(
        kernel,
        grid=(steps,),
        out_shape=[shape(rows, columns, dtype=F32)] * 3,
        in_specs=[pl.BlockSpec(memory_space=pltpu.SMEM)]
        + [block_spec] * SPAN
        + [spec] * 3,
        out_specs=[spec] * 3,
        compiler_params=pltpu.CompilerParams(vmem_limit_bytes=16 * 2**20),
        cost_estimate=pl.CostEstimate(
            flops=20 * rows * columns, bytes_accessed=26 * rows * columns, transcendentals=0
        ),
    )(place, *blocks, *arrays)


def in_order(blocks, rep):
    odd = (rep & 1) == 1
    high = (rep & 2) == 2
    low_pair = (jnp.where(odd, blocks[1], blocks[0]), jnp.where(odd, blocks[0], blocks[1]))
    high_pair = (jnp.where(odd, blocks[3], blocks[2]), jnp.where(odd, blocks[2], blocks[3]))
    return (
        jnp.where(high, high_pair[0], low_pair[0]),
        jnp.where(high, high_pair[1], low_pair[1]),
        jnp.where(high, low_pair[0], high_pair[0]),
        jnp.where(high, low_pair[1], high_pair[1]),
    )


def local(
    tokens,
    cotangent,
    segments,
    qkv_weight,
    out_weight,
    up_weight,
    down_weight,
    small_weights,
    qkv_first,
    out_first,
    up_first,
    down_first,
    small_first,
    qkv_second,
    out_second,
    up_second,
    down_second,
    small_second,
):
    rep = lax.axis_index("rep")
    shards = lax.axis_size("shard")
    place = jnp.stack([rep, lax.axis_index("shard")]).astype(jnp.int32)
    rows, width = tokens.shape
    total = SPAN * rows
    part = width // SPAN
    owned = qkv_weight.shape[0]
    ff = up_weight.shape[1]
    ff_part = ff // SPAN
    units = down_weight.shape[0] // SPAN

    def rep_part(block, size, axis):
        return lax.dynamic_slice_in_dim(block, rep * size, size, axis)

    few = shards == FEW
    half = width // 2
    if few:
        first_send, second_send, third_send = call(
            prep_kernel,
            [
                shape(owned, 3 * part + 64),
                shape(owned, half + ff_part),
                shape(units, half + width),
            ],
            [pltpu.VMEM((128, 128), F32)],
            owned * width,
            16,
            place,
            qkv_weight,
            out_weight,
            up_weight,
            down_weight,
            small_weights,
        )
    else:
        low_small = small_weights.astype(BF16).T
        low_qkv = rep_part(qkv_weight.astype(BF16).reshape(owned, 3, SPAN, part), 1, 2)
        low_qkv = low_qkv.reshape(owned, 3 * part)
        pad = 64 - low_small.shape[1]
        first_send = jnp.concatenate([low_qkv, jnp.pad(low_small, ((0, 0), (0, pad)))], axis=1)
        low_up = rep_part(up_weight.astype(BF16).reshape(owned, shards, SPAN, units), 1, 2)
        low_down = rep_part(down_weight, units, 0).astype(BF16)
        low_out = out_weight.astype(BF16)
        second_send = jnp.concatenate([low_out[:, :half], low_up.reshape(owned, -1)], axis=1)
        third_send = jnp.concatenate([low_out[:, half:], low_down], axis=1)
    third_full = lax.all_gather(third_send, "shard", axis=0, tiled=True)
    first_pieces = shard_gather(first_send)
    second_pieces = shard_gather(second_send, first_pieces.arrays[-2 * few])

    seg_block = jnp.pad(segments.astype(BF16)[None, :], ((0, 15), (0, width - rows)))
    token_blocks = rep_blocks(jnp.concatenate([tokens, seg_block], axis=0))
    cot_blocks = rep_blocks(after(cotangent, token_blocks[2]))

    (
        all_tokens,
        qkv_part,
        small,
        queries,
        keys,
        values,
        seg_col,
        seg_row,
        attended,
        log_total,
    ) = call(
        lambda *refs: first_kernel(first_pieces, *refs),
        [
            shape(total, width),
            shape(width, 3 * part),
            shape(16, width, dtype=F32),
            shape(total, part),
            shape(total, part),
            shape(total, part),
            shape(total, 128, dtype=F32),
            shape(8, total, dtype=F32),
            shape(total, part),
            shape(8, total, dtype=F32),
        ],
        [pltpu.VMEM((width, 128), BF16)],
        2 * total * width * 3 * part + 16 * total * total * part,
        20,
        place,
        *token_blocks,
        *first_pieces.arrays,
    )
    up_bias = rep_part(small[8:12].reshape(shards, SPAN, units), 1, 1).reshape(1, -1)
    attended_blocks = rep_blocks(attended)
    (
        out_part,
        all_cot,
        hidden_two,
        act_low,
        pre_low,
        residual,
        near_send,
        far_part,
        own,
    ) = call(
        lambda *refs: second_kernel(second_pieces, *refs),
        [
            shape(width, width),
            shape(total, width),
            shape(total, width),
            shape(total, ff_part),
            shape(total, ff_part),
            shape(rows, width, dtype=F32),
            shape(2 * rows, width),
            shape(rows, width, dtype=F32),
            shape(rows, width, dtype=F32),
        ],
        [pltpu.VMEM((width, ff_part), BF16)],
        10 * total * width * width,
        28,
        place,
        *attended_blocks,
        *cot_blocks,
        *second_pieces.arrays,
        third_full,
        all_tokens,
        small,
        up_bias,
    )
    near, far, far_send = rep_sum(near_send, far_part)
    hidden_two_terms = own, near, far
    *wide_grad, mixed_near, mixed_far, mixed_own, unit_sums = call(
        third_kernel,
        [shape(owned, 2 * width)] * FEW * few
        + [shape(ff_part, 2 * width)] * (not few)
        + [
            shape(2 * rows, width),
            shape(rows, width, dtype=F32),
            shape(rows, width, dtype=F32),
            shape(8, ff_part, dtype=F32),
        ],
        [pltpu.VMEM((ff_part, 2 * width), BF16)],
        6 * total * width * width,
        22,
        place,
        after(act_low, far_send),
        hidden_two,
        pre_low,
        all_cot,
        third_full,
    )
    if few:
        wide_blocks = scatter(lax.optimization_barrier((wide_grad, far))[0])
    resid_grad, branch, sums = call(
        fourth_kernel,
        [
            shape(rows, width, dtype=F32),
            shape(rows, width),
            shape(8, width, dtype=F32),
        ],
        [],
        10 * rows * width,
        16,
        place,
        *hidden_two_terms,
        residual,
        cotangent,
        small,
    )
    branch_blocks = rep_blocks(branch)
    near_mixed, far_mixed, _ = rep_sum(after(mixed_near, branch), mixed_far, branch_blocks[2])
    unit_rows = lax.dynamic_update_slice(
        jnp.zeros((shards, SPAN, units), F32), unit_sums[0].reshape(shards, 1, units), (0, rep, 0)
    ).reshape(ff // width, width)
    unit_rows = jnp.pad(unit_rows, ((0, 8 - ff // width), (0, 0)))
    *last_grad, near_send, far_part, own = call(
        fifth_kernel,
        [shape(owned, 4 * part + 64)] * FEW * few
        + [shape(width, 4 * part + 64)] * (not few)
        + [
            shape(2 * rows, width),
            shape(rows, width, dtype=F32),
            shape(rows, width, dtype=F32),
        ],
        [
            pltpu.VMEM((total, width), BF16),
            pltpu.VMEM((total, part), BF16),
            pltpu.VMEM((total, 3 * part), BF16),
            pltpu.VMEM((total, part), F32),
            pltpu.VMEM((total, part), F32),
            pltpu.VMEM((128, width), F32),
            pltpu.VMEM((width, 4 * part + 64), BF16),
            pltpu.VMEM((total, width), BF16),
        ],
        6 * total * width * width + 40 * total * total * part,
        32,
        place,
        *branch_blocks,
        *attended_blocks,
        out_part,
        qkv_part,
        queries,
        keys,
        values,
        log_total,
        seg_col,
        seg_row,
        all_tokens,
        small,
        sums,
        unit_rows,
    )
    near, far, far_send = rep_sum(near_send, far_part)
    if few:
        last_blocks = scatter(last_grad)
        wide_blocks = rep_blocks(scatter_end(wide_blocks))
    else:
        last_total, wide_total = (
            lax.psum_scatter(grad, "shard", scatter_dimension=0, tiled=True)
            for grad in (last_grad[0], wide_grad[0])
        )
        wide_blocks = rep_blocks(wide_total)
    mixed = residual + (
        mixed_own + near_mixed[rows:].astype(F32) + far_mixed.astype(F32) + small[7]
    )
    mixed = mixed.astype(BF16)
    input_grad = call(
        sixth_kernel,
        [shape(rows, width, dtype=F32)],
        [],
        10 * rows * width,
        16,
        place,
        own,
        near,
        far,
        tokens,
        resid_grad,
        small,
    )[0]
    if few:
        up_res = grid_adam(
            up_adam_kernel,
            3,
            place,
            wide_blocks,
            pl.BlockSpec((owned // 3, width), lambda i: (i, 1)),
            (up_weight, up_first, up_second),
        )
        down_res = grid_adam(
            down_adam_kernel,
            SPAN,
            place,
            wide_blocks,
            pl.BlockSpec((units, width), lambda i: (0, 0)),
            (down_weight, down_first, down_second),
        )
        last_blocks, input_grad, mixed = lax.optimization_barrier(
            (last_blocks, input_grad, mixed)
        )
        last_total = scatter_end(last_blocks)
        results = call(
            adam_kernel,
            [shape(*ref.shape, dtype=F32) for ref in (qkv_weight, out_weight, small_weights)
             for _ in range(3)],
            [],
            20 * qkv_weight.size,
            24,
            place,
            *rep_blocks(last_total),
            qkv_weight,
            qkv_first,
            qkv_second,
            out_weight,
            out_first,
            out_second,
            small_weights,
            small_first,
            small_second,
        )
        qkv_res, out_res, small_res = results[:3], results[3:6], results[6:]
    else:
        wide_own = in_order(wide_blocks, rep)
        down_own = jnp.concatenate([g[:, :width] for g in wide_own], axis=0).astype(F32)
        up_own = [g[:, width:].reshape(owned, shards, units) for g in wide_own]
        up_own = jnp.stack(up_own, axis=2).reshape(owned, ff).astype(F32)
        up_res = adam_update(up_weight, up_own, up_first, up_second, RATE_MATRIX)
        down_res = adam_update(down_weight, down_own, down_first, down_second, RATE_MATRIX)
        last_own = in_order(rep_blocks(last_total), rep)
        out_own = jnp.concatenate([g[:, 3 * part : 4 * part] for g in last_own], axis=1)
        qkv_own = [g[:, : 3 * part].reshape(owned, 3, part) for g in last_own]
        qkv_own = jnp.stack(qkv_own, axis=2).reshape(owned, 3 * width).astype(F32)
        small_own = sum(g[:, 4 * part : 4 * part + 12].astype(F32) for g in last_own).T
        qkv_res = adam_update(qkv_weight, qkv_own, qkv_first, qkv_second, RATE_MATRIX)
        out_res = adam_update(
            out_weight, out_own.astype(F32), out_first, out_second, RATE_MATRIX
        )
        small_res = adam_update(
            small_weights, small_own, small_first, small_second, RATE_SMALL
        )
    return (
        mixed,
        input_grad,
        qkv_res[0],
        out_res[0],
        up_res[0],
        down_res[0],
        small_res[0],
        qkv_res[1],
        out_res[1],
        up_res[1],
        down_res[1],
        small_res[1],
        qkv_res[2],
        out_res[2],
        up_res[2],
        down_res[2],
        small_res[2],
    )


def solution(mesh):
    tokens_spec = P(("rep", "shard"), None)
    rows = P("shard", None)
    columns = P(None, "shard")
    weights = (rows, rows, rows, rows, columns)
    return jax.shard_map(
        local,
        mesh=mesh,
        in_specs=(tokens_spec, tokens_spec, P(("rep", "shard"))) + weights * 3,
        out_specs=(tokens_spec, tokens_spec) + weights * 3,
        check_vma=False,
    )
```

```python
import jax
import jax.numpy as jnp
from jax import lax
from jax.experimental import pallas as pl
from jax.experimental.pallas import tpu as pltpu
from jax.sharding import PartitionSpec as P

HEAD_DIM = 64
SPAN = 4
STEP_NUM = 10


NORM_EPS = 1e-05
BETA_ONE = 0.9
BETA_TWO = 0.95
ADAM_EPS = 1e-08
DECAY = 0.1
RATE_MATRIX = 0.05
RATE_SMALL = 0.3
MASKED = -1e30
BLOCK = 256
FEW = 8
F32 = jnp.float32
BF16 = jnp.bfloat16


def swapped(block, bit):
    return lax.ppermute(block, "rep", [(i, i ^ bit) for i in range(SPAN)])


def rep_blocks(block):
    far = swapped(block, 2)
    near = swapped(block, 1)
    return (block, near, far, swapped(far, 1))


def swap_shard(block, bits):
    return lax.ppermute(block, "shard", [(i, i ^ bits) for i in range(lax.axis_size("shard"))])


def after(block, other):
    return lax.optimization_barrier((block, other))[0]


class Pieces:
    def __init__(self, arrays, codes, rows):
        self.arrays, self.codes, self.rows = arrays, codes, rows

    def place(self, shard, refs, store):
        if self.codes is None:
            store(0, refs[0], 0, refs[0].shape[0])
            return
        for ref, codes in zip(refs, self.codes):
            for index, code in enumerate(codes):
                start = pl.multiple_of((shard ^ code) * self.rows, self.rows)
                store(start, ref, index * self.rows, self.rows)


def shard_gather(block, gate=None):
    shards = lax.axis_size("shard")
    if shards != FEW:
        full = lax.all_gather(block, "shard", axis=0, tiled=True)
        return Pieces([full], None, block.shape[0])
    cross = swap_shard(block, 1)
    sent = block if gate is None else after(block, (gate, cross))
    one = swap_shard(sent, 2)
    two = swap_shard(sent, 4)
    three = swap_shard(sent, 6)
    other = jnp.concatenate([one, two, three], axis=0)
    other = swap_shard(after(other, cross), 1)
    codes = [[0], [1], [2], [4], [6], [3, 5, 7]]
    return Pieces([block, cross, one, two, three, other], codes, block.shape[0])


def middle_kernel(place_ref, kept_ref, received_ref, own_ref, *sent_refs):
    high = place_ref[1] // 2
    rows = own_ref.shape[0]
    for bits in range(len(sent_refs) + 1):
        block = pl.ds(pl.multiple_of((high ^ bits) * rows, rows), rows)
        value = kept_ref[block, :].astype(F32) + received_ref[block, :].astype(F32)
        if bits == 0:
            own_ref[...] = value
        else:
            sent_refs[bits - 1][...] = value.astype(BF16)


def scatter_middle(place, kept, sent):
    received = swap_shard(sent, 1)
    count = FEW // 2
    rows, columns = kept.shape[0] // count, kept.shape[1]
    own, *sends = call(
        middle_kernel,
        [shape(rows, columns, dtype=F32)] + [shape(rows, columns)] * (count - 1),
        [],
        kept.size,
        56,
        place,
        kept,
        received,
    )
    return own, [swap_shard(send, 2 * (bits + 1)) for bits, send in enumerate(sends)]


def scatter_end(own, received):
    total = own
    for block in received:
        total = total + block.astype(F32)
    return total.astype(BF16)


def split_halves(place_ref, full_ref, kept_ref, sent_ref):
    low = place_ref[1] & 1
    rows = full_ref.shape[0] // FEW
    for at in range(FEW // 2):
        target = slice(at * rows, (at + 1) * rows)
        for ref, bit in ((kept_ref, low), (sent_ref, 1 - low)):
            start = pl.multiple_of((2 * at + bit) * rows, rows)
            ref[target, :] = full_ref[pl.ds(start, rows), :]


def norm_parts(values):
    center = jnp.mean(values, axis=-1, keepdims=True)
    centered = values - center
    variance = jnp.mean(centered * centered, axis=-1, keepdims=True)
    inverse = lax.rsqrt(variance + NORM_EPS)
    return centered * inverse, inverse


def norm_back(normalized, inverse, gain, grad):
    scaled = grad * gain
    mean_one = jnp.mean(scaled, axis=-1, keepdims=True)
    mean_two = jnp.mean(scaled * normalized, axis=-1, keepdims=True)
    return inverse * (scaled - mean_one - normalized * mean_two)


def contract_rows(left_side, right_side):
    return lax.dot_general(
        left_side, right_side, (((0,), (0,)), ((), ())), preferred_element_type=F32
    )


def contract_cols(left_side, right_side):
    return lax.dot_general(
        left_side, right_side, (((1,), (1,)), ((), ())), preferred_element_type=F32
    )


def adam_update(master, gradient, moment_one, moment_two, step_rate):
    first_new = BETA_ONE * moment_one + (1.0 - BETA_ONE) * gradient
    second_new = BETA_TWO * moment_two + (1.0 - BETA_TWO) * gradient * gradient
    fix_one = 1.0 - BETA_ONE**STEP_NUM
    fix_two = 1.0 - BETA_TWO**STEP_NUM
    step_dir = first_new / fix_one / (jnp.sqrt(second_new / fix_two) + ADAM_EPS)
    return (master - step_rate * (step_dir + DECAY * master), first_new, second_new)


def dot(left_side, right_side):
    return jnp.dot(left_side, right_side, preferred_element_type=F32)


def chosen(values, index):
    result = values[0]
    for at in range(1, len(values)):
        result = jnp.where(index == at, values[at], result)
    return result


def mask_bias(seg_col_ref, seg_row_ref, start, keys):
    same = seg_col_ref[:keys, 0:1] == seg_row_ref[0:1, start : start + BLOCK]
    key_at = lax.broadcasted_iota(jnp.int32, (keys, BLOCK), 0)
    query_at = lax.broadcasted_iota(jnp.int32, (keys, BLOCK), 1) + start
    return jnp.where(same & (key_at <= query_at), 0.0, MASKED)


def head_lanes(shape, head):
    lane = lax.broadcasted_iota(jnp.int32, shape, 1)
    return (lane >= head * HEAD_DIM) & (lane < (head + 1) * HEAD_DIM)


def attend(q_ref, k_ref, v_ref, seg_col_ref, seg_row_ref, out_ref, lse_ref):
    total, width = q_ref.shape
    heads = width // HEAD_DIM
    value_t = v_ref[...].T
    lse_ref[...] = jnp.zeros_like(lse_ref)
    for start in range(0, total, BLOCK):
        keys = start + BLOCK
        bias = mask_bias(seg_col_ref, seg_row_ref, start, keys)
        query = q_ref[start : start + BLOCK, :]
        pieces = []
        for head in range(heads):
            masked = jnp.where(head_lanes(query.shape, head), query, 0)
            scores = contract_cols(k_ref[:keys, :], masked) + bias
            peak = jnp.max(scores, axis=0, keepdims=True)
            exponent = jnp.exp(scores - peak)
            row_total = jnp.sum(exponent, axis=0, keepdims=True)
            mixed = dot(
                value_t[head * HEAD_DIM : (head + 1) * HEAD_DIM, :keys], exponent.astype(BF16)
            )
            pieces.append(mixed / row_total)
            lse_ref[head : head + 1, start : start + BLOCK] = peak + jnp.log(row_total)
        out_ref[start : start + BLOCK, :] = jnp.concatenate(pieces, axis=0).T.astype(BF16)


def attend_back(
    q_ref, k_ref, v_ref, do_ref, lse_ref, seg_col_ref, seg_row_ref, grad_ref, dk_ref, dv_ref
):
    total, width = q_ref.shape
    heads = width // HEAD_DIM
    key_t = k_ref[...].T
    dk_ref[...] = jnp.zeros_like(dk_ref)
    dv_ref[...] = jnp.zeros_like(dv_ref)
    for start in range(0, total, BLOCK):
        keys = start + BLOCK
        bias = mask_bias(seg_col_ref, seg_row_ref, start, keys)
        query = q_ref[start : start + BLOCK, :]
        grad = do_ref[start : start + BLOCK, :]
        pieces = []
        dk = dk_ref[:keys, :]
        dv = dv_ref[:keys, :]
        for head in range(heads):
            lanes = head_lanes(query.shape, head)
            query_h = jnp.where(lanes, query, 0)
            grad_h = jnp.where(lanes, grad, 0)
            scores = contract_cols(k_ref[:keys, :], query_h) + bias
            probs = jnp.exp(scores - lse_ref[head : head + 1, start : start + BLOCK])
            prob_grad = contract_cols(v_ref[:keys, :], grad_h)
            inner = jnp.sum(prob_grad * probs, axis=0, keepdims=True)
            score_grad = (probs * (prob_grad - inner)).astype(BF16)
            dv = dv + dot(probs.astype(BF16), grad_h)
            dk = dk + dot(score_grad, query_h)
            pieces.append(
                dot(key_t[head * HEAD_DIM : (head + 1) * HEAD_DIM, :keys], score_grad)
            )
        dk_ref[:keys, :] = dk
        dv_ref[:keys, :] = dv
        dq = jnp.concatenate(pieces, axis=0).T * HEAD_DIM ** (-0.5)
        grad_ref[start : start + BLOCK, :width] = dq.astype(BF16)
    grad_ref[:, width : 2 * width] = dk_ref[...].astype(BF16)
    grad_ref[:, 2 * width :] = dv_ref[...].astype(BF16)


def call(kernel, outs, scratch, flops, limit, *operands):
    sizes = [o.size * o.dtype.itemsize for o in operands] + [
        o.size * jnp.dtype(o.dtype).itemsize for o in outs
    ]
    vmem = pl.BlockSpec(memory_space=pltpu.VMEM)
    return pl.pallas_call(
        kernel,
        out_shape=tuple(outs),
        in_specs=[pl.BlockSpec(memory_space=pltpu.SMEM)] + [vmem] * (len(operands) - 1),
        out_specs=tuple([vmem] * len(outs)),
        scratch_shapes=scratch,
        compiler_params=pltpu.CompilerParams(vmem_limit_bytes=limit * 2**20),
        cost_estimate=pl.CostEstimate(
            flops=flops, bytes_accessed=sum(sizes), transcendentals=0
        ),
    )(*operands)


def shape(*dims, dtype=BF16):
    return jax.ShapeDtypeStruct(dims, dtype)


def send_parts(value, at, near_ref, far_ref, own_ref):
    rows = value.shape[0]

    @pl.when(at == 0)
    def _():
        own_ref[...] = value

    @pl.when(at == 1)
    def _():
        near_ref[rows:, :] = value.astype(BF16)

    @pl.when(at == 2)
    def _():
        far_ref[...] = value

    @pl.when(at == 3)
    def _():
        near_ref[:rows, :] = value.astype(BF16)


def rep_sum(near_send, far_part, gate=None):
    rows = far_part.shape[0]
    near = swapped(near_send, 1)
    far_send = (far_part + near[:rows].astype(F32)).astype(BF16)
    if gate is not None:
        far_send = after(far_send, gate)
    return near, swapped(far_send, 2), far_send


def place_store(target, columns, limit=None):
    def store(start, ref, first, rows):
        target[pl.ds(start, rows), :limit] = ref[first : first + rows, columns]

    return store


def prep_kernel(
    place_ref,
    qkv_ref,
    out_ref,
    up_ref,
    down_ref,
    small_ref,
    first_ref,
    second_ref,
    third_ref,
    small_rows,
):
    rep = place_ref[0]
    owned, width = out_ref.shape
    part, half = width // SPAN, width // 2
    units = third_ref.shape[0]
    small_rows[...] = jnp.zeros_like(small_rows)
    small_rows[: small_ref.shape[0], : small_ref.shape[1]] = small_ref[...]
    for which in range(3):
        first = which * width
        options = [qkv_ref[:, first + r * part : first + (r + 1) * part] for r in range(SPAN)]
        first_ref[:, which * part : (which + 1) * part] = chosen(options, rep).astype(BF16)
    first_ref[:, 3 * part :] = small_rows[...].T[:owned, :64].astype(BF16)
    second_ref[:, :half] = out_ref[:, :half].astype(BF16)
    pieces = []
    for first in range(0, up_ref.shape[1], SPAN * units):
        options = [up_ref[:, first + r * units : first + (r + 1) * units] for r in range(SPAN)]
        pieces.append(chosen(options, rep))
    second_ref[:, half:] = jnp.concatenate(pieces, axis=1).astype(BF16)
    third_ref[:, :half] = out_ref[:, half:].astype(BF16)
    start = pl.multiple_of(rep * units, units)
    third_ref[:, half:] = down_ref[pl.ds(start, units), :].astype(BF16)


def first_kernel(pieces, *refs):
    place_ref, refs = refs[0], refs[1:]
    token_refs, refs = refs[:SPAN], refs[SPAN:]
    count = len(pieces.arrays)
    weight_refs, refs = refs[:count], refs[count:]
    (
        all_ref,
        weight_ref,
        small_ref,
        q_ref,
        k_ref,
        v_ref,
        seg_col_ref,
        seg_row_ref,
        out_ref,
        lse_ref,
        small_cols,
    ) = refs
    rep, shard = place_ref[0], place_ref[1]
    total, width = all_ref.shape
    rows = total // SPAN
    part = q_ref.shape[1]
    pieces.place(shard, weight_refs, place_store(weight_ref, slice(0, 3 * part)))
    last = small_cols.shape[1]
    pieces.place(
        shard, weight_refs, place_store(small_cols, slice(3 * part + 64 - last, 3 * part + 64))
    )
    small = small_cols[...].astype(F32).T
    small = small[last - 64 : last - 48, :]
    small_ref[...] = small
    gain, bias = small[0:1, :], small[1:2, :]
    query_bias = chosen([small[2:3, r * part : (r + 1) * part] for r in range(SPAN)], rep)
    value_bias = chosen([small[3:4, r * part : (r + 1) * part] for r in range(SPAN)], rep)
    for at in range(SPAN):
        start = pl.multiple_of((rep ^ at) * rows, rows)
        block = token_refs[at][:rows, :]
        all_ref[pl.ds(start, rows), :] = block
        hidden = (norm_parts(block.astype(F32))[0] * gain + bias).astype(BF16)
        segs = token_refs[at][rows : rows + 16, :rows].astype(F32)
        seg_row_ref[:, pl.ds(start, rows)] = segs[:8, :]
        seg_col_ref[pl.ds(start, rows), 0:16] = segs.T
        projected = dot(hidden, weight_ref[...])
        q_ref[pl.ds(start, rows), :] = (
            (projected[:, :part] + query_bias) * HEAD_DIM ** (-0.5)
        ).astype(BF16)
        k_ref[pl.ds(start, rows), :] = projected[:, part : 2 * part].astype(BF16)
        v_ref[pl.ds(start, rows), :] = (projected[:, 2 * part :] + value_bias).astype(BF16)
    attend(q_ref, k_ref, v_ref, seg_col_ref, seg_row_ref, out_ref, lse_ref)


def second_kernel(pieces, place_ref, *refs):
    attended_refs, refs = refs[:SPAN], refs[SPAN:]
    cot_refs, refs = refs[:SPAN], refs[SPAN:]
    count = len(pieces.arrays)
    piece_refs, refs = refs[:count], refs[count:]
    (
        wide_ref,
        all_ref,
        small_ref,
        up_bias_ref,
        out_weight,
        cot_ref,
        hidden_ref,
        act_ref,
        pre_ref,
        residual_ref,
        near_ref,
        far_ref,
        own_ref,
        up_weight,
    ) = refs
    rep = place_ref[0]
    total, width = all_ref.shape
    rows = total // SPAN
    part = attended_refs[0].shape[1]
    half = width // 2
    pieces.place(place_ref[1], piece_refs, place_store(up_weight, slice(half, None)))
    pieces.place(place_ref[1], piece_refs, place_store(out_weight, slice(0, half), half))
    out_weight[:, half:] = wide_ref[:, :half]
    for at in range(SPAN):
        cot_ref[pl.ds(pl.multiple_of((rep ^ at) * rows, rows), rows), :] = cot_refs[at][...]
    out_bias, gain, bias = small_ref[4:5, :], small_ref[5:6, :], small_ref[6:7, :]

    @pl.loop(0, SPAN)
    def _(index):
        block = pl.ds(pl.multiple_of(index * rows, rows), rows)
        mixed = out_bias
        for at in range(SPAN):
            from_rows = pl.ds(pl.multiple_of((rep ^ at) * part, part), part)
            mixed = mixed + dot(attended_refs[at][block, :], out_weight[from_rows, :])
        residual = all_ref[block, :].astype(F32) + mixed

        @pl.when(index == rep)
        def _():
            residual_ref[...] = residual

        hidden = (norm_parts(residual)[0] * gain + bias).astype(BF16)
        hidden_ref[block, :] = hidden
        pre_act = dot(hidden, up_weight[...]) + up_bias_ref[...]
        cdf = 0.5 * (1.0 + lax.erf(pre_act * (0.5**0.5)))
        act_ref[block, :] = (pre_act * cdf).astype(BF16)
        slope = cdf + pre_act * (jnp.exp(-0.5 * pre_act * pre_act) * 0.3989422804014327)
        pre_low = (contract_cols(cot_ref[block, :], wide_ref[:, half:]) * slope).astype(BF16)
        pre_ref[block, :] = pre_low
        grad = contract_cols(pre_low, up_weight[...])
        send_parts(grad, index ^ rep, near_ref, far_ref, own_ref)


def third_kernel(place_ref, act_ref, hidden_ref, pre_ref, cot_ref, wide_ref, *refs):
    grad_refs, (near_ref, far_ref, own_ref, sum_ref, grad_ref) = refs[:-5], refs[-5:]
    rep = place_ref[0]
    total, width = cot_ref.shape
    rows = total // SPAN
    units = act_ref.shape[1]
    step = units // 3
    for first in range(0, units, step):
        grad_ref[first : first + step, :width] = contract_rows(
            act_ref[:, first : first + step], cot_ref[...]
        ).astype(BF16)
    step = width // 3
    for first in range(0, width, step):
        grad_ref[first : first + step, width:] = contract_rows(
            hidden_ref[:, first : first + step], pre_ref[...]
        ).astype(BF16)
    sum_ref[...] = jnp.broadcast_to(
        jnp.sum(pre_ref[...].astype(F32), axis=0, keepdims=True), sum_ref.shape
    )

    @pl.loop(0, SPAN)
    def _(index):
        block = pl.ds(pl.multiple_of(index * rows, rows), rows)
        send_parts(
            dot(act_ref[block, :], wide_ref[:, -width:]), index ^ rep, near_ref, far_ref, own_ref
        )

    if len(grad_refs) == 2:
        split_halves(place_ref, grad_ref, *grad_refs)
    else:
        grad_refs[0][...] = grad_ref[...]


def fourth_kernel(
    place_ref,
    own_ref,
    near_ref,
    far_ref,
    residual_ref,
    cotangent_ref,
    small_ref,
    resid_grad_ref,
    branch_ref,
    sums_ref,
):
    grad = own_ref[...] + near_ref[own_ref.shape[0] :, :].astype(F32) + far_ref[...].astype(F32)
    normalized, inverse = norm_parts(residual_ref[...])
    cotangent = cotangent_ref[...].astype(F32)
    resid_grad = cotangent + norm_back(normalized, inverse, small_ref[5:6, :], grad)
    branch = resid_grad.astype(BF16)
    resid_grad_ref[...] = resid_grad
    branch_ref[...] = branch
    sums_ref[...] = jnp.zeros_like(sums_ref)
    sums_ref[4:5, :] = jnp.sum(branch.astype(F32), axis=0, keepdims=True)
    sums_ref[5:6, :] = jnp.sum(grad * normalized, axis=0, keepdims=True)
    sums_ref[6:7, :] = jnp.sum(grad, axis=0, keepdims=True)
    sums_ref[7:8, :] = jnp.sum(cotangent, axis=0, keepdims=True)


def fifth_kernel(
    place_ref,
    branch_a,
    branch_b,
    branch_c,
    branch_d,
    attended_a,
    attended_b,
    attended_c,
    attended_d,
    out_weight,
    qkv_weight,
    q_ref,
    k_ref,
    v_ref,
    lse_ref,
    seg_col_ref,
    seg_row_ref,
    all_ref,
    small_ref,
    sums_ref,
    unit_sums_ref,
    *refs,
):
    grad_refs, refs = refs[:-11], refs[-11:]
    (
        near_ref,
        far_ref,
        own_ref,
        branch_ref,
        back_ref,
        proj_ref,
        dk_ref,
        dv_ref,
        small_grads,
        grad_ref,
        hidden_ref,
    ) = refs
    rep = place_ref[0]
    total, width = all_ref.shape
    rows = total // SPAN
    part = q_ref.shape[1]
    own_rows = pl.ds(pl.multiple_of(rep * part, part), part)
    for at, ref in enumerate((branch_a, branch_b, branch_c, branch_d)):
        start = pl.multiple_of((rep ^ at) * rows, rows)
        branch_ref[pl.ds(start, rows), :] = ref[...]
    back_ref[...] = contract_cols(branch_ref[...], out_weight[own_rows, :]).astype(BF16)
    attend_back(
        q_ref,
        k_ref,
        v_ref,
        back_ref,
        lse_ref,
        seg_col_ref,
        seg_row_ref,
        proj_ref,
        dk_ref,
        dv_ref,
    )
    gain = small_ref[0:1, :]
    small_grads[...] = jnp.zeros_like(small_grads)
    small_grads[0:8, :] = sums_ref[...]
    small_grads[8:16, :] = unit_sums_ref[...]

    @pl.loop(0, SPAN)
    def _(index):
        block = pl.ds(pl.multiple_of(index * rows, rows), rows)
        grad = contract_cols(proj_ref[block, :], qkv_weight[...])
        normalized = norm_parts(all_ref[block, :].astype(F32))[0]
        hidden_ref[block, :] = (normalized * gain + small_ref[1:2, :]).astype(BF16)
        small_grads[0:1, :] += jnp.sum(grad * normalized, axis=0, keepdims=True)
        small_grads[1:2, :] += jnp.sum(grad, axis=0, keepdims=True)
        send_parts(grad, index ^ rep, near_ref, far_ref, own_ref)

    lane = lax.broadcasted_iota(jnp.int32, (1, width), 1)
    mine = (lane >= rep * part) & (lane < (rep + 1) * part)
    for row, first in ((2, 0), (3, 2 * part)):
        column_sum = jnp.sum(
            proj_ref[:, first : first + part].astype(F32), axis=0, keepdims=True
        )
        small_grads[row : row + 1, :] = jnp.where(
            mine, jnp.concatenate([column_sum] * SPAN, axis=1), 0.0
        )
    step = width // 3
    for first in range(0, width, step):
        grad_ref[first : first + step, : 3 * part] = contract_rows(
            hidden_ref[:, first : first + step], proj_ref[...]
        ).astype(BF16)
    branch_part = chosen(
        [branch_ref[:, r * part : (r + 1) * part] for r in range(SPAN)], rep
    )
    for at, ref in enumerate((attended_a, attended_b, attended_c, attended_d)):
        from_rows = pl.ds(pl.multiple_of((rep ^ at) * part, part), part)
        grad_ref[from_rows, 3 * part : 4 * part] = contract_rows(ref[...], branch_part).astype(
            BF16
        )
    grad_ref[:, 4 * part :] = small_grads[...].T[:, :64].astype(BF16)
    if len(grad_refs) == 2:
        split_halves(place_ref, grad_ref, *grad_refs)
    else:
        grad_refs[0][...] = grad_ref[...]


def sixth_kernel(
    place_ref, own_ref, near_ref, far_ref, tokens_ref, resid_grad_ref, small_ref, out_ref
):
    grad = own_ref[...] + near_ref[own_ref.shape[0] :, :].astype(F32) + far_ref[...].astype(F32)
    normalized, inverse = norm_parts(tokens_ref[...].astype(F32))
    out_ref[...] = resid_grad_ref[...] + norm_back(normalized, inverse, small_ref[0:1, :], grad)


def rep_order(refs, rep):
    blocks = [ref[...].astype(F32) for ref in refs]
    odd, high = (rep & 1) == 1, (rep & 2) == 2
    pairs = []
    for first in (0, 2):
        lower, upper = blocks[first], blocks[first + 1]
        pairs.append((jnp.where(odd, upper, lower), jnp.where(odd, lower, upper)))
    low = [jnp.where(high, b, a) for a, b in zip(*pairs)]
    return low + [jnp.where(high, a, b) for a, b in zip(*pairs)]


def adam_kernel(place_ref, *refs):
    blocks = rep_order(refs[:SPAN], place_ref[0])
    ins, outs = refs[SPAN : SPAN + 9], refs[SPAN + 9 :]
    part = ins[3].shape[1] // SPAN
    qkv = [b[:, c * part : (c + 1) * part] for c in range(3) for b in blocks]
    out = [b[:, 3 * part : 4 * part] for b in blocks]
    small = blocks[0][:, 4 * part :]
    for block in blocks[1:]:
        small = small + block[:, 4 * part :]
    small = jnp.concatenate([small, small], axis=1).T[:12, :]
    grads = (jnp.concatenate(qkv, axis=1), jnp.concatenate(out, axis=1), small)
    for at, (gradient, rate) in enumerate(zip(grads, (RATE_MATRIX, RATE_MATRIX, RATE_SMALL))):
        weight, first, second = (ref[...] for ref in ins[3 * at : 3 * at + 3])
        results = adam_update(weight, gradient, first, second, rate)
        for ref, value in zip(outs[3 * at : 3 * at + 3], results):
            ref[...] = value


def up_adam_kernel(place_ref, *refs):
    blocks = rep_order(refs[:SPAN], place_ref[0])
    weight, first, second, *outs = refs[SPAN:]
    width = weight.shape[1] // SPAN
    units = width // FEW
    pieces = [b[:, at * units : (at + 1) * units] for at in range(FEW) for b in blocks]
    results = adam_update(
        weight[...], jnp.concatenate(pieces, axis=1), first[...], second[...], RATE_MATRIX
    )
    for ref, value in zip(outs, results):
        ref[...] = value


def down_adam_kernel(place_ref, *refs):
    at = pl.program_id(0) ^ place_ref[0]
    gradient = chosen([ref[...] for ref in refs[:SPAN]], at).astype(F32)
    weight, first, second, *outs = refs[SPAN:]
    results = adam_update(weight[...], gradient, first[...], second[...], RATE_MATRIX)
    for ref, value in zip(outs, results):
        ref[...] = value


def grid_adam(kernel, steps, place, blocks, block_spec, arrays):
    rows, columns = arrays[0].shape
    spec = pl.BlockSpec((rows // steps, columns), lambda i: (i, 0))
    return list(pl.pallas_call(
        kernel,
        grid=(steps,),
        out_shape=[shape(rows, columns, dtype=F32)] * 3,
        in_specs=[pl.BlockSpec(memory_space=pltpu.SMEM)]
        + [block_spec] * SPAN
        + [spec] * 3,
        out_specs=[spec] * 3,
        compiler_params=pltpu.CompilerParams(vmem_limit_bytes=16 * 2**20),
        cost_estimate=pl.CostEstimate(
            flops=20 * rows * columns, bytes_accessed=26 * rows * columns, transcendentals=0
        ),
    )(place, *blocks, *arrays))


def in_order(blocks, rep):
    odd = (rep & 1) == 1
    high = (rep & 2) == 2
    low_pair = (jnp.where(odd, blocks[1], blocks[0]), jnp.where(odd, blocks[0], blocks[1]))
    high_pair = (jnp.where(odd, blocks[3], blocks[2]), jnp.where(odd, blocks[2], blocks[3]))
    return (
        jnp.where(high, high_pair[0], low_pair[0]),
        jnp.where(high, high_pair[1], low_pair[1]),
        jnp.where(high, low_pair[0], high_pair[0]),
        jnp.where(high, low_pair[1], high_pair[1]),
    )


def local(
    tokens,
    cotangent,
    segments,
    qkv_weight,
    out_weight,
    up_weight,
    down_weight,
    small_weights,
    qkv_first,
    out_first,
    up_first,
    down_first,
    small_first,
    qkv_second,
    out_second,
    up_second,
    down_second,
    small_second,
):
    rep = lax.axis_index("rep")
    shards = lax.axis_size("shard")
    place = jnp.stack([rep, lax.axis_index("shard")]).astype(jnp.int32)
    rows, width = tokens.shape
    total = SPAN * rows
    part = width // SPAN
    owned = qkv_weight.shape[0]
    ff = up_weight.shape[1]
    ff_part = ff // SPAN
    units = down_weight.shape[0] // SPAN

    def rep_part(block, size, axis):
        return lax.dynamic_slice_in_dim(block, rep * size, size, axis)

    few = shards == FEW
    half = width // 2
    if few:
        first_send, second_send, third_send = call(
            prep_kernel,
            [
                shape(owned, 3 * part + 64),
                shape(owned, half + ff_part),
                shape(units, half + width),
            ],
            [pltpu.VMEM((128, 128), F32)],
            owned * width,
            56,
            place,
            qkv_weight,
            out_weight,
            up_weight,
            down_weight,
            small_weights,
        )
    else:
        low_small = small_weights.astype(BF16).T
        low_qkv = rep_part(qkv_weight.astype(BF16).reshape(owned, 3, SPAN, part), 1, 2)
        low_qkv = low_qkv.reshape(owned, 3 * part)
        pad = 64 - low_small.shape[1]
        first_send = jnp.concatenate([low_qkv, jnp.pad(low_small, ((0, 0), (0, pad)))], axis=1)
        low_up = rep_part(up_weight.astype(BF16).reshape(owned, shards, SPAN, units), 1, 2)
        low_down = rep_part(down_weight, units, 0).astype(BF16)
        low_out = out_weight.astype(BF16)
        second_send = jnp.concatenate([low_out[:, :half], low_up.reshape(owned, -1)], axis=1)
        third_send = jnp.concatenate([low_out[:, half:], low_down], axis=1)
    third_full = lax.all_gather(third_send, "shard", axis=0, tiled=True)
    first_pieces = shard_gather(first_send)
    second_pieces = shard_gather(second_send, first_pieces.arrays[-2 * few])

    seg_block = jnp.pad(segments.astype(BF16)[None, :], ((0, 15), (0, width - rows)))
    token_blocks = rep_blocks(jnp.concatenate([tokens, seg_block], axis=0))
    cot_blocks = rep_blocks(after(cotangent, token_blocks[2]))

    (
        all_tokens,
        qkv_part,
        small,
        queries,
        keys,
        values,
        seg_col,
        seg_row,
        attended,
        log_total,
    ) = call(
        lambda *refs: first_kernel(first_pieces, *refs),
        [
            shape(total, width),
            shape(width, 3 * part),
            shape(16, width, dtype=F32),
            shape(total, part),
            shape(total, part),
            shape(total, part),
            shape(total, 128, dtype=F32),
            shape(8, total, dtype=F32),
            shape(total, part),
            shape(8, total, dtype=F32),
        ],
        [pltpu.VMEM((width, 128), BF16)],
        12 * total * width * width + 24 * total * total * part,
        56,
        place,
        *token_blocks,
        *first_pieces.arrays,
    )
    up_bias = rep_part(small[8:12].reshape(shards, SPAN, units), 1, 1).reshape(1, -1)
    attended_blocks = rep_blocks(attended)
    (
        out_part,
        all_cot,
        hidden_two,
        act_low,
        pre_low,
        residual,
        near_send,
        far_part,
        own,
    ) = call(
        lambda *refs: second_kernel(second_pieces, *refs),
        [
            shape(width, width),
            shape(total, width),
            shape(total, width),
            shape(total, ff_part),
            shape(total, ff_part),
            shape(rows, width, dtype=F32),
            shape(2 * rows, width),
            shape(rows, width, dtype=F32),
            shape(rows, width, dtype=F32),
        ],
        [pltpu.VMEM((width, ff_part), BF16)],
        32 * total * width * width,
        56,
        place,
        *attended_blocks,
        *cot_blocks,
        *second_pieces.arrays,
        third_full,
        all_tokens,
        small,
        up_bias,
    )
    near, far, far_send = rep_sum(near_send, far_part)
    hidden_two_terms = own, near, far
    *wide_grad, mixed_near, mixed_far, mixed_own, unit_sums = call(
        third_kernel,
        [shape(ff_part // 2, 2 * width)] * 2 * few
        + [shape(ff_part, 2 * width)] * (not few)
        + [
            shape(2 * rows, width),
            shape(rows, width, dtype=F32),
            shape(rows, width, dtype=F32),
            shape(8, ff_part, dtype=F32),
        ],
        [pltpu.VMEM((ff_part, 2 * width), BF16)],
        18 * total * width * width,
        56,
        place,
        after(act_low, far_send),
        hidden_two,
        pre_low,
        all_cot,
        third_full,
    )
    near, unit_sums = lax.optimization_barrier((near, unit_sums))
    hidden_two_terms = own, near, far
    resid_grad, branch, sums = call(
        fourth_kernel,
        [
            shape(rows, width, dtype=F32),
            shape(rows, width),
            shape(8, width, dtype=F32),
        ],
        [],
        10 * rows * width,
        56,
        place,
        *hidden_two_terms,
        residual,
        cotangent,
        small,
    )
    branch_blocks = rep_blocks(branch)
    near_mixed, far_mixed, _ = rep_sum(after(mixed_near, branch), mixed_far, branch_blocks[2])
    if few:
        kept = after(wide_grad[0], branch_blocks[2])
        wide_own, wide_received = scatter_middle(place, kept, after(wide_grad[1], far))
        branch_blocks = (after(branch, wide_own),) + branch_blocks[1:]
    unit_rows = lax.dynamic_update_slice(
        jnp.zeros((shards, SPAN, units), F32), unit_sums[0].reshape(shards, 1, units), (0, rep, 0)
    ).reshape(ff // width, width)
    unit_rows = jnp.pad(unit_rows, ((0, 8 - ff // width), (0, 0)))
    *last_grad, near_send, far_part, own = call(
        fifth_kernel,
        [shape(width // 2, 4 * part + 64)] * 2 * few
        + [shape(width, 4 * part + 64)] * (not few)
        + [
            shape(2 * rows, width),
            shape(rows, width, dtype=F32),
            shape(rows, width, dtype=F32),
        ],
        [
            pltpu.VMEM((total, width), BF16),
            pltpu.VMEM((total, part), BF16),
            pltpu.VMEM((total, 3 * part), BF16),
            pltpu.VMEM((total, part), F32),
            pltpu.VMEM((total, part), F32),
            pltpu.VMEM((128, width), F32),
            pltpu.VMEM((width, 4 * part + 64), BF16),
            pltpu.VMEM((total, width), BF16),
        ],
        12 * total * width * width + 72 * total * total * part,
        56,
        place,
        *branch_blocks,
        *attended_blocks,
        out_part,
        qkv_part,
        queries,
        keys,
        values,
        log_total,
        seg_col,
        seg_row,
        all_tokens,
        small,
        sums,
        unit_rows,
    )
    near, far, far_send = rep_sum(near_send, far_part)
    if few:
        last_kept, last_sent = last_grad
        last_sent, wide_received = lax.optimization_barrier((last_sent, wide_received))
        last_own, last_received = scatter_middle(place, last_kept, last_sent)
        wide_blocks = rep_blocks(scatter_end(wide_own, wide_received))
    else:
        last_total, wide_total = (
            lax.psum_scatter(grad, "shard", scatter_dimension=0, tiled=True)
            for grad in (last_grad[0], wide_grad[0])
        )
        wide_blocks = rep_blocks(wide_total)
    mixed = residual + (
        mixed_own + near_mixed[rows:].astype(F32) + far_mixed.astype(F32) + small[7]
    )
    mixed = mixed.astype(BF16)
    input_grad = call(
        sixth_kernel,
        [shape(rows, width, dtype=F32)],
        [],
        10 * rows * width,
        56,
        place,
        own,
        near,
        far,
        tokens,
        resid_grad,
        small,
    )[0]
    if few:
        up_res = grid_adam(
            up_adam_kernel,
            3,
            place,
            wide_blocks,
            pl.BlockSpec((owned // 3, width), lambda i: (i, 1)),
            (up_weight, up_first, up_second),
        )
        down_res = grid_adam(
            down_adam_kernel,
            SPAN,
            place,
            wide_blocks,
            pl.BlockSpec((units, width), lambda i: (0, 0)),
            (down_weight, down_first, down_second),
        )
        last_received, input_grad, mixed, up_res[0], down_res[0] = lax.optimization_barrier(
            (last_received, input_grad, mixed, up_res[0], down_res[0])
        )
        last_total = scatter_end(last_own, last_received)
        results = call(
            adam_kernel,
            [shape(*ref.shape, dtype=F32) for ref in (qkv_weight, out_weight, small_weights)
             for _ in range(3)],
            [],
            20 * qkv_weight.size,
            56,
            place,
            *rep_blocks(last_total),
            qkv_weight,
            qkv_first,
            qkv_second,
            out_weight,
            out_first,
            out_second,
            small_weights,
            small_first,
            small_second,
        )
        qkv_res, out_res, small_res = results[:3], results[3:6], results[6:]
    else:
        wide_own = in_order(wide_blocks, rep)
        down_own = jnp.concatenate([g[:, :width] for g in wide_own], axis=0).astype(F32)
        up_own = [g[:, width:].reshape(owned, shards, units) for g in wide_own]
        up_own = jnp.stack(up_own, axis=2).reshape(owned, ff).astype(F32)
        up_res = adam_update(up_weight, up_own, up_first, up_second, RATE_MATRIX)
        down_res = adam_update(down_weight, down_own, down_first, down_second, RATE_MATRIX)
        last_own = in_order(rep_blocks(last_total), rep)
        out_own = jnp.concatenate([g[:, 3 * part : 4 * part] for g in last_own], axis=1)
        qkv_own = [g[:, : 3 * part].reshape(owned, 3, part) for g in last_own]
        qkv_own = jnp.stack(qkv_own, axis=2).reshape(owned, 3 * width).astype(F32)
        small_own = sum(g[:, 4 * part : 4 * part + 12].astype(F32) for g in last_own).T
        qkv_res = adam_update(qkv_weight, qkv_own, qkv_first, qkv_second, RATE_MATRIX)
        out_res = adam_update(
            out_weight, out_own.astype(F32), out_first, out_second, RATE_MATRIX
        )
        small_res = adam_update(
            small_weights, small_own, small_first, small_second, RATE_SMALL
        )
    return (
        mixed,
        input_grad,
        qkv_res[0],
        out_res[0],
        up_res[0],
        down_res[0],
        small_res[0],
        qkv_res[1],
        out_res[1],
        up_res[1],
        down_res[1],
        small_res[1],
        qkv_res[2],
        out_res[2],
        up_res[2],
        down_res[2],
        small_res[2],
    )


def solution(mesh):
    tokens_spec = P(("rep", "shard"), None)
    rows = P("shard", None)
    columns = P(None, "shard")
    weights = (rows, rows, rows, rows, columns)
    return jax.shard_map(
        local,
        mesh=mesh,
        in_specs=(tokens_spec, tokens_spec, P(("rep", "shard"))) + weights * 3,
        out_specs=(tokens_spec, tokens_spec) + weights * 3,
        check_vma=False,
    )
```

```python
import jax
import jax.numpy as jnp
from jax import lax
from jax.experimental import pallas as pl
from jax.experimental.pallas import tpu as pltpu
from jax.sharding import PartitionSpec as P

HEAD_DIM = 64
SPAN = 4
STEP_NUM = 10


NORM_EPS = 1e-05
BETA_ONE = 0.9
BETA_TWO = 0.95
ADAM_EPS = 1e-08
DECAY = 0.1
RATE_MATRIX = 0.05
RATE_SMALL = 0.3
MASKED = -1e30
BLOCK = 256
FEW = 8
F32 = jnp.float32
BF16 = jnp.bfloat16


def swapped(block, bit):
    return lax.ppermute(block, "rep", [(i, i ^ bit) for i in range(SPAN)])


def rep_blocks(block, gate=None):
    far = swapped(block, 2)
    near = swapped(block, 1)
    if gate is not None:
        far = after(far, gate)
    return (block, near, far, swapped(far, 1))


def swap_shard(block, bits):
    return lax.ppermute(block, "shard", [(i, i ^ bits) for i in range(lax.axis_size("shard"))])


def after(block, other):
    return lax.optimization_barrier((block, other))[0]


class Pieces:
    def __init__(self, arrays, codes, rows):
        self.arrays, self.codes, self.rows = arrays, codes, rows

    def place(self, shard, refs, store):
        if self.codes is None:
            store(0, refs[0], 0, refs[0].shape[0])
            return
        for ref, codes in zip(refs, self.codes):
            for index, code in enumerate(codes):
                start = pl.multiple_of((shard ^ code) * self.rows, self.rows)
                store(start, ref, index * self.rows, self.rows)


def shard_gather(block, *others):
    blocks = (block,) + others
    if lax.axis_size("shard") != FEW:
        return [
            Pieces([lax.all_gather(b, "shard", axis=0, tiled=True)], None, b.shape[0])
            for b in blocks
        ]
    crossed = [swap_shard(b, 1) for b in blocks]
    codes = [[0], [1], [2], [4], [6], [3, 5, 7]]
    results = []
    gate = None
    for b, cross in zip(blocks, crossed):
        sent = b if gate is None else after(b, (gate, crossed))
        one, two, three = (swap_shard(sent, bits) for bits in (2, 4, 6))
        gate = three
        other = jnp.concatenate([one, two, three], axis=0)
        other = swap_shard(after(other, crossed), 1)
        results.append(Pieces([b, cross, one, two, three, other], codes, b.shape[0]))
    return results


def middle_kernel(place_ref, kept_ref, received_ref, own_ref, *sent_refs):
    high = place_ref[1] // 2
    rows = own_ref.shape[0]
    for bits in range(len(sent_refs) + 1):
        block = pl.ds(pl.multiple_of((high ^ bits) * rows, rows), rows)
        value = kept_ref[block, :].astype(F32) + received_ref[block, :].astype(F32)
        if bits == 0:
            own_ref[...] = value
        else:
            sent_refs[bits - 1][...] = value.astype(BF16)


def scatter_middle(place, kept, sent):
    return scatter_high(place, kept, swap_shard(sent, 1))


def scatter_high(place, kept, received):
    count = FEW // 2
    rows, columns = kept.shape[0] // count, kept.shape[1]
    own, *sends = call(
        middle_kernel,
        [shape(rows, columns, dtype=F32)] + [shape(rows, columns)] * (count - 1),
        [],
        kept.size,
        56,
        place,
        kept,
        received,
    )
    return own, [swap_shard(send, 2 * (bits + 1)) for bits, send in enumerate(sends)]


def scatter_end(own, received):
    total = own
    for block in received:
        total = total + block.astype(F32)
    return total.astype(BF16)


def split_halves(place_ref, full_ref, kept_ref, sent_ref):
    low = place_ref[1] & 1
    rows = full_ref.shape[0] // FEW
    for at in range(FEW // 2):
        target = slice(at * rows, (at + 1) * rows)
        for ref, bit in ((kept_ref, low), (sent_ref, 1 - low)):
            start = pl.multiple_of((2 * at + bit) * rows, rows)
            ref[target, :] = full_ref[pl.ds(start, rows), :]


def norm_parts(values):
    center = jnp.mean(values, axis=-1, keepdims=True)
    centered = values - center
    variance = jnp.mean(centered * centered, axis=-1, keepdims=True)
    inverse = lax.rsqrt(variance + NORM_EPS)
    return centered * inverse, inverse


def norm_back(normalized, inverse, gain, grad):
    scaled = grad * gain
    mean_one = jnp.mean(scaled, axis=-1, keepdims=True)
    mean_two = jnp.mean(scaled * normalized, axis=-1, keepdims=True)
    return inverse * (scaled - mean_one - normalized * mean_two)


def contract_rows(left_side, right_side):
    return lax.dot_general(
        left_side, right_side, (((0,), (0,)), ((), ())), preferred_element_type=F32
    )


def contract_cols(left_side, right_side):
    return lax.dot_general(
        left_side, right_side, (((1,), (1,)), ((), ())), preferred_element_type=F32
    )


def adam_update(master, gradient, moment_one, moment_two, step_rate):
    first_new = BETA_ONE * moment_one + (1.0 - BETA_ONE) * gradient
    second_new = BETA_TWO * moment_two + (1.0 - BETA_TWO) * gradient * gradient
    fix_one = 1.0 - BETA_ONE**STEP_NUM
    fix_two = 1.0 - BETA_TWO**STEP_NUM
    step_dir = first_new / fix_one / (jnp.sqrt(second_new / fix_two) + ADAM_EPS)
    return (master - step_rate * (step_dir + DECAY * master), first_new, second_new)


def dot(left_side, right_side):
    return jnp.dot(left_side, right_side, preferred_element_type=F32)


def chosen(values, index):
    result = values[0]
    for at in range(1, len(values)):
        result = jnp.where(index == at, values[at], result)
    return result


def mask_bias(seg_col_ref, seg_row_ref, start, keys):
    same = seg_col_ref[:keys, 0:1] == seg_row_ref[0:1, start : start + BLOCK]
    key_at = lax.broadcasted_iota(jnp.int32, (keys, BLOCK), 0)
    query_at = lax.broadcasted_iota(jnp.int32, (keys, BLOCK), 1) + start
    return jnp.where(same & (key_at <= query_at), 0.0, MASKED)


def head_lanes(shape, head):
    lane = lax.broadcasted_iota(jnp.int32, shape, 1)
    return (lane >= head * HEAD_DIM) & (lane < (head + 1) * HEAD_DIM)


def attend(q_ref, k_ref, v_ref, seg_col_ref, seg_row_ref, out_ref, lse_ref):
    total, width = q_ref.shape
    heads = width // HEAD_DIM
    value_t = v_ref[...].T
    lse_ref[...] = jnp.zeros_like(lse_ref)
    for start in range(0, total, BLOCK):
        keys = start + BLOCK
        bias = mask_bias(seg_col_ref, seg_row_ref, start, keys)
        query = q_ref[start : start + BLOCK, :]
        pieces = []
        for head in range(heads):
            masked = jnp.where(head_lanes(query.shape, head), query, 0)
            scores = contract_cols(k_ref[:keys, :], masked) + bias
            peak = jnp.max(scores, axis=0, keepdims=True)
            exponent = jnp.exp(scores - peak)
            row_total = jnp.sum(exponent, axis=0, keepdims=True)
            mixed = dot(
                value_t[head * HEAD_DIM : (head + 1) * HEAD_DIM, :keys], exponent.astype(BF16)
            )
            pieces.append(mixed / row_total)
            lse_ref[head : head + 1, start : start + BLOCK] = peak + jnp.log(row_total)
        out_ref[start : start + BLOCK, :] = jnp.concatenate(pieces, axis=0).T.astype(BF16)


def attend_back(
    q_ref, k_ref, v_ref, do_ref, lse_ref, seg_col_ref, seg_row_ref, grad_ref, dk_ref, dv_ref
):
    total, width = q_ref.shape
    heads = width // HEAD_DIM
    key_t = k_ref[...].T
    dk_ref[...] = jnp.zeros_like(dk_ref)
    dv_ref[...] = jnp.zeros_like(dv_ref)
    for start in range(0, total, BLOCK):
        keys = start + BLOCK
        bias = mask_bias(seg_col_ref, seg_row_ref, start, keys)
        query = q_ref[start : start + BLOCK, :]
        grad = do_ref[start : start + BLOCK, :]
        pieces = []
        dk = dk_ref[:keys, :]
        dv = dv_ref[:keys, :]
        for head in range(heads):
            lanes = head_lanes(query.shape, head)
            query_h = jnp.where(lanes, query, 0)
            grad_h = jnp.where(lanes, grad, 0)
            scores = contract_cols(k_ref[:keys, :], query_h) + bias
            probs = jnp.exp(scores - lse_ref[head : head + 1, start : start + BLOCK])
            prob_grad = contract_cols(v_ref[:keys, :], grad_h)
            inner = jnp.sum(prob_grad * probs, axis=0, keepdims=True)
            score_grad = (probs * (prob_grad - inner)).astype(BF16)
            dv = dv + dot(probs.astype(BF16), grad_h)
            dk = dk + dot(score_grad, query_h)
            pieces.append(
                dot(key_t[head * HEAD_DIM : (head + 1) * HEAD_DIM, :keys], score_grad)
            )
        dk_ref[:keys, :] = dk
        dv_ref[:keys, :] = dv
        dq = jnp.concatenate(pieces, axis=0).T * HEAD_DIM ** (-0.5)
        grad_ref[start : start + BLOCK, :width] = dq.astype(BF16)
    grad_ref[:, width : 2 * width] = dk_ref[...].astype(BF16)
    grad_ref[:, 2 * width :] = dv_ref[...].astype(BF16)


def call(kernel, outs, scratch, flops, limit, *operands):
    sizes = [o.size * o.dtype.itemsize for o in operands] + [
        o.size * jnp.dtype(o.dtype).itemsize for o in outs
    ]
    vmem = pl.BlockSpec(memory_space=pltpu.VMEM)
    return pl.pallas_call(
        kernel,
        out_shape=tuple(outs),
        in_specs=[pl.BlockSpec(memory_space=pltpu.SMEM)] + [vmem] * (len(operands) - 1),
        out_specs=tuple([vmem] * len(outs)),
        scratch_shapes=scratch,
        compiler_params=pltpu.CompilerParams(vmem_limit_bytes=limit * 2**20),
        cost_estimate=pl.CostEstimate(
            flops=flops, bytes_accessed=sum(sizes), transcendentals=0
        ),
    )(*operands)


def shape(*dims, dtype=BF16):
    return jax.ShapeDtypeStruct(dims, dtype)


def send_parts(value, at, near_ref, far_ref, own_ref):
    rows = value.shape[0]

    @pl.when(at == 0)
    def _():
        own_ref[...] = value

    @pl.when(at == 1)
    def _():
        near_ref[rows:, :] = value.astype(BF16)

    @pl.when(at == 2)
    def _():
        far_ref[...] = value

    @pl.when(at == 3)
    def _():
        near_ref[:rows, :] = value.astype(BF16)


def rep_sum(near_send, far_part, gate=None):
    rows = far_part.shape[0]
    near = swapped(near_send, 1)
    far_send = (far_part + near[:rows].astype(F32)).astype(BF16)
    if gate is not None:
        far_send = after(far_send, gate)
    return near, swapped(far_send, 2), far_send


def place_store(target, columns, limit=None):
    def store(start, ref, first, rows):
        target[pl.ds(start, rows), :limit] = ref[first : first + rows, columns]

    return store


def prep_kernel(
    place_ref,
    qkv_ref,
    out_ref,
    up_ref,
    down_ref,
    small_ref,
    first_ref,
    second_ref,
    third_ref,
    small_rows,
):
    rep = place_ref[0]
    owned, width = out_ref.shape
    part, half = width // SPAN, width // 2
    units = third_ref.shape[0]
    small_rows[...] = jnp.zeros_like(small_rows)
    small_rows[: small_ref.shape[0], : small_ref.shape[1]] = small_ref[...]
    for which in range(3):
        first = which * width
        options = [qkv_ref[:, first + r * part : first + (r + 1) * part] for r in range(SPAN)]
        first_ref[:, which * part : (which + 1) * part] = chosen(options, rep).astype(BF16)
    first_ref[:, 3 * part :] = small_rows[...].T[:owned, :64].astype(BF16)
    second_ref[:, :half] = out_ref[:, :half].astype(BF16)
    pieces = []
    for first in range(0, up_ref.shape[1], SPAN * units):
        options = [up_ref[:, first + r * units : first + (r + 1) * units] for r in range(SPAN)]
        pieces.append(chosen(options, rep))
    second_ref[:, half:] = jnp.concatenate(pieces, axis=1).astype(BF16)
    third_ref[:, :half] = out_ref[:, half:].astype(BF16)
    start = pl.multiple_of(rep * units, units)
    third_ref[:, half:] = down_ref[pl.ds(start, units), :].astype(BF16)


def first_kernel(pieces, *refs):
    place_ref, refs = refs[0], refs[1:]
    token_refs, refs = refs[:SPAN], refs[SPAN:]
    count = len(pieces.arrays)
    weight_refs, refs = refs[:count], refs[count:]
    (
        all_ref,
        weight_ref,
        small_ref,
        q_ref,
        k_ref,
        v_ref,
        seg_col_ref,
        seg_row_ref,
        out_ref,
        lse_ref,
        small_cols,
    ) = refs
    rep, shard = place_ref[0], place_ref[1]
    total, width = all_ref.shape
    rows = total // SPAN
    part = q_ref.shape[1]
    pieces.place(shard, weight_refs, place_store(weight_ref, slice(0, 3 * part)))
    last = small_cols.shape[1]
    pieces.place(
        shard, weight_refs, place_store(small_cols, slice(3 * part + 64 - last, 3 * part + 64))
    )
    small = small_cols[...].astype(F32).T
    small = small[last - 64 : last - 48, :]
    small_ref[...] = small
    gain, bias = small[0:1, :], small[1:2, :]
    query_bias = chosen([small[2:3, r * part : (r + 1) * part] for r in range(SPAN)], rep)
    value_bias = chosen([small[3:4, r * part : (r + 1) * part] for r in range(SPAN)], rep)
    for at in range(SPAN):
        start = pl.multiple_of((rep ^ at) * rows, rows)
        block = token_refs[at][:rows, :]
        all_ref[pl.ds(start, rows), :] = block
        hidden = (norm_parts(block.astype(F32))[0] * gain + bias).astype(BF16)
        segs = token_refs[at][rows : rows + 16, :rows].astype(F32)
        seg_row_ref[:, pl.ds(start, rows)] = segs[:8, :]
        seg_col_ref[pl.ds(start, rows), 0:16] = segs.T
        projected = dot(hidden, weight_ref[...])
        q_ref[pl.ds(start, rows), :] = (
            (projected[:, :part] + query_bias) * HEAD_DIM ** (-0.5)
        ).astype(BF16)
        k_ref[pl.ds(start, rows), :] = projected[:, part : 2 * part].astype(BF16)
        v_ref[pl.ds(start, rows), :] = (projected[:, 2 * part :] + value_bias).astype(BF16)
    attend(q_ref, k_ref, v_ref, seg_col_ref, seg_row_ref, out_ref, lse_ref)


def second_kernel(pieces, place_ref, *refs):
    attended_refs, refs = refs[:SPAN], refs[SPAN:]
    cot_refs, refs = refs[:SPAN], refs[SPAN:]
    count = len(pieces.arrays)
    piece_refs, refs = refs[:count], refs[count:]
    (
        wide_ref,
        all_ref,
        small_ref,
        up_bias_ref,
        out_weight,
        cot_ref,
        hidden_ref,
        act_ref,
        pre_ref,
        residual_ref,
        near_ref,
        far_ref,
        own_ref,
        up_weight,
    ) = refs
    rep = place_ref[0]
    total, width = all_ref.shape
    rows = total // SPAN
    part = attended_refs[0].shape[1]
    half = width // 2
    pieces.place(place_ref[1], piece_refs, place_store(up_weight, slice(half, None)))
    pieces.place(place_ref[1], piece_refs, place_store(out_weight, slice(0, half), half))
    out_weight[:, half:] = wide_ref[:, :half]
    for at in range(SPAN):
        cot_ref[pl.ds(pl.multiple_of((rep ^ at) * rows, rows), rows), :] = cot_refs[at][...]
    out_bias, gain, bias = small_ref[4:5, :], small_ref[5:6, :], small_ref[6:7, :]

    @pl.loop(0, SPAN)
    def _(index):
        block = pl.ds(pl.multiple_of(index * rows, rows), rows)
        mixed = out_bias
        for at in range(SPAN):
            from_rows = pl.ds(pl.multiple_of((rep ^ at) * part, part), part)
            mixed = mixed + dot(attended_refs[at][block, :], out_weight[from_rows, :])
        residual = all_ref[block, :].astype(F32) + mixed

        @pl.when(index == rep)
        def _():
            residual_ref[...] = residual

        hidden = (norm_parts(residual)[0] * gain + bias).astype(BF16)
        hidden_ref[block, :] = hidden
        pre_act = dot(hidden, up_weight[...]) + up_bias_ref[...]
        cdf = 0.5 * (1.0 + lax.erf(pre_act * (0.5**0.5)))
        act_ref[block, :] = (pre_act * cdf).astype(BF16)
        slope = cdf + pre_act * (jnp.exp(-0.5 * pre_act * pre_act) * 0.3989422804014327)
        pre_low = (contract_cols(cot_ref[block, :], wide_ref[:, half:]) * slope).astype(BF16)
        pre_ref[block, :] = pre_low
        grad = contract_cols(pre_low, up_weight[...])
        send_parts(grad, index ^ rep, near_ref, far_ref, own_ref)


def down_grad_kernel(place_ref, act_ref, cot_ref, *refs):
    grad_refs, grad_ref = refs[:-1], refs[-1]
    units = act_ref.shape[1]
    step = units // 3
    for first in range(0, units, step):
        grad_ref[first : first + step, :] = contract_rows(
            act_ref[:, first : first + step], cot_ref[...]
        ).astype(BF16)
    if len(grad_refs) == 2:
        split_halves(place_ref, grad_ref, *grad_refs)
    else:
        grad_refs[0][...] = grad_ref[...]


def third_kernel(place_ref, act_ref, hidden_ref, pre_ref, wide_ref, *refs):
    grad_refs, (near_ref, far_ref, own_ref, sum_ref, grad_ref) = refs[:-5], refs[-5:]
    rep = place_ref[0]
    total, width = hidden_ref.shape
    rows = total // SPAN
    step = width // 3
    for first in range(0, width, step):
        grad_ref[first : first + step, :] = contract_rows(
            hidden_ref[:, first : first + step], pre_ref[...]
        ).astype(BF16)
    sum_ref[...] = jnp.broadcast_to(
        jnp.sum(pre_ref[...].astype(F32), axis=0, keepdims=True), sum_ref.shape
    )

    @pl.loop(0, SPAN)
    def _(index):
        block = pl.ds(pl.multiple_of(index * rows, rows), rows)
        send_parts(
            dot(act_ref[block, :], wide_ref[:, -width:]), index ^ rep, near_ref, far_ref, own_ref
        )

    if len(grad_refs) == 2:
        split_halves(place_ref, grad_ref, *grad_refs)
    else:
        grad_refs[0][...] = grad_ref[...]


def fourth_kernel(
    place_ref,
    own_ref,
    near_ref,
    far_ref,
    residual_ref,
    cotangent_ref,
    small_ref,
    resid_grad_ref,
    branch_ref,
    sums_ref,
):
    grad = own_ref[...] + near_ref[own_ref.shape[0] :, :].astype(F32) + far_ref[...].astype(F32)
    normalized, inverse = norm_parts(residual_ref[...])
    cotangent = cotangent_ref[...].astype(F32)
    resid_grad = cotangent + norm_back(normalized, inverse, small_ref[5:6, :], grad)
    branch = resid_grad.astype(BF16)
    resid_grad_ref[...] = resid_grad
    branch_ref[...] = branch
    sums_ref[...] = jnp.zeros_like(sums_ref)
    sums_ref[4:5, :] = jnp.sum(branch.astype(F32), axis=0, keepdims=True)
    sums_ref[5:6, :] = jnp.sum(grad * normalized, axis=0, keepdims=True)
    sums_ref[6:7, :] = jnp.sum(grad, axis=0, keepdims=True)
    sums_ref[7:8, :] = jnp.sum(cotangent, axis=0, keepdims=True)


def fifth_kernel(
    place_ref,
    branch_a,
    branch_b,
    branch_c,
    branch_d,
    attended_a,
    attended_b,
    attended_c,
    attended_d,
    out_weight,
    qkv_weight,
    q_ref,
    k_ref,
    v_ref,
    lse_ref,
    seg_col_ref,
    seg_row_ref,
    all_ref,
    small_ref,
    sums_ref,
    unit_sums_ref,
    *refs,
):
    grad_refs, refs = refs[:-11], refs[-11:]
    (
        near_ref,
        far_ref,
        own_ref,
        branch_ref,
        back_ref,
        proj_ref,
        dk_ref,
        dv_ref,
        small_grads,
        grad_ref,
        hidden_ref,
    ) = refs
    rep = place_ref[0]
    total, width = all_ref.shape
    rows = total // SPAN
    part = q_ref.shape[1]
    own_rows = pl.ds(pl.multiple_of(rep * part, part), part)
    for at, ref in enumerate((branch_a, branch_b, branch_c, branch_d)):
        start = pl.multiple_of((rep ^ at) * rows, rows)
        branch_ref[pl.ds(start, rows), :] = ref[...]
    back_ref[...] = contract_cols(branch_ref[...], out_weight[own_rows, :]).astype(BF16)
    attend_back(
        q_ref,
        k_ref,
        v_ref,
        back_ref,
        lse_ref,
        seg_col_ref,
        seg_row_ref,
        proj_ref,
        dk_ref,
        dv_ref,
    )
    gain = small_ref[0:1, :]
    small_grads[...] = jnp.zeros_like(small_grads)
    small_grads[0:8, :] = sums_ref[...]
    small_grads[8:16, :] = unit_sums_ref[...]

    @pl.loop(0, SPAN)
    def _(index):
        block = pl.ds(pl.multiple_of(index * rows, rows), rows)
        grad = contract_cols(proj_ref[block, :], qkv_weight[...])
        normalized = norm_parts(all_ref[block, :].astype(F32))[0]
        hidden_ref[block, :] = (normalized * gain + small_ref[1:2, :]).astype(BF16)
        small_grads[0:1, :] += jnp.sum(grad * normalized, axis=0, keepdims=True)
        small_grads[1:2, :] += jnp.sum(grad, axis=0, keepdims=True)
        send_parts(grad, index ^ rep, near_ref, far_ref, own_ref)

    lane = lax.broadcasted_iota(jnp.int32, (1, width), 1)
    mine = (lane >= rep * part) & (lane < (rep + 1) * part)
    for row, first in ((2, 0), (3, 2 * part)):
        column_sum = jnp.sum(
            proj_ref[:, first : first + part].astype(F32), axis=0, keepdims=True
        )
        small_grads[row : row + 1, :] = jnp.where(
            mine, jnp.concatenate([column_sum] * SPAN, axis=1), 0.0
        )
    step = width // 3
    for first in range(0, width, step):
        grad_ref[first : first + step, : 3 * part] = contract_rows(
            hidden_ref[:, first : first + step], proj_ref[...]
        ).astype(BF16)
    branch_part = chosen(
        [branch_ref[:, r * part : (r + 1) * part] for r in range(SPAN)], rep
    )
    for at, ref in enumerate((attended_a, attended_b, attended_c, attended_d)):
        from_rows = pl.ds(pl.multiple_of((rep ^ at) * part, part), part)
        grad_ref[from_rows, 3 * part : 4 * part] = contract_rows(ref[...], branch_part).astype(
            BF16
        )
    grad_ref[:, 4 * part :] = small_grads[...].T.astype(BF16)
    if len(grad_refs) == 2:
        split_halves(place_ref, grad_ref, *grad_refs)
    else:
        grad_refs[0][...] = grad_ref[...]


def sixth_kernel(
    place_ref, own_ref, near_ref, far_ref, tokens_ref, resid_grad_ref, small_ref, out_ref
):
    grad = own_ref[...] + near_ref[own_ref.shape[0] :, :].astype(F32) + far_ref[...].astype(F32)
    normalized, inverse = norm_parts(tokens_ref[...].astype(F32))
    out_ref[...] = resid_grad_ref[...] + norm_back(normalized, inverse, small_ref[0:1, :], grad)


def rep_order(refs, rep):
    blocks = [ref[...].astype(F32) for ref in refs]
    odd, high = (rep & 1) == 1, (rep & 2) == 2
    pairs = []
    for first in (0, 2):
        lower, upper = blocks[first], blocks[first + 1]
        pairs.append((jnp.where(odd, upper, lower), jnp.where(odd, lower, upper)))
    low = [jnp.where(high, b, a) for a, b in zip(*pairs)]
    return low + [jnp.where(high, a, b) for a, b in zip(*pairs)]


def adam_kernel(place_ref, *refs):
    blocks = rep_order(refs[:SPAN], place_ref[0])
    ins, outs = refs[SPAN : SPAN + 9], refs[SPAN + 9 :]
    part = ins[3].shape[1] // SPAN
    qkv = [b[:, c * part : (c + 1) * part] for c in range(3) for b in blocks]
    out = [b[:, 3 * part : 4 * part] for b in blocks]
    small = blocks[0][:, 4 * part :]
    for block in blocks[1:]:
        small = small + block[:, 4 * part :]
    small = small.T[: ins[6].shape[0], :]
    grads = (jnp.concatenate(qkv, axis=1), jnp.concatenate(out, axis=1), small)
    for at, (gradient, rate) in enumerate(zip(grads, (RATE_MATRIX, RATE_MATRIX, RATE_SMALL))):
        weight, first, second = (ref[...] for ref in ins[3 * at : 3 * at + 3])
        results = adam_update(weight, gradient, first, second, rate)
        for ref, value in zip(outs[3 * at : 3 * at + 3], results):
            ref[...] = value


def up_adam_kernel(place_ref, *refs):
    blocks = rep_order(refs[:SPAN], place_ref[0])
    weight, first, second, *outs = refs[SPAN:]
    width = weight.shape[1] // SPAN
    units = width // FEW
    pieces = [b[:, at * units : (at + 1) * units] for at in range(FEW) for b in blocks]
    results = adam_update(
        weight[...], jnp.concatenate(pieces, axis=1), first[...], second[...], RATE_MATRIX
    )
    for ref, value in zip(outs, results):
        ref[...] = value


def down_adam_kernel(place_ref, *refs):
    at = pl.program_id(0) ^ place_ref[0]
    gradient = chosen([ref[...] for ref in refs[:SPAN]], at).astype(F32)
    weight, first, second, *outs = refs[SPAN:]
    results = adam_update(weight[...], gradient, first[...], second[...], RATE_MATRIX)
    for ref, value in zip(outs, results):
        ref[...] = value


def grid_adam(kernel, steps, place, blocks, block_spec, arrays):
    rows, columns = arrays[0].shape
    spec = pl.BlockSpec((rows // steps, columns), lambda i: (i, 0))
    return list(pl.pallas_call(
        kernel,
        grid=(steps,),
        out_shape=[shape(rows, columns, dtype=F32)] * 3,
        in_specs=[pl.BlockSpec(memory_space=pltpu.SMEM)]
        + [block_spec] * SPAN
        + [spec] * 3,
        out_specs=[spec] * 3,
        compiler_params=pltpu.CompilerParams(vmem_limit_bytes=16 * 2**20),
        cost_estimate=pl.CostEstimate(
            flops=0, bytes_accessed=0, transcendentals=0
        ),
    )(place, *blocks, *arrays))


def in_order(blocks, rep):
    odd = (rep & 1) == 1
    high = (rep & 2) == 2
    low_pair = (jnp.where(odd, blocks[1], blocks[0]), jnp.where(odd, blocks[0], blocks[1]))
    high_pair = (jnp.where(odd, blocks[3], blocks[2]), jnp.where(odd, blocks[2], blocks[3]))
    return (
        jnp.where(high, high_pair[0], low_pair[0]),
        jnp.where(high, high_pair[1], low_pair[1]),
        jnp.where(high, low_pair[0], high_pair[0]),
        jnp.where(high, low_pair[1], high_pair[1]),
    )


def local(
    tokens,
    cotangent,
    segments,
    qkv_weight,
    out_weight,
    up_weight,
    down_weight,
    small_weights,
    qkv_first,
    out_first,
    up_first,
    down_first,
    small_first,
    qkv_second,
    out_second,
    up_second,
    down_second,
    small_second,
):
    rep = lax.axis_index("rep")
    shards = lax.axis_size("shard")
    place = jnp.stack([rep, lax.axis_index("shard")]).astype(jnp.int32)
    rows, width = tokens.shape
    total = SPAN * rows
    part = width // SPAN
    owned = qkv_weight.shape[0]
    ff = up_weight.shape[1]
    ff_part = ff // SPAN
    units = down_weight.shape[0] // SPAN

    def rep_part(block, size, axis):
        return lax.dynamic_slice_in_dim(block, rep * size, size, axis)

    few = shards == FEW
    half = width // 2
    if few:
        first_send, second_send, third_send = call(
            prep_kernel,
            [
                shape(owned, 3 * part + 64),
                shape(owned, half + ff_part),
                shape(units, half + width),
            ],
            [pltpu.VMEM((128, 128), F32)],
            owned * width,
            56,
            place,
            qkv_weight,
            out_weight,
            up_weight,
            down_weight,
            small_weights,
        )
    else:
        low_small = small_weights.astype(BF16).T
        low_qkv = rep_part(qkv_weight.astype(BF16).reshape(owned, 3, SPAN, part), 1, 2)
        low_qkv = low_qkv.reshape(owned, 3 * part)
        pad = 64 - low_small.shape[1]
        first_send = jnp.concatenate([low_qkv, jnp.pad(low_small, ((0, 0), (0, pad)))], axis=1)
        low_up = rep_part(up_weight.astype(BF16).reshape(owned, shards, SPAN, units), 1, 2)
        low_down = rep_part(down_weight, units, 0).astype(BF16)
        low_out = out_weight.astype(BF16)
        second_send = jnp.concatenate([low_out[:, :half], low_up.reshape(owned, -1)], axis=1)
        third_send = jnp.concatenate([low_out[:, half:], low_down], axis=1)
    third_full = lax.all_gather(third_send, "shard", axis=0, tiled=True)
    first_pieces, second_pieces = shard_gather(first_send, second_send)

    seg_block = jnp.pad(segments.astype(BF16)[None, :], ((0, 15), (0, width - rows)))
    with_seg = jnp.concatenate([tokens, seg_block], axis=0)
    token_blocks = rep_blocks(with_seg)
    cot_blocks = rep_blocks(after(cotangent, token_blocks[2]))

    (
        all_tokens,
        qkv_part,
        small,
        queries,
        keys,
        values,
        seg_col,
        seg_row,
        attended,
        log_total,
    ) = call(
        lambda *refs: first_kernel(first_pieces, *refs),
        [
            shape(total, width),
            shape(width, 3 * part),
            shape(16, width, dtype=F32),
            shape(total, part),
            shape(total, part),
            shape(total, part),
            shape(total, 128, dtype=F32),
            shape(8, total, dtype=F32),
            shape(total, part),
            shape(8, total, dtype=F32),
        ],
        [pltpu.VMEM((width, 128), BF16)],
        12 * total * width * width + 24 * total * total * part,
        56,
        place,
        *token_blocks,
        *first_pieces.arrays,
    )
    up_bias = rep_part(small[8:12].reshape(shards, SPAN, units), 1, 1).reshape(1, -1)
    attended_blocks = rep_blocks(attended)
    (
        out_part,
        all_cot,
        hidden_two,
        act_low,
        pre_low,
        residual,
        near_send,
        far_part,
        own,
    ) = call(
        lambda *refs: second_kernel(second_pieces, *refs),
        [
            shape(width, width),
            shape(total, width),
            shape(total, width),
            shape(total, ff_part),
            shape(total, ff_part),
            shape(rows, width, dtype=F32),
            shape(2 * rows, width),
            shape(rows, width, dtype=F32),
            shape(rows, width, dtype=F32),
        ],
        [pltpu.VMEM((width, ff_part), BF16)],
        32 * total * width * width,
        56,
        place,
        *attended_blocks,
        *cot_blocks,
        *second_pieces.arrays,
        third_full,
        all_tokens,
        small,
        up_bias,
    )
    near, far, far_send = rep_sum(near_send, far_part)
    hidden_two_terms = own, near, far
    down_grad = call(
        down_grad_kernel,
        [shape(ff_part // 2, width)] * 2 * few + [shape(ff_part, width)] * (not few),
        [pltpu.VMEM((ff_part, width), BF16)],
        6 * total * width * width,
        56,
        place,
        after(act_low, far_send),
        all_cot,
    )
    if few:
        down_received = swap_shard(down_grad[1], 1)
    hidden_two_terms = own, near, far
    resid_grad, branch, sums = call(
        fourth_kernel,
        [
            shape(rows, width, dtype=F32),
            shape(rows, width),
            shape(8, width, dtype=F32),
        ],
        [],
        10 * rows * width,
        56,
        place,
        *hidden_two_terms,
        residual,
        cotangent,
        small,
    )
    branch_blocks = rep_blocks(branch)
    gate = down_grad[0]
    if few:
        down_own, down_received = scatter_high(place, after(down_grad[0], branch), down_received)
        gate = down_own
    *up_grad, mixed_near, mixed_far, mixed_own, unit_sums = call(
        third_kernel,
        [shape(width // 2, ff_part)] * 2 * few
        + [shape(width, ff_part)] * (not few)
        + [
            shape(2 * rows, width),
            shape(rows, width, dtype=F32),
            shape(rows, width, dtype=F32),
            shape(8, ff_part, dtype=F32),
        ],
        [pltpu.VMEM((width, ff_part), BF16)],
        12 * total * width * width,
        56,
        place,
        after(act_low, gate),
        hidden_two,
        pre_low,
        third_full,
    )
    if few:
        up_received = swap_shard(up_grad[1], 1)
    near_mixed, far_mixed, _ = rep_sum(after(mixed_near, branch), mixed_far, branch_blocks[2])
    unit_rows = lax.dynamic_update_slice(
        jnp.zeros((shards, SPAN, units), F32), unit_sums[0].reshape(shards, 1, units), (0, rep, 0)
    ).reshape(ff // width, width)
    unit_rows = jnp.pad(unit_rows, ((0, 8 - ff // width), (0, 0)))
    *last_grad, near_send, far_part, own = call(
        fifth_kernel,
        [shape(width // 2, 4 * part + 128)] * 2 * few
        + [shape(width, 4 * part + 128)] * (not few)
        + [
            shape(2 * rows, width),
            shape(rows, width, dtype=F32),
            shape(rows, width, dtype=F32),
        ],
        [
            pltpu.VMEM((total, width), BF16),
            pltpu.VMEM((total, part), BF16),
            pltpu.VMEM((total, 3 * part), BF16),
            pltpu.VMEM((total, part), F32),
            pltpu.VMEM((total, part), F32),
            pltpu.VMEM((128, width), F32),
            pltpu.VMEM((width, 4 * part + 128), BF16),
            pltpu.VMEM((total, width), BF16),
        ],
        12 * total * width * width + 72 * total * total * part,
        56,
        place,
        *branch_blocks,
        *attended_blocks,
        out_part,
        qkv_part,
        queries,
        keys,
        values,
        log_total,
        seg_col,
        seg_row,
        all_tokens,
        small,
        sums,
        unit_rows,
    )
    near, far, far_send = rep_sum(near_send, far_part)
    if few:
        last_kept, last_sent = last_grad
        last_sent, down_received = lax.optimization_barrier((last_sent, down_received))
        last_own, last_received = scatter_middle(place, last_kept, last_sent)
        up_own, up_received = scatter_high(
            place, after(up_grad[0], (last_grad[0], down_received)), up_received
        )
        down_own, up_received = after((down_own, up_received), last_own)
        wide_total = jnp.concatenate(
            [scatter_end(down_own, down_received), scatter_end(up_own, up_received)], axis=1
        )
        wide_blocks = rep_blocks(wide_total, last_received)
    else:
        last_total, down_total, up_total = (
            lax.psum_scatter(grad, "shard", scatter_dimension=0, tiled=True)
            for grad in (last_grad[0], down_grad[0], up_grad[0])
        )
    mixed = residual + (
        mixed_own + near_mixed[rows:].astype(F32) + far_mixed.astype(F32) + small[7]
    )
    mixed = mixed.astype(BF16)
    input_grad = call(
        sixth_kernel,
        [shape(rows, width, dtype=F32)],
        [],
        10 * rows * width,
        56,
        place,
        own,
        near,
        far,
        tokens,
        resid_grad,
        small,
    )[0]
    if few:
        up_res = grid_adam(
            up_adam_kernel,
            3,
            place,
            wide_blocks,
            pl.BlockSpec((owned // 3, width), lambda i: (i, 1)),
            (up_weight, up_first, up_second),
        )
        down_res = grid_adam(
            down_adam_kernel,
            SPAN,
            place,
            wide_blocks,
            pl.BlockSpec((units, width), lambda i: (0, 0)),
            (down_weight, down_first, down_second),
        )
        last_received, input_grad, mixed = lax.optimization_barrier(
            (last_received, input_grad, mixed)
        )
        last_total = scatter_end(last_own, last_received)
        last_blocks = rep_blocks(last_total)
        last_near, up_res[0], down_res[0] = lax.optimization_barrier(
            (last_blocks[1], up_res[0], down_res[0])
        )
        last_blocks = (last_blocks[0], last_near) + last_blocks[2:]
        results = call(
            adam_kernel,
            [shape(*ref.shape, dtype=F32) for ref in (qkv_weight, out_weight, small_weights)
             for _ in range(3)],
            [],
            20 * qkv_weight.size,
            56,
            place,
            *last_blocks,
            qkv_weight,
            qkv_first,
            qkv_second,
            out_weight,
            out_first,
            out_second,
            small_weights,
            small_first,
            small_second,
        )
        qkv_res, out_res, small_res = results[:3], results[3:6], results[6:]
    else:
        down_own = jnp.concatenate(in_order(rep_blocks(down_total), rep), axis=0).astype(F32)
        up_own = in_order(rep_blocks(up_total), rep)
        up_own = [g.reshape(owned, shards, units) for g in up_own]
        up_own = jnp.stack(up_own, axis=2).reshape(owned, ff).astype(F32)
        up_res = adam_update(up_weight, up_own, up_first, up_second, RATE_MATRIX)
        down_res = adam_update(down_weight, down_own, down_first, down_second, RATE_MATRIX)
        last_own = in_order(rep_blocks(last_total), rep)
        out_own = jnp.concatenate([g[:, 3 * part : 4 * part] for g in last_own], axis=1)
        qkv_own = [g[:, : 3 * part].reshape(owned, 3, part) for g in last_own]
        qkv_own = jnp.stack(qkv_own, axis=2).reshape(owned, 3 * width).astype(F32)
        small_own = sum(g[:, 4 * part : 4 * part + 12].astype(F32) for g in last_own).T
        qkv_res = adam_update(qkv_weight, qkv_own, qkv_first, qkv_second, RATE_MATRIX)
        out_res = adam_update(
            out_weight, out_own.astype(F32), out_first, out_second, RATE_MATRIX
        )
        small_res = adam_update(
            small_weights, small_own, small_first, small_second, RATE_SMALL
        )
    return (
        mixed,
        input_grad,
        qkv_res[0],
        out_res[0],
        up_res[0],
        down_res[0],
        small_res[0],
        qkv_res[1],
        out_res[1],
        up_res[1],
        down_res[1],
        small_res[1],
        qkv_res[2],
        out_res[2],
        up_res[2],
        down_res[2],
        small_res[2],
    )


def solution(mesh):
    tokens_spec = P(("rep", "shard"), None)
    rows = P("shard", None)
    columns = P(None, "shard")
    weights = (rows, rows, rows, rows, columns)
    return jax.shard_map(
        local,
        mesh=mesh,
        in_specs=(tokens_spec, tokens_spec, P(("rep", "shard"))) + weights * 3,
        out_specs=(tokens_spec, tokens_spec) + weights * 3,
        check_vma=False,
    )
```

```python
import jax
import jax.numpy as jnp
from jax import lax
from jax.experimental import pallas as pl
from jax.experimental.pallas import tpu as pltpu
from jax.sharding import PartitionSpec as P

HEAD_DIM = 64
SPAN = 4
STEP_NUM = 10


NORM_EPS = 1e-05
BETA_ONE = 0.9
BETA_TWO = 0.95
ADAM_EPS = 1e-08
DECAY = 0.1
RATE_MATRIX = 0.05
RATE_SMALL = 0.3
MASKED = -1e30
BLOCK = 256
FEW = 8
F32 = jnp.float32
BF16 = jnp.bfloat16


def swapped(block, bit):
    return lax.ppermute(block, "rep", [(i, i ^ bit) for i in range(SPAN)])


def rep_blocks(block, gate=None, near_gate=None):
    far = swapped(block, 2)
    near = swapped(block if near_gate is None else after(block, near_gate), 1)
    if gate is not None:
        far = after(far, gate)
    return (block, near, far, swapped(far, 1))


def swap_shard(block, bits):
    return lax.ppermute(block, "shard", [(i, i ^ bits) for i in range(lax.axis_size("shard"))])


def after(block, other):
    return lax.optimization_barrier((block, other))[0]


class Pieces:
    def __init__(self, arrays, codes, rows):
        self.arrays, self.codes, self.rows = arrays, codes, rows

    def place(self, shard, refs, store):
        if self.codes is None:
            store(0, refs[0], 0, refs[0].shape[0])
            return
        for ref, codes in zip(refs, self.codes):
            for index, code in enumerate(codes):
                start = pl.multiple_of((shard ^ code) * self.rows, self.rows)
                store(start, ref, index * self.rows, self.rows)


def shard_gather(block, *others):
    blocks = (block,) + others
    if lax.axis_size("shard") != FEW:
        return [
            Pieces([lax.all_gather(b, "shard", axis=0, tiled=True)], None, b.shape[0])
            for b in blocks
        ]
    crossed = [swap_shard(b, 1) for b in blocks]
    codes = [[0], [1], [2], [4], [6], [3, 5, 7]]
    results = []
    gate = None
    for b, cross in zip(blocks, crossed):
        sent = b if gate is None else after(b, (gate, crossed))
        one, two, three = (swap_shard(sent, bits) for bits in (2, 4, 6))
        gate = three
        other = jnp.concatenate([one, two, three], axis=0)
        other = swap_shard(after(other, crossed), 1)
        results.append(Pieces([b, cross, one, two, three, other], codes, b.shape[0]))
    return results


def middle_kernel(place_ref, kept_ref, received_ref, own_ref, *sent_refs):
    high = place_ref[1] // 2
    rows = own_ref.shape[0]
    for bits in range(len(sent_refs) + 1):
        block = pl.ds(pl.multiple_of((high ^ bits) * rows, rows), rows)
        value = kept_ref[block, :].astype(F32) + received_ref[block, :].astype(F32)
        if bits == 0:
            own_ref[...] = value
        else:
            sent_refs[bits - 1][...] = value.astype(BF16)


def scatter_middle(place, kept, sent):
    return scatter_high(place, kept, swap_shard(sent, 1))


def scatter_high(place, kept, received):
    count = FEW // 2
    rows, columns = kept.shape[0] // count, kept.shape[1]
    own, *sends = call(
        middle_kernel,
        [shape(rows, columns, dtype=F32)] + [shape(rows, columns)] * (count - 1),
        [],
        kept.size,
        56,
        place,
        kept,
        received,
    )
    return own, [swap_shard(send, 2 * (bits + 1)) for bits, send in enumerate(sends)]


def scatter_end(own, received):
    total = own
    for block in received:
        total = total + block.astype(F32)
    return total.astype(BF16)


def split_halves(place_ref, full_ref, kept_ref, sent_ref):
    low = place_ref[1] & 1
    rows = full_ref.shape[0] // FEW
    for at in range(FEW // 2):
        target = slice(at * rows, (at + 1) * rows)
        for ref, bit in ((kept_ref, low), (sent_ref, 1 - low)):
            start = pl.multiple_of((2 * at + bit) * rows, rows)
            ref[target, :] = full_ref[pl.ds(start, rows), :]


def norm_parts(values):
    center = jnp.mean(values, axis=-1, keepdims=True)
    centered = values - center
    variance = jnp.mean(centered * centered, axis=-1, keepdims=True)
    inverse = lax.rsqrt(variance + NORM_EPS)
    return centered * inverse, inverse


def norm_back(normalized, inverse, gain, grad):
    scaled = grad * gain
    mean_one = jnp.mean(scaled, axis=-1, keepdims=True)
    mean_two = jnp.mean(scaled * normalized, axis=-1, keepdims=True)
    return inverse * (scaled - mean_one - normalized * mean_two)


def contract_rows(left_side, right_side):
    return lax.dot_general(
        left_side, right_side, (((0,), (0,)), ((), ())), preferred_element_type=F32
    )


def contract_cols(left_side, right_side):
    return lax.dot_general(
        left_side, right_side, (((1,), (1,)), ((), ())), preferred_element_type=F32
    )


def adam_update(master, gradient, moment_one, moment_two, step_rate):
    first_new = BETA_ONE * moment_one + (1.0 - BETA_ONE) * gradient
    second_new = BETA_TWO * moment_two + (1.0 - BETA_TWO) * gradient * gradient
    fix_one = 1.0 - BETA_ONE**STEP_NUM
    fix_two = 1.0 - BETA_TWO**STEP_NUM
    step_dir = first_new / fix_one / (jnp.sqrt(second_new / fix_two) + ADAM_EPS)
    return (master - step_rate * (step_dir + DECAY * master), first_new, second_new)


def dot(left_side, right_side):
    return jnp.dot(left_side, right_side, preferred_element_type=F32)


def chosen(values, index):
    result = values[0]
    for at in range(1, len(values)):
        result = jnp.where(index == at, values[at], result)
    return result


def mask_bias(seg_col_ref, seg_row_ref, start, keys):
    same = seg_col_ref[:keys, 0:1] == seg_row_ref[0:1, start : start + BLOCK]
    key_at = lax.broadcasted_iota(jnp.int32, (keys, BLOCK), 0)
    query_at = lax.broadcasted_iota(jnp.int32, (keys, BLOCK), 1) + start
    return jnp.where(same & (key_at <= query_at), 0.0, MASKED)


def head_lanes(shape, head):
    lane = lax.broadcasted_iota(jnp.int32, shape, 1)
    return (lane >= head * HEAD_DIM) & (lane < (head + 1) * HEAD_DIM)


def attend(q_ref, k_ref, v_ref, seg_col_ref, seg_row_ref, out_ref, lse_ref):
    total, width = q_ref.shape
    heads = width // HEAD_DIM
    value_t = v_ref[...].T
    lse_ref[...] = jnp.zeros_like(lse_ref)
    for start in range(0, total, BLOCK):
        keys = start + BLOCK
        bias = mask_bias(seg_col_ref, seg_row_ref, start, keys)
        query = q_ref[start : start + BLOCK, :]
        pieces = []
        for head in range(heads):
            masked = jnp.where(head_lanes(query.shape, head), query, 0)
            scores = contract_cols(k_ref[:keys, :], masked) + bias
            peak = jnp.max(scores, axis=0, keepdims=True)
            exponent = jnp.exp(scores - peak)
            row_total = jnp.sum(exponent, axis=0, keepdims=True)
            mixed = dot(
                value_t[head * HEAD_DIM : (head + 1) * HEAD_DIM, :keys], exponent.astype(BF16)
            )
            pieces.append(mixed / row_total)
            lse_ref[head : head + 1, start : start + BLOCK] = peak + jnp.log(row_total)
        out_ref[start : start + BLOCK, :] = jnp.concatenate(pieces, axis=0).T.astype(BF16)


def attend_back(
    q_ref, k_ref, v_ref, do_ref, lse_ref, seg_col_ref, seg_row_ref, grad_ref, dk_ref, dv_ref
):
    total, width = q_ref.shape
    heads = width // HEAD_DIM
    key_t = k_ref[...].T
    dk_ref[...] = jnp.zeros_like(dk_ref)
    dv_ref[...] = jnp.zeros_like(dv_ref)
    for start in range(0, total, BLOCK):
        keys = start + BLOCK
        bias = mask_bias(seg_col_ref, seg_row_ref, start, keys)
        query = q_ref[start : start + BLOCK, :]
        grad = do_ref[start : start + BLOCK, :]
        pieces = []
        dk = dk_ref[:keys, :]
        dv = dv_ref[:keys, :]
        for head in range(heads):
            lanes = head_lanes(query.shape, head)
            query_h = jnp.where(lanes, query, 0)
            grad_h = jnp.where(lanes, grad, 0)
            scores = contract_cols(k_ref[:keys, :], query_h) + bias
            probs = jnp.exp(scores - lse_ref[head : head + 1, start : start + BLOCK])
            prob_grad = contract_cols(v_ref[:keys, :], grad_h)
            inner = jnp.sum(prob_grad * probs, axis=0, keepdims=True)
            score_grad = (probs * (prob_grad - inner)).astype(BF16)
            dv = dv + dot(probs.astype(BF16), grad_h)
            dk = dk + dot(score_grad, query_h)
            pieces.append(
                dot(key_t[head * HEAD_DIM : (head + 1) * HEAD_DIM, :keys], score_grad)
            )
        dk_ref[:keys, :] = dk
        dv_ref[:keys, :] = dv
        dq = jnp.concatenate(pieces, axis=0).T * HEAD_DIM ** (-0.5)
        grad_ref[start : start + BLOCK, :width] = dq.astype(BF16)
    grad_ref[:, width : 2 * width] = dk_ref[...].astype(BF16)
    grad_ref[:, 2 * width :] = dv_ref[...].astype(BF16)


def call(kernel, outs, scratch, flops, limit, *operands):
    sizes = [o.size * o.dtype.itemsize for o in operands] + [
        o.size * jnp.dtype(o.dtype).itemsize for o in outs
    ]
    vmem = pl.BlockSpec(memory_space=pltpu.VMEM)
    return pl.pallas_call(
        kernel,
        out_shape=tuple(outs),
        in_specs=[pl.BlockSpec(memory_space=pltpu.SMEM)] + [vmem] * (len(operands) - 1),
        out_specs=tuple([vmem] * len(outs)),
        scratch_shapes=scratch,
        compiler_params=pltpu.CompilerParams(vmem_limit_bytes=limit * 2**20),
        cost_estimate=pl.CostEstimate(
            flops=flops, bytes_accessed=sum(sizes), transcendentals=0
        ),
    )(*operands)


def shape(*dims, dtype=BF16):
    return jax.ShapeDtypeStruct(dims, dtype)


def send_parts(value, at, near_ref, far_ref, own_ref):
    rows = value.shape[0]

    @pl.when(at == 0)
    def _():
        own_ref[...] = value

    @pl.when(at == 1)
    def _():
        near_ref[rows:, :] = value.astype(BF16)

    @pl.when(at == 2)
    def _():
        far_ref[...] = value

    @pl.when(at == 3)
    def _():
        near_ref[:rows, :] = value.astype(BF16)


def rep_sum(near_send, far_part, gate=None):
    rows = far_part.shape[0]
    near = swapped(near_send, 1)
    far_send = (far_part + near[:rows].astype(F32)).astype(BF16)
    if gate is not None:
        far_send = after(far_send, gate)
    return near, swapped(far_send, 2), far_send


def place_store(target, columns, limit=None):
    def store(start, ref, first, rows):
        target[pl.ds(start, rows), :limit] = ref[first : first + rows, columns]

    return store


def first_prep_kernel(place_ref, qkv_ref, small_ref, first_ref, small_rows):
    rep = place_ref[0]
    owned, width = qkv_ref.shape[0], qkv_ref.shape[1] // 3
    part = width // SPAN
    small_rows[...] = jnp.zeros_like(small_rows)
    small_rows[: small_ref.shape[0], : small_ref.shape[1]] = small_ref[...]
    for which in range(3):
        first = which * width
        options = [qkv_ref[:, first + r * part : first + (r + 1) * part] for r in range(SPAN)]
        first_ref[:, which * part : (which + 1) * part] = chosen(options, rep).astype(BF16)
    first_ref[:, 3 * part :] = small_rows[...].T[:owned, :64].astype(BF16)


def second_prep_kernel(place_ref, out_ref, up_ref, down_ref, second_ref, third_ref):
    rep = place_ref[0]
    cut = out_ref.shape[1] // 3
    units = third_ref.shape[0]
    second_ref[:, :cut] = out_ref[:, :cut].astype(BF16)
    pieces = []
    for first in range(0, up_ref.shape[1], SPAN * units):
        options = [up_ref[:, first + r * units : first + (r + 1) * units] for r in range(SPAN)]
        pieces.append(chosen(options, rep))
    second_ref[:, cut:] = jnp.concatenate(pieces, axis=1).astype(BF16)
    third_ref[:, : 2 * cut] = out_ref[:, cut:].astype(BF16)
    start = pl.multiple_of(rep * units, units)
    third_ref[:, 2 * cut :] = down_ref[pl.ds(start, units), :].astype(BF16)


def first_kernel(pieces, *refs):
    place_ref, refs = refs[0], refs[1:]
    token_refs, refs = refs[:SPAN], refs[SPAN:]
    count = len(pieces.arrays)
    weight_refs, refs = refs[:count], refs[count:]
    (
        all_ref,
        weight_ref,
        small_ref,
        q_ref,
        k_ref,
        v_ref,
        seg_col_ref,
        seg_row_ref,
        out_ref,
        lse_ref,
        small_cols,
    ) = refs
    rep, shard = place_ref[0], place_ref[1]
    total, width = all_ref.shape
    rows = total // SPAN
    part = q_ref.shape[1]
    pieces.place(shard, weight_refs, place_store(weight_ref, slice(0, 3 * part)))
    last = small_cols.shape[1]
    pieces.place(
        shard, weight_refs, place_store(small_cols, slice(3 * part + 64 - last, 3 * part + 64))
    )
    small = small_cols[...].astype(F32).T
    small = small[last - 64 : last - 48, :]
    small_ref[...] = small
    gain, bias = small[0:1, :], small[1:2, :]
    query_bias = chosen([small[2:3, r * part : (r + 1) * part] for r in range(SPAN)], rep)
    value_bias = chosen([small[3:4, r * part : (r + 1) * part] for r in range(SPAN)], rep)
    for at in range(SPAN):
        start = pl.multiple_of((rep ^ at) * rows, rows)
        block = token_refs[at][:rows, :]
        all_ref[pl.ds(start, rows), :] = block
        hidden = (norm_parts(block.astype(F32))[0] * gain + bias).astype(BF16)
        segs = token_refs[at][rows : rows + 16, :rows].astype(F32)
        seg_row_ref[:, pl.ds(start, rows)] = segs[:8, :]
        seg_col_ref[pl.ds(start, rows), 0:16] = segs.T
        projected = dot(hidden, weight_ref[...])
        q_ref[pl.ds(start, rows), :] = (
            (projected[:, :part] + query_bias) * HEAD_DIM ** (-0.5)
        ).astype(BF16)
        k_ref[pl.ds(start, rows), :] = projected[:, part : 2 * part].astype(BF16)
        v_ref[pl.ds(start, rows), :] = (projected[:, 2 * part :] + value_bias).astype(BF16)
    attend(q_ref, k_ref, v_ref, seg_col_ref, seg_row_ref, out_ref, lse_ref)


def second_kernel(pieces, place_ref, *refs):
    attended_refs, refs = refs[:SPAN], refs[SPAN:]
    cot_refs, refs = refs[:SPAN], refs[SPAN:]
    count = len(pieces.arrays)
    piece_refs, refs = refs[:count], refs[count:]
    (
        wide_ref,
        all_ref,
        small_ref,
        up_bias_ref,
        out_own_ref,
        hidden_ref,
        act_ref,
        pre_ref,
        residual_ref,
        near_ref,
        far_ref,
        own_ref,
        up_weight,
        out_weight,
        cot_ref,
    ) = refs
    rep = place_ref[0]
    total, width = all_ref.shape
    rows = total // SPAN
    part = attended_refs[0].shape[1]
    cut = width // 3
    pieces.place(place_ref[1], piece_refs, place_store(up_weight, slice(cut, None)))
    pieces.place(place_ref[1], piece_refs, place_store(out_weight, slice(0, cut), cut))
    out_weight[:, cut:] = wide_ref[:, : 2 * cut]
    own_rows = pl.ds(pl.multiple_of(rep * part, part), part)
    out_own_ref[...] = out_weight[own_rows, :]
    for at in range(SPAN):
        cot_ref[pl.ds(pl.multiple_of((rep ^ at) * rows, rows), rows), :] = cot_refs[at][...]
    out_bias, gain, bias = small_ref[4:5, :], small_ref[5:6, :], small_ref[6:7, :]

    @pl.loop(0, SPAN)
    def _(index):
        block = pl.ds(pl.multiple_of(index * rows, rows), rows)
        mixed = out_bias
        for at in range(SPAN):
            from_rows = pl.ds(pl.multiple_of((rep ^ at) * part, part), part)
            mixed = mixed + dot(attended_refs[at][block, :], out_weight[from_rows, :])
        residual = all_ref[block, :].astype(F32) + mixed

        @pl.when(index == rep)
        def _():
            residual_ref[...] = residual

        hidden = (norm_parts(residual)[0] * gain + bias).astype(BF16)
        hidden_ref[block, :] = hidden
        pre_act = dot(hidden, up_weight[...]) + up_bias_ref[...]
        cdf = 0.5 * (1.0 + lax.erf(pre_act * (0.5**0.5)))
        act_ref[block, :] = (pre_act * cdf).astype(BF16)
        slope = cdf + pre_act * (jnp.exp(-0.5 * pre_act * pre_act) * 0.3989422804014327)
        pre_low = (contract_cols(cot_ref[block, :], wide_ref[:, 2 * cut :]) * slope).astype(BF16)
        pre_ref[block, :] = pre_low
        grad = contract_cols(pre_low, up_weight[...])
        send_parts(grad, index ^ rep, near_ref, far_ref, own_ref)


def down_grad_kernel(place_ref, act_ref, cot_a, cot_b, cot_c, cot_d, *refs):
    grad_refs, (grad_ref, cot_ref) = refs[:-2], refs[-2:]
    rows = cot_a.shape[0]
    for at, ref in enumerate((cot_a, cot_b, cot_c, cot_d)):
        start = pl.multiple_of((place_ref[0] ^ at) * rows, rows)
        cot_ref[pl.ds(start, rows), :] = ref[...]
    units = act_ref.shape[1]
    step = units // 3
    for first in range(0, units, step):
        grad_ref[first : first + step, :] = contract_rows(
            act_ref[:, first : first + step], cot_ref[...]
        ).astype(BF16)
    if len(grad_refs) == 2:
        split_halves(place_ref, grad_ref, *grad_refs)
    else:
        grad_refs[0][...] = grad_ref[...]


def third_kernel(place_ref, act_ref, hidden_ref, pre_ref, wide_ref, *refs):
    grad_refs, (near_ref, far_ref, own_ref, sum_ref, grad_ref) = refs[:-5], refs[-5:]
    rep = place_ref[0]
    total, width = hidden_ref.shape
    rows = total // SPAN
    step = width // 3
    for first in range(0, width, step):
        grad_ref[first : first + step, :] = contract_rows(
            hidden_ref[:, first : first + step], pre_ref[...]
        ).astype(BF16)
    sum_ref[...] = jnp.broadcast_to(
        jnp.sum(pre_ref[...].astype(F32), axis=0, keepdims=True), sum_ref.shape
    )

    @pl.loop(0, SPAN)
    def _(index):
        block = pl.ds(pl.multiple_of(index * rows, rows), rows)
        send_parts(
            dot(act_ref[block, :], wide_ref[:, -width:]), index ^ rep, near_ref, far_ref, own_ref
        )

    if len(grad_refs) == 2:
        split_halves(place_ref, grad_ref, *grad_refs)
    else:
        grad_refs[0][...] = grad_ref[...]


def fourth_kernel(
    place_ref,
    own_ref,
    near_ref,
    far_ref,
    residual_ref,
    cotangent_ref,
    small_ref,
    resid_grad_ref,
    branch_ref,
    sums_ref,
):
    grad = own_ref[...] + near_ref[own_ref.shape[0] :, :].astype(F32) + far_ref[...].astype(F32)
    normalized, inverse = norm_parts(residual_ref[...])
    cotangent = cotangent_ref[...].astype(F32)
    resid_grad = cotangent + norm_back(normalized, inverse, small_ref[5:6, :], grad)
    branch = resid_grad.astype(BF16)
    resid_grad_ref[...] = resid_grad
    branch_ref[...] = branch
    sums_ref[...] = jnp.zeros_like(sums_ref)
    sums_ref[4:5, :] = jnp.sum(branch.astype(F32), axis=0, keepdims=True)
    sums_ref[5:6, :] = jnp.sum(grad * normalized, axis=0, keepdims=True)
    sums_ref[6:7, :] = jnp.sum(grad, axis=0, keepdims=True)
    sums_ref[7:8, :] = jnp.sum(cotangent, axis=0, keepdims=True)


def fifth_kernel(
    place_ref,
    branch_a,
    branch_b,
    branch_c,
    branch_d,
    attended_a,
    attended_b,
    attended_c,
    attended_d,
    out_weight,
    qkv_weight,
    q_ref,
    k_ref,
    v_ref,
    lse_ref,
    seg_col_ref,
    seg_row_ref,
    all_ref,
    small_ref,
    sums_ref,
    unit_sums_ref,
    *refs,
):
    grad_refs, refs = refs[:-11], refs[-11:]
    (
        near_ref,
        far_ref,
        own_ref,
        branch_ref,
        back_ref,
        proj_ref,
        dk_ref,
        dv_ref,
        small_grads,
        grad_ref,
        hidden_ref,
    ) = refs
    rep = place_ref[0]
    total, width = all_ref.shape
    rows = total // SPAN
    part = q_ref.shape[1]
    for at, ref in enumerate((branch_a, branch_b, branch_c, branch_d)):
        start = pl.multiple_of((rep ^ at) * rows, rows)
        branch_ref[pl.ds(start, rows), :] = ref[...]
    back_ref[...] = contract_cols(branch_ref[...], out_weight[...]).astype(BF16)
    attend_back(
        q_ref,
        k_ref,
        v_ref,
        back_ref,
        lse_ref,
        seg_col_ref,
        seg_row_ref,
        proj_ref,
        dk_ref,
        dv_ref,
    )
    gain = small_ref[0:1, :]
    small_grads[...] = jnp.zeros_like(small_grads)
    small_grads[0:8, :] = sums_ref[...]
    small_grads[8:16, :] = unit_sums_ref[...]

    @pl.loop(0, SPAN)
    def _(index):
        block = pl.ds(pl.multiple_of(index * rows, rows), rows)
        grad = contract_cols(proj_ref[block, :], qkv_weight[...])
        normalized = norm_parts(all_ref[block, :].astype(F32))[0]
        hidden_ref[block, :] = (normalized * gain + small_ref[1:2, :]).astype(BF16)
        small_grads[0:1, :] += jnp.sum(grad * normalized, axis=0, keepdims=True)
        small_grads[1:2, :] += jnp.sum(grad, axis=0, keepdims=True)
        send_parts(grad, index ^ rep, near_ref, far_ref, own_ref)

    lane = lax.broadcasted_iota(jnp.int32, (1, width), 1)
    mine = (lane >= rep * part) & (lane < (rep + 1) * part)
    for row, first in ((2, 0), (3, 2 * part)):
        column_sum = jnp.sum(
            proj_ref[:, first : first + part].astype(F32), axis=0, keepdims=True
        )
        small_grads[row : row + 1, :] = jnp.where(
            mine, jnp.concatenate([column_sum] * SPAN, axis=1), 0.0
        )
    step = width // 3
    for first in range(0, width, step):
        grad_ref[first : first + step, : 3 * part] = contract_rows(
            hidden_ref[:, first : first + step], proj_ref[...]
        ).astype(BF16)
    branch_part = chosen(
        [branch_ref[:, r * part : (r + 1) * part] for r in range(SPAN)], rep
    )
    for at, ref in enumerate((attended_a, attended_b, attended_c, attended_d)):
        from_rows = pl.ds(pl.multiple_of((rep ^ at) * part, part), part)
        grad_ref[from_rows, 3 * part : 4 * part] = contract_rows(ref[...], branch_part).astype(
            BF16
        )
    grad_ref[:, 4 * part :] = small_grads[...].T.astype(BF16)
    if len(grad_refs) == 2:
        split_halves(place_ref, grad_ref, *grad_refs)
    else:
        grad_refs[0][...] = grad_ref[...]


def sixth_kernel(
    place_ref, own_ref, near_ref, far_ref, tokens_ref, resid_grad_ref, small_ref, out_ref
):
    grad = own_ref[...] + near_ref[own_ref.shape[0] :, :].astype(F32) + far_ref[...].astype(F32)
    normalized, inverse = norm_parts(tokens_ref[...].astype(F32))
    out_ref[...] = resid_grad_ref[...] + norm_back(normalized, inverse, small_ref[0:1, :], grad)


def rep_order(refs, rep):
    blocks = [ref[...].astype(F32) for ref in refs]
    odd, high = (rep & 1) == 1, (rep & 2) == 2
    pairs = []
    for first in (0, 2):
        lower, upper = blocks[first], blocks[first + 1]
        pairs.append((jnp.where(odd, upper, lower), jnp.where(odd, lower, upper)))
    low = [jnp.where(high, b, a) for a, b in zip(*pairs)]
    return low + [jnp.where(high, a, b) for a, b in zip(*pairs)]


def adam_kernel(place_ref, *refs):
    blocks = rep_order(refs[:SPAN], place_ref[0])
    small_refs, refs = refs[SPAN : 2 * SPAN], refs[2 * SPAN :]
    ins, outs = refs[:9], refs[9:]
    part = ins[3].shape[1] // SPAN
    qkv = [b[:, c * part : (c + 1) * part] for c in range(3) for b in blocks]
    out = [b[:, 3 * part : 4 * part] for b in blocks]

    def update(at, gradient, rate):
        weight, first, second = (ref[...] for ref in ins[3 * at : 3 * at + 3])
        results = adam_update(weight, gradient, first, second, rate)
        for ref, value in zip(outs[3 * at : 3 * at + 3], results):
            ref[...] = value

    update(0, jnp.concatenate(qkv, axis=1), RATE_MATRIX)
    update(1, jnp.concatenate(out, axis=1), RATE_MATRIX)

    @pl.when(pl.program_id(0) == 0)
    def _():
        small = small_refs[0][...].astype(F32)
        for ref in small_refs[1:]:
            small = small + ref[...].astype(F32)
        update(2, small.T[: ins[6].shape[0], :], RATE_SMALL)


def last_adam(place, blocks, arrays):
    steps = 3
    rows, columns = arrays[0].shape
    width = arrays[3].shape[1]

    def row_block(count):
        return pl.BlockSpec((rows // steps, count), lambda i: (i, 0))

    whole = pl.BlockSpec(arrays[6].shape, lambda i: (0, 0))
    specs = [row_block(columns)] * 3 + [row_block(width)] * 3 + [whole] * 3
    small = pl.BlockSpec((rows, 128), lambda i: (0, width // 128))
    return pl.pallas_call(
        adam_kernel,
        grid=(steps,),
        out_shape=[shape(*a.shape, dtype=F32) for a in arrays],
        in_specs=[pl.BlockSpec(memory_space=pltpu.SMEM)]
        + [row_block(width)] * SPAN
        + [small] * SPAN
        + specs,
        out_specs=specs,
        compiler_params=pltpu.CompilerParams(vmem_limit_bytes=16 * 2**20),
    )(place, *blocks, *blocks, *arrays)


def up_adam_kernel(place_ref, *refs):
    blocks = rep_order(refs[:SPAN], place_ref[0])
    weight, first, second, *outs = refs[SPAN:]
    width = weight.shape[1] // SPAN
    units = width // FEW
    pieces = [b[:, at * units : (at + 1) * units] for at in range(FEW) for b in blocks]
    results = adam_update(
        weight[...], jnp.concatenate(pieces, axis=1), first[...], second[...], RATE_MATRIX
    )
    for ref, value in zip(outs, results):
        ref[...] = value


def down_adam_kernel(place_ref, *refs):
    at = pl.program_id(0) ^ place_ref[0]
    gradient = chosen([ref[...] for ref in refs[:SPAN]], at).astype(F32)
    weight, first, second, *outs = refs[SPAN:]
    results = adam_update(weight[...], gradient, first[...], second[...], RATE_MATRIX)
    for ref, value in zip(outs, results):
        ref[...] = value


def grid_adam(kernel, steps, place, blocks, block_spec, arrays):
    rows, columns = arrays[0].shape
    spec = pl.BlockSpec((rows // steps, columns), lambda i: (i, 0))
    return list(pl.pallas_call(
        kernel,
        grid=(steps,),
        out_shape=[shape(rows, columns, dtype=F32)] * 3,
        in_specs=[pl.BlockSpec(memory_space=pltpu.SMEM)]
        + [block_spec] * SPAN
        + [spec] * 3,
        out_specs=[spec] * 3,
        compiler_params=pltpu.CompilerParams(vmem_limit_bytes=16 * 2**20),
        cost_estimate=pl.CostEstimate(
            flops=0, bytes_accessed=0, transcendentals=0
        ),
    )(place, *blocks, *arrays))


def in_order(blocks, rep):
    odd = (rep & 1) == 1
    high = (rep & 2) == 2
    low_pair = (jnp.where(odd, blocks[1], blocks[0]), jnp.where(odd, blocks[0], blocks[1]))
    high_pair = (jnp.where(odd, blocks[3], blocks[2]), jnp.where(odd, blocks[2], blocks[3]))
    return (
        jnp.where(high, high_pair[0], low_pair[0]),
        jnp.where(high, high_pair[1], low_pair[1]),
        jnp.where(high, low_pair[0], high_pair[0]),
        jnp.where(high, low_pair[1], high_pair[1]),
    )


def local(
    tokens,
    cotangent,
    segments,
    qkv_weight,
    out_weight,
    up_weight,
    down_weight,
    small_weights,
    qkv_first,
    out_first,
    up_first,
    down_first,
    small_first,
    qkv_second,
    out_second,
    up_second,
    down_second,
    small_second,
):
    rep = lax.axis_index("rep")
    shards = lax.axis_size("shard")
    place = jnp.stack([rep, lax.axis_index("shard")]).astype(jnp.int32)
    rows, width = tokens.shape
    total = SPAN * rows
    part = width // SPAN
    owned = qkv_weight.shape[0]
    ff = up_weight.shape[1]
    ff_part = ff // SPAN
    units = down_weight.shape[0] // SPAN

    def rep_part(block, size, axis):
        return lax.dynamic_slice_in_dim(block, rep * size, size, axis)

    few = shards == FEW
    third = width // 3
    if few:
        first_send = call(
            first_prep_kernel,
            [shape(owned, 3 * part + 64)],
            [pltpu.VMEM((128, 128), F32)],
            owned * width,
            56,
            place,
            qkv_weight,
            small_weights,
        )[0]
        second_send, third_send = call(
            second_prep_kernel,
            [shape(owned, third + ff_part), shape(units, 2 * third + width)],
            [],
            owned * width,
            56,
            place,
            out_weight,
            up_weight,
            down_weight,
        )
    else:
        low_small = small_weights.astype(BF16).T
        low_qkv = rep_part(qkv_weight.astype(BF16).reshape(owned, 3, SPAN, part), 1, 2)
        low_qkv = low_qkv.reshape(owned, 3 * part)
        pad = 64 - low_small.shape[1]
        first_send = jnp.concatenate([low_qkv, jnp.pad(low_small, ((0, 0), (0, pad)))], axis=1)
        low_up = rep_part(up_weight.astype(BF16).reshape(owned, shards, SPAN, units), 1, 2)
        low_down = rep_part(down_weight, units, 0).astype(BF16)
        low_out = out_weight.astype(BF16)
        second_send = jnp.concatenate([low_out[:, :third], low_up.reshape(owned, -1)], axis=1)
        third_send = jnp.concatenate([low_out[:, third:], low_down], axis=1)
    third_full = lax.all_gather(third_send, "shard", axis=0, tiled=True)
    first_pieces, second_pieces = shard_gather(first_send, second_send)

    seg_block = jnp.pad(segments.astype(BF16)[None, :], ((0, 15), (0, width - rows)))
    with_seg = jnp.concatenate([tokens, seg_block], axis=0)
    token_blocks = rep_blocks(with_seg)
    cot_blocks = rep_blocks(after(cotangent, token_blocks[2]))

    (
        all_tokens,
        qkv_part,
        small,
        queries,
        keys,
        values,
        seg_col,
        seg_row,
        attended,
        log_total,
    ) = call(
        lambda *refs: first_kernel(first_pieces, *refs),
        [
            shape(total, width),
            shape(width, 3 * part),
            shape(16, width, dtype=F32),
            shape(total, part),
            shape(total, part),
            shape(total, part),
            shape(total, 128, dtype=F32),
            shape(8, total, dtype=F32),
            shape(total, part),
            shape(8, total, dtype=F32),
        ],
        [pltpu.VMEM((width, 128), BF16)],
        12 * total * width * width + 24 * total * total * part,
        56,
        place,
        *token_blocks,
        *first_pieces.arrays,
    )
    up_bias = rep_part(small[8:12].reshape(shards, SPAN, units), 1, 1).reshape(1, -1)
    attended_blocks = rep_blocks(attended)
    (
        out_own,
        hidden_two,
        act_low,
        pre_low,
        residual,
        near_send,
        far_part,
        own,
    ) = call(
        lambda *refs: second_kernel(second_pieces, *refs),
        [
            shape(part, width),
            shape(total, width),
            shape(total, ff_part),
            shape(total, ff_part),
            shape(rows, width, dtype=F32),
            shape(2 * rows, width),
            shape(rows, width, dtype=F32),
            shape(rows, width, dtype=F32),
        ],
        [
            pltpu.VMEM((width, ff_part), BF16),
            pltpu.VMEM((width, width), BF16),
            pltpu.VMEM((total, width), BF16),
        ],
        32 * total * width * width,
        56,
        place,
        *attended_blocks,
        *cot_blocks,
        *second_pieces.arrays,
        third_full,
        all_tokens,
        small,
        up_bias,
    )
    near, far, far_send = rep_sum(near_send, far_part)
    hidden_two_terms = own, near, far
    down_grad = call(
        down_grad_kernel,
        [shape(ff_part // 2, width)] * 2 * few + [shape(ff_part, width)] * (not few),
        [pltpu.VMEM((ff_part, width), BF16), pltpu.VMEM((total, width), BF16)],
        6 * total * width * width,
        56,
        place,
        after(act_low, far_send),
        *cot_blocks,
    )
    *up_grad, mixed_near, mixed_far, mixed_own, unit_sums = call(
        third_kernel,
        [shape(width // 2, ff_part)] * 2 * few
        + [shape(width, ff_part)] * (not few)
        + [
            shape(2 * rows, width),
            shape(rows, width, dtype=F32),
            shape(rows, width, dtype=F32),
            shape(8, ff_part, dtype=F32),
        ],
        [pltpu.VMEM((width, ff_part), BF16)],
        12 * total * width * width,
        56,
        place,
        after(act_low, down_grad[0]),
        hidden_two,
        pre_low,
        third_full,
    )
    if few:
        down_received = swap_shard(down_grad[1], 1)
    near, unit_sums = lax.optimization_barrier((near, unit_sums))
    hidden_two_terms = own, near, far
    resid_grad, branch, sums = call(
        fourth_kernel,
        [
            shape(rows, width, dtype=F32),
            shape(rows, width),
            shape(8, width, dtype=F32),
        ],
        [],
        10 * rows * width,
        56,
        place,
        *hidden_two_terms,
        residual,
        cotangent,
        small,
    )
    branch_blocks = rep_blocks(branch, None, down_received if few else None)
    if few:
        down_own, down_received = scatter_high(place, after(down_grad[0], branch), down_received)
        branch_blocks = (after(branch, down_own),) + branch_blocks[1:]
        up_received = swap_shard(up_grad[1], 1)
    unit_rows = lax.dynamic_update_slice(
        jnp.zeros((shards, SPAN, units), F32), unit_sums[0].reshape(shards, 1, units), (0, rep, 0)
    ).reshape(ff // width, width)
    unit_rows = jnp.pad(unit_rows, ((0, 8 - ff // width), (0, 0)))
    *last_grad, near_send, far_part, own = call(
        fifth_kernel,
        [shape(width // 2, 4 * part + 128)] * 2 * few
        + [shape(width, 4 * part + 128)] * (not few)
        + [
            shape(2 * rows, width),
            shape(rows, width, dtype=F32),
            shape(rows, width, dtype=F32),
        ],
        [
            pltpu.VMEM((total, width), BF16),
            pltpu.VMEM((total, part), BF16),
            pltpu.VMEM((total, 3 * part), BF16),
            pltpu.VMEM((total, part), F32),
            pltpu.VMEM((total, part), F32),
            pltpu.VMEM((128, width), F32),
            pltpu.VMEM((width, 4 * part + 128), BF16),
            pltpu.VMEM((total, width), BF16),
        ],
        12 * total * width * width + 72 * total * total * part,
        56,
        place,
        *branch_blocks,
        *attended_blocks,
        out_own,
        qkv_part,
        queries,
        keys,
        values,
        log_total,
        seg_col,
        seg_row,
        all_tokens,
        small,
        sums,
        unit_rows,
    )
    if few:
        last_kept, last_sent = last_grad
        last_sent, near_send, down_received, up_received = lax.optimization_barrier(
            (last_sent, near_send, down_received, up_received)
        )
    near, far, _ = rep_sum(near_send, far_part)
    near_mixed, far_mixed, _ = rep_sum(mixed_near, mixed_far, far)
    if few:
        last_kept, far = lax.optimization_barrier((last_kept, far))
        last_own, last_received = scatter_middle(place, last_kept, last_sent)
        far_mixed = after(far_mixed, last_own)
        up_own, up_received = scatter_high(
            place, after(up_grad[0], (last_grad[0], down_received)), up_received
        )
        down_own, up_received = after((down_own, up_received), last_own)
        wide_total = jnp.concatenate(
            [scatter_end(down_own, down_received), scatter_end(up_own, up_received)], axis=1
        )
        wide_blocks = rep_blocks(wide_total, last_received)
    else:
        last_total, down_total, up_total = (
            lax.psum_scatter(grad, "shard", scatter_dimension=0, tiled=True)
            for grad in (last_grad[0], down_grad[0], up_grad[0])
        )
    mixed = residual + (
        mixed_own + near_mixed[rows:].astype(F32) + far_mixed.astype(F32) + small[7]
    )
    mixed = mixed.astype(BF16)
    input_grad = call(
        sixth_kernel,
        [shape(rows, width, dtype=F32)],
        [],
        10 * rows * width,
        56,
        place,
        own,
        near,
        far,
        tokens,
        resid_grad,
        small,
    )[0]
    if few:
        up_res = grid_adam(
            up_adam_kernel,
            3,
            place,
            wide_blocks,
            pl.BlockSpec((owned // 3, width), lambda i: (i, 1)),
            (up_weight, up_first, up_second),
        )
        down_res = grid_adam(
            down_adam_kernel,
            SPAN,
            place,
            wide_blocks,
            pl.BlockSpec((units, width), lambda i: (0, 0)),
            (down_weight, down_first, down_second),
        )
        last_received, input_grad, mixed = lax.optimization_barrier(
            (last_received, input_grad, mixed)
        )
        last_total = scatter_end(last_own, last_received)
        last_blocks = rep_blocks(last_total, (up_res[0], down_res[0]))
        results = last_adam(
            place,
            last_blocks,
            (
                qkv_weight,
                qkv_first,
                qkv_second,
                out_weight,
                out_first,
                out_second,
                small_weights,
                small_first,
                small_second,
            ),
        )
        qkv_res, out_res, small_res = results[:3], results[3:6], results[6:]
    else:
        down_own = jnp.concatenate(in_order(rep_blocks(down_total), rep), axis=0).astype(F32)
        up_own = in_order(rep_blocks(up_total), rep)
        up_own = [g.reshape(owned, shards, units) for g in up_own]
        up_own = jnp.stack(up_own, axis=2).reshape(owned, ff).astype(F32)
        up_res = adam_update(up_weight, up_own, up_first, up_second, RATE_MATRIX)
        down_res = adam_update(down_weight, down_own, down_first, down_second, RATE_MATRIX)
        last_own = in_order(rep_blocks(last_total), rep)
        out_own = jnp.concatenate([g[:, 3 * part : 4 * part] for g in last_own], axis=1)
        qkv_own = [g[:, : 3 * part].reshape(owned, 3, part) for g in last_own]
        qkv_own = jnp.stack(qkv_own, axis=2).reshape(owned, 3 * width).astype(F32)
        small_own = sum(g[:, 4 * part : 4 * part + 12].astype(F32) for g in last_own).T
        qkv_res = adam_update(qkv_weight, qkv_own, qkv_first, qkv_second, RATE_MATRIX)
        out_res = adam_update(
            out_weight, out_own.astype(F32), out_first, out_second, RATE_MATRIX
        )
        small_res = adam_update(
            small_weights, small_own, small_first, small_second, RATE_SMALL
        )
    return (
        mixed,
        input_grad,
        qkv_res[0],
        out_res[0],
        up_res[0],
        down_res[0],
        small_res[0],
        qkv_res[1],
        out_res[1],
        up_res[1],
        down_res[1],
        small_res[1],
        qkv_res[2],
        out_res[2],
        up_res[2],
        down_res[2],
        small_res[2],
    )


def solution(mesh):
    tokens_spec = P(("rep", "shard"), None)
    rows = P("shard", None)
    columns = P(None, "shard")
    weights = (rows, rows, rows, rows, columns)
    return jax.shard_map(
        local,
        mesh=mesh,
        in_specs=(tokens_spec, tokens_spec, P(("rep", "shard"))) + weights * 3,
        out_specs=(tokens_spec, tokens_spec) + weights * 3,
        check_vma=False,
    )
```

```python
import jax
import jax.numpy as jnp
from jax import lax
from jax.experimental import pallas as pl
from jax.experimental.pallas import tpu as pltpu
from jax.sharding import PartitionSpec as P

HEAD_DIM = 64
SPAN = 4
STEP_NUM = 10


NORM_EPS = 1e-05
BETA_ONE = 0.9
BETA_TWO = 0.95
ADAM_EPS = 1e-08
DECAY = 0.1
RATE_MATRIX = 0.05
RATE_SMALL = 0.3
MASKED = -1e30
BLOCK = 256
FEW = 8
F32 = jnp.float32
BF16 = jnp.bfloat16


def swapped(block, bit):
    return lax.ppermute(block, "rep", [(i, i ^ bit) for i in range(SPAN)])


def rep_blocks(block, gate=None, near_gate=None):
    far = swapped(block, 2)
    near = swapped(block if near_gate is None else after(block, near_gate), 1)
    if gate is not None:
        far = after(far, gate)
    return (block, near, far, swapped(far, 1))


def swap_shard(block, bits):
    return lax.ppermute(block, "shard", [(i, i ^ bits) for i in range(lax.axis_size("shard"))])


def after(block, other):
    return lax.optimization_barrier((block, other))[0]


class Pieces:
    def __init__(self, arrays, codes, rows):
        self.arrays, self.codes, self.rows = arrays, codes, rows

    def place(self, shard, refs, store):
        if self.codes is None:
            store(0, refs[0], 0, refs[0].shape[0])
            return
        for ref, codes in zip(refs, self.codes):
            for index, code in enumerate(codes):
                start = pl.multiple_of((shard ^ code) * self.rows, self.rows)
                store(start, ref, index * self.rows, self.rows)


def shard_gather(block, *others):
    blocks = (block,) + others
    if lax.axis_size("shard") != FEW:
        return [
            Pieces([lax.all_gather(b, "shard", axis=0, tiled=True)], None, b.shape[0])
            for b in blocks
        ]
    crossed = [swap_shard(b, 1) for b in blocks]
    codes = [[0], [1], [2], [4], [6], [3, 5, 7]]
    results = []
    gate = None
    for b, cross in zip(blocks, crossed):
        sent = b if gate is None else after(b, (gate, crossed))
        one, two, three = (swap_shard(sent, bits) for bits in (2, 4, 6))
        gate = three
        other = jnp.concatenate([one, two, three], axis=0)
        other = swap_shard(after(other, crossed), 1)
        results.append(Pieces([b, cross, one, two, three, other], codes, b.shape[0]))
    return results


def middle_kernel(place_ref, kept_ref, received_ref, own_ref, *sent_refs):
    high = place_ref[1] // 2
    rows = own_ref.shape[0]
    for bits in range(len(sent_refs) + 1):
        block = pl.ds(pl.multiple_of((high ^ bits) * rows, rows), rows)
        value = kept_ref[block, :].astype(F32) + received_ref[block, :].astype(F32)
        if bits == 0:
            own_ref[...] = value
        else:
            sent_refs[bits - 1][...] = value.astype(BF16)


def scatter_middle(place, kept, sent):
    return scatter_high(place, kept, swap_shard(sent, 1))


def scatter_high(place, kept, received):
    count = FEW // 2
    rows, columns = kept.shape[0] // count, kept.shape[1]
    own, *sends = call(
        middle_kernel,
        [shape(rows, columns, dtype=F32)] + [shape(rows, columns)] * (count - 1),
        [],
        kept.size,
        56,
        place,
        kept,
        received,
    )
    return own, [swap_shard(send, 2 * (bits + 1)) for bits, send in enumerate(sends)]


def scatter_end(own, received):
    total = own
    for block in received:
        total = total + block.astype(F32)
    return total.astype(BF16)


def split_halves(place_ref, full_ref, kept_ref, sent_ref):
    low = place_ref[1] & 1
    rows = full_ref.shape[0] // FEW
    for at in range(FEW // 2):
        target = slice(at * rows, (at + 1) * rows)
        for ref, bit in ((kept_ref, low), (sent_ref, 1 - low)):
            start = pl.multiple_of((2 * at + bit) * rows, rows)
            ref[target, :] = full_ref[pl.ds(start, rows), :]


def norm_parts(values):
    center = jnp.mean(values, axis=-1, keepdims=True)
    centered = values - center
    variance = jnp.mean(centered * centered, axis=-1, keepdims=True)
    inverse = lax.rsqrt(variance + NORM_EPS)
    return centered * inverse, inverse


def norm_back(normalized, inverse, gain, grad):
    scaled = grad * gain
    mean_one = jnp.mean(scaled, axis=-1, keepdims=True)
    mean_two = jnp.mean(scaled * normalized, axis=-1, keepdims=True)
    return inverse * (scaled - mean_one - normalized * mean_two)


def contract_rows(left_side, right_side):
    return lax.dot_general(
        left_side, right_side, (((0,), (0,)), ((), ())), preferred_element_type=F32
    )


def contract_cols(left_side, right_side):
    return lax.dot_general(
        left_side, right_side, (((1,), (1,)), ((), ())), preferred_element_type=F32
    )


def adam_update(master, gradient, moment_one, moment_two, step_rate):
    first_new = BETA_ONE * moment_one + (1.0 - BETA_ONE) * gradient
    second_new = BETA_TWO * moment_two + (1.0 - BETA_TWO) * gradient * gradient
    fix_one = 1.0 - BETA_ONE**STEP_NUM
    fix_two = 1.0 - BETA_TWO**STEP_NUM
    step_dir = first_new / fix_one / (jnp.sqrt(second_new / fix_two) + ADAM_EPS)
    return (master - step_rate * (step_dir + DECAY * master), first_new, second_new)


def dot(left_side, right_side):
    return jnp.dot(left_side, right_side, preferred_element_type=F32)


def chosen(values, index):
    result = values[0]
    for at in range(1, len(values)):
        result = jnp.where(index == at, values[at], result)
    return result


def mask_bias(seg_col_ref, seg_row_ref, start, keys):
    same = seg_col_ref[:keys, 0:1] == seg_row_ref[0:1, start : start + BLOCK]
    key_at = lax.broadcasted_iota(jnp.int32, (keys, BLOCK), 0)
    query_at = lax.broadcasted_iota(jnp.int32, (keys, BLOCK), 1) + start
    return jnp.where(same & (key_at <= query_at), 0.0, MASKED)


def head_lanes(shape, head):
    lane = lax.broadcasted_iota(jnp.int32, shape, 1)
    return (lane >= head * HEAD_DIM) & (lane < (head + 1) * HEAD_DIM)


def attend(q_ref, k_ref, v_ref, seg_col_ref, seg_row_ref, out_ref, lse_ref):
    total, width = q_ref.shape
    heads = width // HEAD_DIM
    value_t = v_ref[...].T
    lse_ref[...] = jnp.zeros_like(lse_ref)
    for start in range(0, total, BLOCK):
        keys = start + BLOCK
        bias = mask_bias(seg_col_ref, seg_row_ref, start, keys)
        query = q_ref[start : start + BLOCK, :]
        pieces = []
        for head in range(heads):
            masked = jnp.where(head_lanes(query.shape, head), query, 0)
            scores = contract_cols(k_ref[:keys, :], masked) + bias
            peak = jnp.max(scores, axis=0, keepdims=True)
            exponent = jnp.exp(scores - peak)
            row_total = jnp.sum(exponent, axis=0, keepdims=True)
            mixed = dot(
                value_t[head * HEAD_DIM : (head + 1) * HEAD_DIM, :keys], exponent.astype(BF16)
            )
            pieces.append(mixed / row_total)
            lse_ref[head : head + 1, start : start + BLOCK] = peak + jnp.log(row_total)
        out_ref[start : start + BLOCK, :] = jnp.concatenate(pieces, axis=0).T.astype(BF16)


def attend_back(
    q_ref, k_ref, v_ref, do_ref, lse_ref, seg_col_ref, seg_row_ref, grad_ref, dk_ref, dv_ref
):
    total, width = q_ref.shape
    heads = width // HEAD_DIM
    key_t = k_ref[...].T
    dk_ref[...] = jnp.zeros_like(dk_ref)
    dv_ref[...] = jnp.zeros_like(dv_ref)
    for start in range(0, total, BLOCK):
        keys = start + BLOCK
        bias = mask_bias(seg_col_ref, seg_row_ref, start, keys)
        query = q_ref[start : start + BLOCK, :]
        grad = do_ref[start : start + BLOCK, :]
        pieces = []
        dk = dk_ref[:keys, :]
        dv = dv_ref[:keys, :]
        for head in range(heads):
            lanes = head_lanes(query.shape, head)
            query_h = jnp.where(lanes, query, 0)
            grad_h = jnp.where(lanes, grad, 0)
            scores = contract_cols(k_ref[:keys, :], query_h) + bias
            probs = jnp.exp(scores - lse_ref[head : head + 1, start : start + BLOCK])
            prob_grad = contract_cols(v_ref[:keys, :], grad_h)
            inner = jnp.sum(prob_grad * probs, axis=0, keepdims=True)
            score_grad = (probs * (prob_grad - inner)).astype(BF16)
            dv = dv + dot(probs.astype(BF16), grad_h)
            dk = dk + dot(score_grad, query_h)
            pieces.append(
                dot(key_t[head * HEAD_DIM : (head + 1) * HEAD_DIM, :keys], score_grad)
            )
        dk_ref[:keys, :] = dk
        dv_ref[:keys, :] = dv
        dq = jnp.concatenate(pieces, axis=0).T * HEAD_DIM ** (-0.5)
        grad_ref[start : start + BLOCK, :width] = dq.astype(BF16)
    grad_ref[:, width : 2 * width] = dk_ref[...].astype(BF16)
    grad_ref[:, 2 * width :] = dv_ref[...].astype(BF16)


def call(kernel, outs, scratch, flops, limit, *operands):
    sizes = [o.size * o.dtype.itemsize for o in operands] + [
        o.size * jnp.dtype(o.dtype).itemsize for o in outs
    ]
    vmem = pl.BlockSpec(memory_space=pltpu.VMEM)
    return pl.pallas_call(
        kernel,
        out_shape=tuple(outs),
        in_specs=[pl.BlockSpec(memory_space=pltpu.SMEM)] + [vmem] * (len(operands) - 1),
        out_specs=tuple([vmem] * len(outs)),
        scratch_shapes=scratch,
        compiler_params=pltpu.CompilerParams(vmem_limit_bytes=limit * 2**20),
        cost_estimate=pl.CostEstimate(
            flops=flops, bytes_accessed=sum(sizes), transcendentals=0
        ),
    )(*operands)


def shape(*dims, dtype=BF16):
    return jax.ShapeDtypeStruct(dims, dtype)


def send_parts(value, at, near_ref, far_ref, own_ref):
    rows = value.shape[0]

    @pl.when(at == 0)
    def _():
        own_ref[...] = value

    @pl.when(at == 1)
    def _():
        near_ref[rows:, :] = value.astype(BF16)

    @pl.when(at == 2)
    def _():
        far_ref[...] = value

    @pl.when(at == 3)
    def _():
        near_ref[:rows, :] = value.astype(BF16)


def rep_sum(near_send, far_part, gate=None):
    rows = far_part.shape[0]
    near = swapped(near_send, 1)
    far_send = (far_part + near[:rows].astype(F32)).astype(BF16)
    if gate is not None:
        far_send = after(far_send, gate)
    return near, swapped(far_send, 2), far_send


def place_store(target, columns, limit=None):
    def store(start, ref, first, rows):
        target[pl.ds(start, rows), :limit] = ref[first : first + rows, columns]

    return store


def first_prep(place_ref, qkv_ref, small_ref, first_ref, small_rows):
    rep = place_ref[0]
    owned, width = qkv_ref.shape[0], qkv_ref.shape[1] // 3
    part = width // SPAN
    small_rows[...] = jnp.zeros_like(small_rows)
    small_rows[: small_ref.shape[0], : small_ref.shape[1]] = small_ref[...]
    for which in range(3):
        first = which * width
        options = [qkv_ref[:, first + r * part : first + (r + 1) * part] for r in range(SPAN)]
        first_ref[:, which * part : (which + 1) * part] = chosen(options, rep).astype(BF16)
    first_ref[:, 3 * part :] = small_rows[...].T[:owned, :64].astype(BF16)


def second_prep(place_ref, out_ref, up_ref, down_ref, second_ref, third_ref):
    rep = place_ref[0]
    cut = out_ref.shape[1] // 3
    units = third_ref.shape[0]
    second_ref[:, :cut] = out_ref[:, :cut].astype(BF16)
    pieces = []
    for first in range(0, up_ref.shape[1], SPAN * units):
        options = [up_ref[:, first + r * units : first + (r + 1) * units] for r in range(SPAN)]
        pieces.append(chosen(options, rep))
    second_ref[:, cut:] = jnp.concatenate(pieces, axis=1).astype(BF16)
    third_ref[:, : 2 * cut] = out_ref[:, cut:].astype(BF16)
    start = pl.multiple_of(rep * units, units)
    third_ref[:, 2 * cut :] = down_ref[pl.ds(start, units), :].astype(BF16)


def prep_kernel(
    place_ref,
    qkv_ref,
    small_ref,
    out_ref,
    up_ref,
    down_ref,
    first_ref,
    second_ref,
    third_ref,
    small_rows,
):
    first_prep(place_ref, qkv_ref, small_ref, first_ref, small_rows)
    second_prep(place_ref, out_ref, up_ref, down_ref, second_ref, third_ref)


def first_kernel(pieces, *refs):
    place_ref, refs = refs[0], refs[1:]
    token_refs, refs = refs[:SPAN], refs[SPAN:]
    count = len(pieces.arrays)
    weight_refs, refs = refs[:count], refs[count:]
    (
        all_ref,
        weight_ref,
        small_ref,
        q_ref,
        k_ref,
        v_ref,
        seg_col_ref,
        seg_row_ref,
        out_ref,
        lse_ref,
        small_cols,
    ) = refs
    rep, shard = place_ref[0], place_ref[1]
    total, width = all_ref.shape
    rows = total // SPAN
    part = q_ref.shape[1]
    pieces.place(shard, weight_refs, place_store(weight_ref, slice(0, 3 * part)))
    last = small_cols.shape[1]
    pieces.place(
        shard, weight_refs, place_store(small_cols, slice(3 * part + 64 - last, 3 * part + 64))
    )
    small = small_cols[...].astype(F32).T
    small = small[last - 64 : last - 48, :]
    small_ref[...] = small
    gain, bias = small[0:1, :], small[1:2, :]
    query_bias = chosen([small[2:3, r * part : (r + 1) * part] for r in range(SPAN)], rep)
    value_bias = chosen([small[3:4, r * part : (r + 1) * part] for r in range(SPAN)], rep)
    for at in range(SPAN):
        start = pl.multiple_of((rep ^ at) * rows, rows)
        block = token_refs[at][:rows, :]
        all_ref[pl.ds(start, rows), :] = block
        hidden = (norm_parts(block.astype(F32))[0] * gain + bias).astype(BF16)
        segs = token_refs[at][rows : rows + 16, :rows].astype(F32)
        seg_row_ref[:, pl.ds(start, rows)] = segs[:8, :]
        seg_col_ref[pl.ds(start, rows), 0:16] = segs.T
        projected = dot(hidden, weight_ref[...])
        q_ref[pl.ds(start, rows), :] = (
            (projected[:, :part] + query_bias) * HEAD_DIM ** (-0.5)
        ).astype(BF16)
        k_ref[pl.ds(start, rows), :] = projected[:, part : 2 * part].astype(BF16)
        v_ref[pl.ds(start, rows), :] = (projected[:, 2 * part :] + value_bias).astype(BF16)
    attend(q_ref, k_ref, v_ref, seg_col_ref, seg_row_ref, out_ref, lse_ref)


def second_kernel(pieces, place_ref, *refs):
    attended_refs, refs = refs[:SPAN], refs[SPAN:]
    cot_refs, refs = refs[:SPAN], refs[SPAN:]
    count = len(pieces.arrays)
    piece_refs, refs = refs[:count], refs[count:]
    (
        wide_ref,
        all_ref,
        small_ref,
        up_bias_ref,
        out_own_ref,
        hidden_ref,
        act_ref,
        pre_ref,
        residual_ref,
        near_ref,
        far_ref,
        own_ref,
        up_weight,
        out_weight,
        cot_ref,
    ) = refs
    rep = place_ref[0]
    total, width = all_ref.shape
    rows = total // SPAN
    part = attended_refs[0].shape[1]
    cut = width // 3
    pieces.place(place_ref[1], piece_refs, place_store(up_weight, slice(cut, None)))
    pieces.place(place_ref[1], piece_refs, place_store(out_weight, slice(0, cut), cut))
    out_weight[:, cut:] = wide_ref[:, : 2 * cut]
    own_rows = pl.ds(pl.multiple_of(rep * part, part), part)
    out_own_ref[...] = out_weight[own_rows, :]
    for at in range(SPAN):
        cot_ref[pl.ds(pl.multiple_of((rep ^ at) * rows, rows), rows), :] = cot_refs[at][...]
    out_bias, gain, bias = small_ref[4:5, :], small_ref[5:6, :], small_ref[6:7, :]

    def one_block(index):
        block = slice(index * rows, (index + 1) * rows)
        mixed = out_bias
        for at in range(SPAN):
            from_rows = pl.ds(pl.multiple_of((rep ^ at) * part, part), part)
            mixed = mixed + dot(attended_refs[at][block, :], out_weight[from_rows, :])
        residual = all_ref[block, :].astype(F32) + mixed

        @pl.when(index == rep)
        def _():
            residual_ref[...] = residual

        hidden = (norm_parts(residual)[0] * gain + bias).astype(BF16)
        hidden_ref[block, :] = hidden
        pre_act = dot(hidden, up_weight[...]) + up_bias_ref[...]
        cdf = 0.5 * (1.0 + lax.erf(pre_act * (0.5**0.5)))
        act_ref[block, :] = (pre_act * cdf).astype(BF16)
        slope = cdf + pre_act * (jnp.exp(-0.5 * pre_act * pre_act) * 0.3989422804014327)
        pre_low = (contract_cols(cot_ref[block, :], wide_ref[:, 2 * cut :]) * slope).astype(BF16)
        pre_ref[block, :] = pre_low
        grad = contract_cols(pre_low, up_weight[...])
        send_parts(grad, index ^ rep, near_ref, far_ref, own_ref)

    for index in range(SPAN):
        one_block(index)


def down_grad_kernel(place_ref, act_ref, cot_a, cot_b, cot_c, cot_d, *refs):
    grad_refs, (grad_ref, cot_ref) = refs[:-2], refs[-2:]
    rows = cot_a.shape[0]
    for at, ref in enumerate((cot_a, cot_b, cot_c, cot_d)):
        start = pl.multiple_of((place_ref[0] ^ at) * rows, rows)
        cot_ref[pl.ds(start, rows), :] = ref[...]
    units = act_ref.shape[1]
    step = units // 3
    for first in range(0, units, step):
        grad_ref[first : first + step, :] = contract_rows(
            act_ref[:, first : first + step], cot_ref[...]
        ).astype(BF16)
    if len(grad_refs) == 2:
        split_halves(place_ref, grad_ref, *grad_refs)
    else:
        grad_refs[0][...] = grad_ref[...]


def third_kernel(place_ref, act_ref, hidden_ref, pre_ref, wide_ref, *refs):
    grad_refs, (near_ref, far_ref, own_ref, sum_ref, grad_ref) = refs[:-5], refs[-5:]
    rep = place_ref[0]
    total, width = hidden_ref.shape
    rows = total // SPAN
    step = width // 3
    for first in range(0, width, step):
        grad_ref[first : first + step, :] = contract_rows(
            hidden_ref[:, first : first + step], pre_ref[...]
        ).astype(BF16)
    sum_ref[...] = jnp.broadcast_to(
        jnp.sum(pre_ref[...].astype(F32), axis=0, keepdims=True), sum_ref.shape
    )

    for index in range(SPAN):
        block = slice(index * rows, (index + 1) * rows)
        send_parts(
            dot(act_ref[block, :], wide_ref[:, -width:]), index ^ rep, near_ref, far_ref, own_ref
        )

    if len(grad_refs) == 2:
        split_halves(place_ref, grad_ref, *grad_refs)
    else:
        grad_refs[0][...] = grad_ref[...]


def fourth_kernel(
    place_ref,
    own_ref,
    near_ref,
    far_ref,
    residual_ref,
    cotangent_ref,
    small_ref,
    resid_grad_ref,
    branch_ref,
    sums_ref,
):
    grad = own_ref[...] + near_ref[own_ref.shape[0] :, :].astype(F32) + far_ref[...].astype(F32)
    normalized, inverse = norm_parts(residual_ref[...])
    cotangent = cotangent_ref[...].astype(F32)
    resid_grad = cotangent + norm_back(normalized, inverse, small_ref[5:6, :], grad)
    branch = resid_grad.astype(BF16)
    resid_grad_ref[...] = resid_grad
    branch_ref[...] = branch
    sums_ref[...] = jnp.zeros_like(sums_ref)
    sums_ref[4:5, :] = jnp.sum(branch.astype(F32), axis=0, keepdims=True)
    sums_ref[5:6, :] = jnp.sum(grad * normalized, axis=0, keepdims=True)
    sums_ref[6:7, :] = jnp.sum(grad, axis=0, keepdims=True)
    sums_ref[7:8, :] = jnp.sum(cotangent, axis=0, keepdims=True)


def fifth_kernel(
    place_ref,
    branch_a,
    branch_b,
    branch_c,
    branch_d,
    attended_a,
    attended_b,
    attended_c,
    attended_d,
    out_weight,
    qkv_weight,
    q_ref,
    k_ref,
    v_ref,
    lse_ref,
    seg_col_ref,
    seg_row_ref,
    all_ref,
    small_ref,
    sums_ref,
    unit_sums_ref,
    *refs,
):
    grad_refs, refs = refs[:-11], refs[-11:]
    (
        near_ref,
        far_ref,
        own_ref,
        branch_ref,
        back_ref,
        proj_ref,
        dk_ref,
        dv_ref,
        small_grads,
        grad_ref,
        hidden_ref,
    ) = refs
    rep = place_ref[0]
    total, width = all_ref.shape
    rows = total // SPAN
    part = q_ref.shape[1]
    for at, ref in enumerate((branch_a, branch_b, branch_c, branch_d)):
        start = pl.multiple_of((rep ^ at) * rows, rows)
        branch_ref[pl.ds(start, rows), :] = ref[...]
    back_ref[...] = contract_cols(branch_ref[...], out_weight[...]).astype(BF16)
    attend_back(
        q_ref,
        k_ref,
        v_ref,
        back_ref,
        lse_ref,
        seg_col_ref,
        seg_row_ref,
        proj_ref,
        dk_ref,
        dv_ref,
    )
    gain = small_ref[0:1, :]
    small_grads[...] = jnp.zeros_like(small_grads)
    small_grads[0:8, :] = sums_ref[...]
    small_grads[8:16, :] = unit_sums_ref[...]

    for index in range(SPAN):
        block = slice(index * rows, (index + 1) * rows)
        grad = contract_cols(proj_ref[block, :], qkv_weight[...])
        normalized = norm_parts(all_ref[block, :].astype(F32))[0]
        hidden_ref[block, :] = (normalized * gain + small_ref[1:2, :]).astype(BF16)
        small_grads[0:1, :] += jnp.sum(grad * normalized, axis=0, keepdims=True)
        small_grads[1:2, :] += jnp.sum(grad, axis=0, keepdims=True)
        send_parts(grad, index ^ rep, near_ref, far_ref, own_ref)

    lane = lax.broadcasted_iota(jnp.int32, (1, width), 1)
    mine = (lane >= rep * part) & (lane < (rep + 1) * part)
    for row, first in ((2, 0), (3, 2 * part)):
        column_sum = jnp.sum(
            proj_ref[:, first : first + part].astype(F32), axis=0, keepdims=True
        )
        small_grads[row : row + 1, :] = jnp.where(
            mine, jnp.concatenate([column_sum] * SPAN, axis=1), 0.0
        )
    step = width // 3
    for first in range(0, width, step):
        grad_ref[first : first + step, : 3 * part] = contract_rows(
            hidden_ref[:, first : first + step], proj_ref[...]
        ).astype(BF16)
    branch_part = chosen(
        [branch_ref[:, r * part : (r + 1) * part] for r in range(SPAN)], rep
    )
    for at, ref in enumerate((attended_a, attended_b, attended_c, attended_d)):
        from_rows = pl.ds(pl.multiple_of((rep ^ at) * part, part), part)
        grad_ref[from_rows, 3 * part : 4 * part] = contract_rows(ref[...], branch_part).astype(
            BF16
        )
    grad_ref[:, 4 * part :] = small_grads[...].T.astype(BF16)
    if len(grad_refs) == 2:
        split_halves(place_ref, grad_ref, *grad_refs)
    else:
        grad_refs[0][...] = grad_ref[...]


def sixth_kernel(
    place_ref, own_ref, near_ref, far_ref, tokens_ref, resid_grad_ref, small_ref, out_ref
):
    grad = own_ref[...] + near_ref[own_ref.shape[0] :, :].astype(F32) + far_ref[...].astype(F32)
    normalized, inverse = norm_parts(tokens_ref[...].astype(F32))
    out_ref[...] = resid_grad_ref[...] + norm_back(normalized, inverse, small_ref[0:1, :], grad)


def rep_order(refs, rep):
    blocks = [ref[...].astype(F32) for ref in refs]
    odd, high = (rep & 1) == 1, (rep & 2) == 2
    pairs = []
    for first in (0, 2):
        lower, upper = blocks[first], blocks[first + 1]
        pairs.append((jnp.where(odd, upper, lower), jnp.where(odd, lower, upper)))
    low = [jnp.where(high, b, a) for a, b in zip(*pairs)]
    return low + [jnp.where(high, a, b) for a, b in zip(*pairs)]


def adam_kernel(place_ref, *refs):
    blocks = rep_order(refs[:SPAN], place_ref[0])
    small_refs, refs = refs[SPAN : 2 * SPAN], refs[2 * SPAN :]
    ins, outs = refs[:9], refs[9:]
    part = ins[3].shape[1] // SPAN
    qkv = [b[:, c * part : (c + 1) * part] for c in range(3) for b in blocks]
    out = [b[:, 3 * part : 4 * part] for b in blocks]

    def update(at, gradient, rate):
        weight, first, second = (ref[...] for ref in ins[3 * at : 3 * at + 3])
        results = adam_update(weight, gradient, first, second, rate)
        for ref, value in zip(outs[3 * at : 3 * at + 3], results):
            ref[...] = value

    update(0, jnp.concatenate(qkv, axis=1), RATE_MATRIX)
    update(1, jnp.concatenate(out, axis=1), RATE_MATRIX)

    @pl.when(pl.program_id(0) == 0)
    def _():
        small = small_refs[0][...].astype(F32)
        for ref in small_refs[1:]:
            small = small + ref[...].astype(F32)
        update(2, small.T[: ins[6].shape[0], :], RATE_SMALL)


def last_adam(place, blocks, arrays):
    steps = 3
    rows, columns = arrays[0].shape
    width = arrays[3].shape[1]

    def row_block(count):
        return pl.BlockSpec((rows // steps, count), lambda i: (i, 0))

    whole = pl.BlockSpec(arrays[6].shape, lambda i: (0, 0))
    specs = [row_block(columns)] * 3 + [row_block(width)] * 3 + [whole] * 3
    small = pl.BlockSpec((rows, 128), lambda i: (0, width // 128))
    return pl.pallas_call(
        adam_kernel,
        grid=(steps,),
        out_shape=[shape(*a.shape, dtype=F32) for a in arrays],
        in_specs=[pl.BlockSpec(memory_space=pltpu.SMEM)]
        + [row_block(width)] * SPAN
        + [small] * SPAN
        + specs,
        out_specs=specs,
        compiler_params=pltpu.CompilerParams(vmem_limit_bytes=16 * 2**20),
    )(place, *blocks, *blocks, *arrays)


def up_adam_kernel(place_ref, *refs):
    blocks = rep_order(refs[:SPAN], place_ref[0])
    weight, first, second, *outs = refs[SPAN:]
    width = weight.shape[1] // SPAN
    units = width // FEW
    pieces = [b[:, at * units : (at + 1) * units] for at in range(FEW) for b in blocks]
    results = adam_update(
        weight[...], jnp.concatenate(pieces, axis=1), first[...], second[...], RATE_MATRIX
    )
    for ref, value in zip(outs, results):
        ref[...] = value


def down_adam_kernel(place_ref, *refs):
    at = pl.program_id(0) ^ place_ref[0]
    gradient = chosen([ref[...] for ref in refs[:SPAN]], at).astype(F32)
    weight, first, second, *outs = refs[SPAN:]
    results = adam_update(weight[...], gradient, first[...], second[...], RATE_MATRIX)
    for ref, value in zip(outs, results):
        ref[...] = value


def grid_adam(kernel, steps, place, blocks, block_spec, arrays):
    rows, columns = arrays[0].shape
    spec = pl.BlockSpec((rows // steps, columns), lambda i: (i, 0))
    return list(pl.pallas_call(
        kernel,
        grid=(steps,),
        out_shape=[shape(rows, columns, dtype=F32)] * 3,
        in_specs=[pl.BlockSpec(memory_space=pltpu.SMEM)]
        + [block_spec] * SPAN
        + [spec] * 3,
        out_specs=[spec] * 3,
        compiler_params=pltpu.CompilerParams(vmem_limit_bytes=16 * 2**20),
        cost_estimate=pl.CostEstimate(
            flops=0, bytes_accessed=0, transcendentals=0
        ),
    )(place, *blocks, *arrays))


def in_order(blocks, rep):
    odd = (rep & 1) == 1
    high = (rep & 2) == 2
    low_pair = (jnp.where(odd, blocks[1], blocks[0]), jnp.where(odd, blocks[0], blocks[1]))
    high_pair = (jnp.where(odd, blocks[3], blocks[2]), jnp.where(odd, blocks[2], blocks[3]))
    return (
        jnp.where(high, high_pair[0], low_pair[0]),
        jnp.where(high, high_pair[1], low_pair[1]),
        jnp.where(high, low_pair[0], high_pair[0]),
        jnp.where(high, low_pair[1], high_pair[1]),
    )


def local(
    tokens,
    cotangent,
    segments,
    qkv_weight,
    out_weight,
    up_weight,
    down_weight,
    small_weights,
    qkv_first,
    out_first,
    up_first,
    down_first,
    small_first,
    qkv_second,
    out_second,
    up_second,
    down_second,
    small_second,
):
    rep = lax.axis_index("rep")
    shards = lax.axis_size("shard")
    place = jnp.stack([rep, lax.axis_index("shard")]).astype(jnp.int32)
    rows, width = tokens.shape
    total = SPAN * rows
    part = width // SPAN
    owned = qkv_weight.shape[0]
    ff = up_weight.shape[1]
    ff_part = ff // SPAN
    units = down_weight.shape[0] // SPAN

    def rep_part(block, size, axis):
        return lax.dynamic_slice_in_dim(block, rep * size, size, axis)

    few = shards == FEW
    third = width // 3
    if few:
        first_send, second_send, third_send = call(
            prep_kernel,
            [
                shape(owned, 3 * part + 64),
                shape(owned, third + ff_part),
                shape(units, 2 * third + width),
            ],
            [pltpu.VMEM((128, 128), F32)],
            owned * width,
            56,
            place,
            qkv_weight,
            small_weights,
            out_weight,
            up_weight,
            down_weight,
        )
    else:
        low_small = small_weights.astype(BF16).T
        low_qkv = rep_part(qkv_weight.astype(BF16).reshape(owned, 3, SPAN, part), 1, 2)
        low_qkv = low_qkv.reshape(owned, 3 * part)
        pad = 64 - low_small.shape[1]
        first_send = jnp.concatenate([low_qkv, jnp.pad(low_small, ((0, 0), (0, pad)))], axis=1)
        low_up = rep_part(up_weight.astype(BF16).reshape(owned, shards, SPAN, units), 1, 2)
        low_down = rep_part(down_weight, units, 0).astype(BF16)
        low_out = out_weight.astype(BF16)
        second_send = jnp.concatenate([low_out[:, :third], low_up.reshape(owned, -1)], axis=1)
        third_send = jnp.concatenate([low_out[:, third:], low_down], axis=1)
    third_full = lax.all_gather(third_send, "shard", axis=0, tiled=True)
    first_pieces, second_pieces = shard_gather(first_send, second_send)

    seg_block = jnp.pad(segments.astype(BF16)[None, :], ((0, 15), (0, width - rows)))
    with_seg = jnp.concatenate([tokens, seg_block], axis=0)
    token_blocks = rep_blocks(with_seg)
    cot_blocks = rep_blocks(after(cotangent, token_blocks[2]))

    (
        all_tokens,
        qkv_part,
        small,
        queries,
        keys,
        values,
        seg_col,
        seg_row,
        attended,
        log_total,
    ) = call(
        lambda *refs: first_kernel(first_pieces, *refs),
        [
            shape(total, width),
            shape(width, 3 * part),
            shape(16, width, dtype=F32),
            shape(total, part),
            shape(total, part),
            shape(total, part),
            shape(total, 128, dtype=F32),
            shape(8, total, dtype=F32),
            shape(total, part),
            shape(8, total, dtype=F32),
        ],
        [pltpu.VMEM((width, 128), BF16)],
        12 * total * width * width + 24 * total * total * part,
        56,
        place,
        *token_blocks,
        *first_pieces.arrays,
    )
    up_bias = rep_part(small[8:12].reshape(shards, SPAN, units), 1, 1).reshape(1, -1)
    attended_blocks = rep_blocks(attended)
    (
        out_own,
        hidden_two,
        act_low,
        pre_low,
        residual,
        near_send,
        far_part,
        own,
    ) = call(
        lambda *refs: second_kernel(second_pieces, *refs),
        [
            shape(part, width),
            shape(total, width),
            shape(total, ff_part),
            shape(total, ff_part),
            shape(rows, width, dtype=F32),
            shape(2 * rows, width),
            shape(rows, width, dtype=F32),
            shape(rows, width, dtype=F32),
        ],
        [
            pltpu.VMEM((width, ff_part), BF16),
            pltpu.VMEM((width, width), BF16),
            pltpu.VMEM((total, width), BF16),
        ],
        32 * total * width * width,
        56,
        place,
        *attended_blocks,
        *cot_blocks,
        *second_pieces.arrays,
        third_full,
        all_tokens,
        small,
        up_bias,
    )
    near, far, far_send = rep_sum(near_send, far_part)
    hidden_two_terms = own, near, far
    down_grad = call(
        down_grad_kernel,
        [shape(ff_part // 2, width)] * 2 * few + [shape(ff_part, width)] * (not few),
        [pltpu.VMEM((ff_part, width), BF16), pltpu.VMEM((total, width), BF16)],
        6 * total * width * width,
        56,
        place,
        after(act_low, far_send),
        *cot_blocks,
    )
    *up_grad, mixed_near, mixed_far, mixed_own, unit_sums = call(
        third_kernel,
        [shape(width // 2, ff_part)] * 2 * few
        + [shape(width, ff_part)] * (not few)
        + [
            shape(2 * rows, width),
            shape(rows, width, dtype=F32),
            shape(rows, width, dtype=F32),
            shape(8, ff_part, dtype=F32),
        ],
        [pltpu.VMEM((width, ff_part), BF16)],
        12 * total * width * width,
        56,
        place,
        after(act_low, down_grad[0]),
        hidden_two,
        pre_low,
        third_full,
    )
    if few:
        down_received = swap_shard(down_grad[1], 1)
    near, unit_sums = lax.optimization_barrier((near, unit_sums))
    hidden_two_terms = own, near, far
    resid_grad, branch, sums = call(
        fourth_kernel,
        [
            shape(rows, width, dtype=F32),
            shape(rows, width),
            shape(8, width, dtype=F32),
        ],
        [],
        10 * rows * width,
        56,
        place,
        *hidden_two_terms,
        residual,
        cotangent,
        small,
    )
    branch_blocks = rep_blocks(branch, None, down_received if few else None)
    if few:
        down_own, down_received = scatter_high(place, after(down_grad[0], branch), down_received)
        branch_blocks = (after(branch, down_own),) + branch_blocks[1:]
        up_received = swap_shard(up_grad[1], 1)
    unit_rows = lax.dynamic_update_slice(
        jnp.zeros((shards, SPAN, units), F32), unit_sums[0].reshape(shards, 1, units), (0, rep, 0)
    ).reshape(ff // width, width)
    unit_rows = jnp.pad(unit_rows, ((0, 8 - ff // width), (0, 0)))
    *last_grad, near_send, far_part, own = call(
        fifth_kernel,
        [shape(width // 2, 4 * part + 128)] * 2 * few
        + [shape(width, 4 * part + 128)] * (not few)
        + [
            shape(2 * rows, width),
            shape(rows, width, dtype=F32),
            shape(rows, width, dtype=F32),
        ],
        [
            pltpu.VMEM((total, width), BF16),
            pltpu.VMEM((total, part), BF16),
            pltpu.VMEM((total, 3 * part), BF16),
            pltpu.VMEM((total, part), F32),
            pltpu.VMEM((total, part), F32),
            pltpu.VMEM((128, width), F32),
            pltpu.VMEM((width, 4 * part + 128), BF16),
            pltpu.VMEM((total, width), BF16),
        ],
        12 * total * width * width + 72 * total * total * part,
        56,
        place,
        *branch_blocks,
        *attended_blocks,
        out_own,
        qkv_part,
        queries,
        keys,
        values,
        log_total,
        seg_col,
        seg_row,
        all_tokens,
        small,
        sums,
        unit_rows,
    )
    if few:
        last_kept, last_sent = last_grad
        last_sent, near_send, down_received, up_received = lax.optimization_barrier(
            (last_sent, near_send, down_received, up_received)
        )
    near, far, _ = rep_sum(near_send, far_part)
    near_mixed, far_mixed, _ = rep_sum(mixed_near, mixed_far, far)
    if few:
        last_kept, far = lax.optimization_barrier((last_kept, far))
        last_own, last_received = scatter_middle(place, last_kept, last_sent)
        far_mixed = after(far_mixed, last_own)
        up_own, up_received = scatter_high(
            place, after(up_grad[0], (last_grad[0], down_received)), up_received
        )
        down_own, up_received = after((down_own, up_received), last_own)
        wide_total = jnp.concatenate(
            [scatter_end(down_own, down_received), scatter_end(up_own, up_received)], axis=1
        )
        wide_blocks = rep_blocks(wide_total, last_received)
    else:
        last_total, down_total, up_total = (
            lax.psum_scatter(grad, "shard", scatter_dimension=0, tiled=True)
            for grad in (last_grad[0], down_grad[0], up_grad[0])
        )
    mixed = residual + (
        mixed_own + near_mixed[rows:].astype(F32) + far_mixed.astype(F32) + small[7]
    )
    mixed = mixed.astype(BF16)
    input_grad = call(
        sixth_kernel,
        [shape(rows, width, dtype=F32)],
        [],
        10 * rows * width,
        56,
        place,
        own,
        near,
        far,
        tokens,
        resid_grad,
        small,
    )[0]
    if few:
        up_res = grid_adam(
            up_adam_kernel,
            3,
            place,
            wide_blocks,
            pl.BlockSpec((owned // 3, width), lambda i: (i, 1)),
            (up_weight, up_first, up_second),
        )
        down_res = grid_adam(
            down_adam_kernel,
            SPAN,
            place,
            wide_blocks,
            pl.BlockSpec((units, width), lambda i: (0, 0)),
            (down_weight, down_first, down_second),
        )
        last_received, input_grad, mixed = lax.optimization_barrier(
            (last_received, input_grad, mixed)
        )
        last_total = scatter_end(last_own, last_received)
        last_blocks = rep_blocks(last_total, (up_res[0], down_res[0]))
        results = last_adam(
            place,
            last_blocks,
            (
                qkv_weight,
                qkv_first,
                qkv_second,
                out_weight,
                out_first,
                out_second,
                small_weights,
                small_first,
                small_second,
            ),
        )
        qkv_res, out_res, small_res = results[:3], results[3:6], results[6:]
    else:
        down_own = jnp.concatenate(in_order(rep_blocks(down_total), rep), axis=0).astype(F32)
        up_own = in_order(rep_blocks(up_total), rep)
        up_own = [g.reshape(owned, shards, units) for g in up_own]
        up_own = jnp.stack(up_own, axis=2).reshape(owned, ff).astype(F32)
        up_res = adam_update(up_weight, up_own, up_first, up_second, RATE_MATRIX)
        down_res = adam_update(down_weight, down_own, down_first, down_second, RATE_MATRIX)
        last_own = in_order(rep_blocks(last_total), rep)
        out_own = jnp.concatenate([g[:, 3 * part : 4 * part] for g in last_own], axis=1)
        qkv_own = [g[:, : 3 * part].reshape(owned, 3, part) for g in last_own]
        qkv_own = jnp.stack(qkv_own, axis=2).reshape(owned, 3 * width).astype(F32)
        small_own = sum(g[:, 4 * part : 4 * part + 12].astype(F32) for g in last_own).T
        qkv_res = adam_update(qkv_weight, qkv_own, qkv_first, qkv_second, RATE_MATRIX)
        out_res = adam_update(
            out_weight, out_own.astype(F32), out_first, out_second, RATE_MATRIX
        )
        small_res = adam_update(
            small_weights, small_own, small_first, small_second, RATE_SMALL
        )
    return (
        mixed,
        input_grad,
        qkv_res[0],
        out_res[0],
        up_res[0],
        down_res[0],
        small_res[0],
        qkv_res[1],
        out_res[1],
        up_res[1],
        down_res[1],
        small_res[1],
        qkv_res[2],
        out_res[2],
        up_res[2],
        down_res[2],
        small_res[2],
    )


def solution(mesh):
    tokens_spec = P(("rep", "shard"), None)
    rows = P("shard", None)
    columns = P(None, "shard")
    weights = (rows, rows, rows, rows, columns)
    return jax.shard_map(
        local,
        mesh=mesh,
        in_specs=(tokens_spec, tokens_spec, P(("rep", "shard"))) + weights * 3,
        out_specs=(tokens_spec, tokens_spec) + weights * 3,
        check_vma=False,
    )
```

```python
import jax
import jax.numpy as jnp
from jax import lax
from jax.experimental import pallas as pl
from jax.experimental.pallas import tpu as pltpu
from jax.sharding import PartitionSpec as P

HEAD_DIM = 64
SPAN = 4
STEP_NUM = 10


NORM_EPS = 1e-05
BETA_ONE = 0.9
BETA_TWO = 0.95
ADAM_EPS = 1e-08
DECAY = 0.1
RATE_MATRIX = 0.05
RATE_SMALL = 0.3
MASKED = -1e30
BLOCK = 256
FEW = 8
F32 = jnp.float32
BF16 = jnp.bfloat16


def swapped(block, bit):
    return lax.ppermute(block, "rep", [(i, i ^ bit) for i in range(SPAN)])


def rep_blocks(block, gate=None, near_gate=None):
    far = swapped(block, 2)
    near = swapped(block if near_gate is None else after(block, near_gate), 1)
    if gate is not None:
        far = after(far, gate)
    return (block, near, far, swapped(far, 1))


def swap_shard(block, bits):
    return lax.ppermute(block, "shard", [(i, i ^ bits) for i in range(lax.axis_size("shard"))])


def after(block, other):
    return lax.optimization_barrier((block, other))[0]


class Pieces:
    def __init__(self, arrays, codes, rows):
        self.arrays, self.codes, self.rows = arrays, codes, rows

    def place(self, shard, refs, store):
        if self.codes is None:
            store(0, refs[0], 0, refs[0].shape[0])
            return
        for ref, codes in zip(refs, self.codes):
            for index, code in enumerate(codes):
                start = pl.multiple_of((shard ^ code) * self.rows, self.rows)
                store(start, ref, index * self.rows, self.rows)


    def swapped_columns(self, count, gate):
        other = swapped(jnp.concatenate([a[:, :count] for a in after(self.arrays, gate)], axis=0), 1)
        codes = None if self.codes is None else [sum(self.codes, [])]
        return Pieces([other], codes, self.rows)


def shard_sends(block, crossed, gate):
    if lax.axis_size("shard") != FEW:
        return [lax.all_gather(block, "shard", axis=0, tiled=True)]
    sent = block if gate is None else after(block, (gate, crossed))
    return [block] + crossed[:1] + [swap_shard(sent, bits) for bits in (2, 4, 6)]


def shard_gather(blocks, gate):
    if len(blocks) == 1:
        return Pieces(blocks, None, blocks[0].shape[0] // lax.axis_size("shard"))
    sent = blocks[2:] if len(blocks) == 5 else blocks
    codes = [[0], [1], [2], [4], [6], [3, 5, 7]]
    if len(blocks) == 4:
        codes = [[0], [2], [4], [6], [1, 3, 5, 7]]
    other = jnp.concatenate(after(sent, gate), axis=0)
    return Pieces(blocks + [swap_shard(other, 1)], codes, blocks[0].shape[0])


def middle_kernel(place_ref, kept_ref, received_ref, own_ref, *sent_refs):
    high = place_ref[1] // 2
    rows = own_ref.shape[0]
    for bits in range(len(sent_refs) + 1):
        block = pl.ds(pl.multiple_of((high ^ bits) * rows, rows), rows)
        value = kept_ref[block, :].astype(F32) + received_ref[block, :].astype(F32)
        if bits == 0:
            own_ref[...] = value
        else:
            sent_refs[bits - 1][...] = value.astype(BF16)


def scatter_middle(place, kept, sent):
    return scatter_high(place, kept, swap_shard(sent, 1))


def scatter_high(place, kept, received):
    count = FEW // 2
    rows, columns = kept.shape[0] // count, kept.shape[1]
    own, *sends = call(
        middle_kernel,
        [shape(rows, columns, dtype=F32)] + [shape(rows, columns)] * (count - 1),
        [],
        kept.size,
        56,
        place,
        kept,
        received,
    )
    return own, [swap_shard(send, 2 * (bits + 1)) for bits, send in enumerate(sends)]


def scatter_end(own, received):
    total = own
    for block in received:
        total = total + block.astype(F32)
    return total.astype(BF16)


def split_halves(place_ref, full_ref, kept_ref, sent_ref):
    low = place_ref[1] & 1
    rows = full_ref.shape[0] // FEW
    for at in range(FEW // 2):
        target = slice(at * rows, (at + 1) * rows)
        for ref, bit in ((kept_ref, low), (sent_ref, 1 - low)):
            start = pl.multiple_of((2 * at + bit) * rows, rows)
            ref[target, :] = full_ref[pl.ds(start, rows), :]


def norm_parts(values):
    center = jnp.mean(values, axis=-1, keepdims=True)
    centered = values - center
    variance = jnp.mean(centered * centered, axis=-1, keepdims=True)
    inverse = lax.rsqrt(variance + NORM_EPS)
    return centered * inverse, inverse


def norm_back(normalized, inverse, gain, grad):
    scaled = grad * gain
    mean_one = jnp.mean(scaled, axis=-1, keepdims=True)
    mean_two = jnp.mean(scaled * normalized, axis=-1, keepdims=True)
    return inverse * (scaled - mean_one - normalized * mean_two)


def contract_rows(left_side, right_side):
    return lax.dot_general(
        left_side, right_side, (((0,), (0,)), ((), ())), preferred_element_type=F32
    )


def contract_cols(left_side, right_side):
    return lax.dot_general(
        left_side, right_side, (((1,), (1,)), ((), ())), preferred_element_type=F32
    )


def adam_update(master, gradient, moment_one, moment_two, step_rate):
    first_new = BETA_ONE * moment_one + (1.0 - BETA_ONE) * gradient
    second_new = BETA_TWO * moment_two + (1.0 - BETA_TWO) * gradient * gradient
    fix_one = 1.0 - BETA_ONE**STEP_NUM
    fix_two = 1.0 - BETA_TWO**STEP_NUM
    step_dir = first_new / fix_one / (jnp.sqrt(second_new / fix_two) + ADAM_EPS)
    return (master - step_rate * (step_dir + DECAY * master), first_new, second_new)


def dot(left_side, right_side):
    return jnp.dot(left_side, right_side, preferred_element_type=F32)


def chosen(values, index):
    result = values[0]
    for at in range(1, len(values)):
        result = jnp.where(index == at, values[at], result)
    return result


def mask_bias(seg_col_ref, seg_row_ref, start, keys):
    same = seg_col_ref[:keys, 0:1] == seg_row_ref[0:1, start : start + BLOCK]
    key_at = lax.broadcasted_iota(jnp.int32, (keys, BLOCK), 0)
    query_at = lax.broadcasted_iota(jnp.int32, (keys, BLOCK), 1) + start
    return jnp.where(same & (key_at <= query_at), 0.0, MASKED)


def head_lanes(shape, head):
    lane = lax.broadcasted_iota(jnp.int32, shape, 1)
    return (lane >= head * HEAD_DIM) & (lane < (head + 1) * HEAD_DIM)


def attend(q_ref, k_ref, v_ref, seg_col_ref, seg_row_ref, out_ref, lse_ref):
    total, width = q_ref.shape
    heads = width // HEAD_DIM
    value_t = v_ref[...].T
    lse_ref[...] = jnp.zeros_like(lse_ref)
    for start in range(0, total, BLOCK):
        keys = start + BLOCK
        bias = mask_bias(seg_col_ref, seg_row_ref, start, keys)
        query = q_ref[start : start + BLOCK, :]
        pieces = []
        for head in range(heads):
            masked = jnp.where(head_lanes(query.shape, head), query, 0)
            scores = contract_cols(k_ref[:keys, :], masked) + bias
            peak = jnp.max(scores, axis=0, keepdims=True)
            exponent = jnp.exp(scores - peak)
            row_total = jnp.sum(exponent, axis=0, keepdims=True)
            mixed = dot(
                value_t[head * HEAD_DIM : (head + 1) * HEAD_DIM, :keys], exponent.astype(BF16)
            )
            pieces.append(mixed / row_total)
            lse_ref[head : head + 1, start : start + BLOCK] = peak + jnp.log(row_total)
        out_ref[start : start + BLOCK, :] = jnp.concatenate(pieces, axis=0).T.astype(BF16)


def attend_back(
    q_ref, k_ref, v_ref, do_ref, lse_ref, seg_col_ref, seg_row_ref, grad_ref, dk_ref, dv_ref
):
    total, width = q_ref.shape
    heads = width // HEAD_DIM
    key_t = k_ref[...].T
    dk_ref[...] = jnp.zeros_like(dk_ref)
    dv_ref[...] = jnp.zeros_like(dv_ref)
    for start in range(0, total, BLOCK):
        keys = start + BLOCK
        bias = mask_bias(seg_col_ref, seg_row_ref, start, keys)
        query = q_ref[start : start + BLOCK, :]
        grad = do_ref[start : start + BLOCK, :]
        pieces = []
        dk = dk_ref[:keys, :]
        dv = dv_ref[:keys, :]
        for head in range(heads):
            lanes = head_lanes(query.shape, head)
            query_h = jnp.where(lanes, query, 0)
            grad_h = jnp.where(lanes, grad, 0)
            scores = contract_cols(k_ref[:keys, :], query_h) + bias
            probs = jnp.exp(scores - lse_ref[head : head + 1, start : start + BLOCK])
            prob_grad = contract_cols(v_ref[:keys, :], grad_h)
            inner = jnp.sum(prob_grad * probs, axis=0, keepdims=True)
            score_grad = (probs * (prob_grad - inner)).astype(BF16)
            dv = dv + dot(probs.astype(BF16), grad_h)
            dk = dk + dot(score_grad, query_h)
            pieces.append(
                dot(key_t[head * HEAD_DIM : (head + 1) * HEAD_DIM, :keys], score_grad)
            )
        dk_ref[:keys, :] = dk
        dv_ref[:keys, :] = dv
        dq = jnp.concatenate(pieces, axis=0).T * HEAD_DIM ** (-0.5)
        grad_ref[start : start + BLOCK, :width] = dq.astype(BF16)
    grad_ref[:, width : 2 * width] = dk_ref[...].astype(BF16)
    grad_ref[:, 2 * width :] = dv_ref[...].astype(BF16)


def call(kernel, outs, scratch, flops, limit, *operands):
    sizes = [o.size * o.dtype.itemsize for o in operands] + [
        o.size * jnp.dtype(o.dtype).itemsize for o in outs
    ]
    vmem = pl.BlockSpec(memory_space=pltpu.VMEM)
    return pl.pallas_call(
        kernel,
        out_shape=tuple(outs),
        in_specs=[pl.BlockSpec(memory_space=pltpu.SMEM)] + [vmem] * (len(operands) - 1),
        out_specs=tuple([vmem] * len(outs)),
        scratch_shapes=scratch,
        compiler_params=pltpu.CompilerParams(vmem_limit_bytes=limit * 2**20),
        cost_estimate=pl.CostEstimate(
            flops=flops, bytes_accessed=sum(sizes), transcendentals=0
        ),
    )(*operands)


def shape(*dims, dtype=BF16):
    return jax.ShapeDtypeStruct(dims, dtype)


def send_parts(value, at, near_ref, far_ref, own_ref):
    rows = value.shape[0]

    @pl.when(at == 0)
    def _():
        own_ref[...] = value

    @pl.when(at == 1)
    def _():
        near_ref[rows:, :] = value.astype(BF16)

    @pl.when(at == 2)
    def _():
        far_ref[...] = value

    @pl.when(at == 3)
    def _():
        near_ref[:rows, :] = value.astype(BF16)


def rep_sum(near_send, far_part, gate=None):
    rows = far_part.shape[0]
    near = swapped(near_send, 1)
    far_send = (far_part + near[:rows].astype(F32)).astype(BF16)
    if gate is not None:
        far_send = after(far_send, gate)
    return near, swapped(far_send, 2), far_send


def place_store(target, columns, target_columns=slice(None)):
    def store(start, ref, first, rows):
        target[pl.ds(start, rows), target_columns] = ref[first : first + rows, columns]

    return store


def first_prep(place_ref, qkv_ref, small_ref, first_ref, small_rows):
    rep = place_ref[0]
    owned, width = qkv_ref.shape[0], qkv_ref.shape[1] // 3
    part = width // SPAN
    small_rows[...] = jnp.zeros_like(small_rows)
    small_rows[: small_ref.shape[0], : small_ref.shape[1]] = small_ref[...]
    for which in range(3):
        first = which * width
        options = [qkv_ref[:, first + r * part : first + (r + 1) * part] for r in range(SPAN)]
        first_ref[:, which * part : (which + 1) * part] = chosen(options, rep).astype(BF16)
    first_ref[:, 3 * part :] = small_rows[...].T[:owned, :64].astype(BF16)


def second_prep(place_ref, out_ref, up_ref, down_ref, second_ref, third_ref):
    rep = place_ref[0]
    half = out_ref.shape[1] // 2
    units = third_ref.shape[0]
    second_ref[:, :half] = chosen([out_ref[:, :half], out_ref[:, half:]], rep & 1).astype(BF16)
    pieces = []
    for first in range(0, up_ref.shape[1], SPAN * units):
        options = [up_ref[:, first + r * units : first + (r + 1) * units] for r in range(SPAN)]
        pieces.append(chosen(options, rep))
    second_ref[:, half:] = jnp.concatenate(pieces, axis=1).astype(BF16)
    start = pl.multiple_of(rep * units, units)
    third_ref[...] = down_ref[pl.ds(start, units), :].astype(BF16)


def prep_kernel(
    place_ref,
    qkv_ref,
    small_ref,
    out_ref,
    up_ref,
    down_ref,
    first_ref,
    second_ref,
    third_ref,
    small_rows,
):
    first_prep(place_ref, qkv_ref, small_ref, first_ref, small_rows)
    second_prep(place_ref, out_ref, up_ref, down_ref, second_ref, third_ref)


def first_kernel(pieces, *refs):
    place_ref, refs = refs[0], refs[1:]
    token_refs, refs = refs[:SPAN], refs[SPAN:]
    count = len(pieces.arrays)
    weight_refs, refs = refs[:count], refs[count:]
    (
        all_ref,
        weight_ref,
        small_ref,
        q_ref,
        k_ref,
        v_ref,
        seg_col_ref,
        seg_row_ref,
        out_ref,
        lse_ref,
        small_cols,
    ) = refs
    rep, shard = place_ref[0], place_ref[1]
    total, width = all_ref.shape
    rows = total // SPAN
    part = q_ref.shape[1]
    pieces.place(shard, weight_refs, place_store(weight_ref, slice(0, 3 * part)))
    last = small_cols.shape[1]
    pieces.place(
        shard, weight_refs, place_store(small_cols, slice(3 * part + 64 - last, 3 * part + 64))
    )
    small = small_cols[...].astype(F32).T
    small = small[last - 64 : last - 48, :]
    small_ref[...] = small
    gain, bias = small[0:1, :], small[1:2, :]
    query_bias = chosen([small[2:3, r * part : (r + 1) * part] for r in range(SPAN)], rep)
    value_bias = chosen([small[3:4, r * part : (r + 1) * part] for r in range(SPAN)], rep)
    for at in range(SPAN):
        start = pl.multiple_of((rep ^ at) * rows, rows)
        block = token_refs[at][:rows, :]
        all_ref[pl.ds(start, rows), :] = block
        hidden = (norm_parts(block.astype(F32))[0] * gain + bias).astype(BF16)
        segs = token_refs[at][rows : rows + 16, :rows].astype(F32)
        seg_row_ref[:, pl.ds(start, rows)] = segs[:8, :]
        seg_col_ref[pl.ds(start, rows), 0:16] = segs.T
        projected = dot(hidden, weight_ref[...])
        q_ref[pl.ds(start, rows), :] = (
            (projected[:, :part] + query_bias) * HEAD_DIM ** (-0.5)
        ).astype(BF16)
        k_ref[pl.ds(start, rows), :] = projected[:, part : 2 * part].astype(BF16)
        v_ref[pl.ds(start, rows), :] = (projected[:, 2 * part :] + value_bias).astype(BF16)
    attend(q_ref, k_ref, v_ref, seg_col_ref, seg_row_ref, out_ref, lse_ref)


def second_kernel(pieces, half_pieces, down_pieces, place_ref, *refs):
    attended_refs, refs = refs[:SPAN], refs[SPAN:]
    cot_refs, refs = refs[:SPAN], refs[SPAN:]
    count = len(pieces.arrays)
    piece_refs, refs = refs[:count], refs[count:]
    half_refs, refs = refs[:1], refs[1:]
    count = len(down_pieces.arrays)
    down_refs, refs = refs[:count], refs[count:]
    (
        all_ref,
        small_ref,
        up_bias_ref,
        out_own_ref,
        down_weight,
        hidden_ref,
        act_ref,
        pre_ref,
        residual_ref,
        near_ref,
        far_ref,
        own_ref,
        up_weight,
        out_weight,
        cot_ref,
    ) = refs
    rep = place_ref[0]
    total, width = all_ref.shape
    rows = total // SPAN
    part = attended_refs[0].shape[1]
    half = width // 2
    core = rep & 1
    own_half = pl.ds(pl.multiple_of(core * half, half), half)
    other_half = pl.ds(pl.multiple_of((1 - core) * half, half), half)
    shard = place_ref[1]
    pieces.place(shard, piece_refs, place_store(up_weight, slice(half, None)))
    pieces.place(shard, piece_refs, place_store(out_weight, slice(0, half), own_half))
    half_pieces.place(shard, half_refs, place_store(out_weight, slice(None), other_half))
    down_pieces.place(shard, down_refs, place_store(down_weight, slice(None)))
    own_rows = pl.ds(pl.multiple_of(rep * part, part), part)
    out_own_ref[...] = out_weight[own_rows, :]
    for at in range(SPAN):
        cot_ref[pl.ds(pl.multiple_of((rep ^ at) * rows, rows), rows), :] = cot_refs[at][...]
    out_bias, gain, bias = small_ref[4:5, :], small_ref[5:6, :], small_ref[6:7, :]

    @pl.loop(0, SPAN)
    def _(index):
        block = pl.ds(pl.multiple_of(index * rows, rows), rows)
        mixed = out_bias
        for at in range(SPAN):
            from_rows = pl.ds(pl.multiple_of((rep ^ at) * part, part), part)
            mixed = mixed + dot(attended_refs[at][block, :], out_weight[from_rows, :])
        residual = all_ref[block, :].astype(F32) + mixed

        @pl.when(index == rep)
        def _():
            residual_ref[...] = residual

        hidden = (norm_parts(residual)[0] * gain + bias).astype(BF16)
        hidden_ref[block, :] = hidden
        pre_act = dot(hidden, up_weight[...]) + up_bias_ref[...]
        cdf = 0.5 * (1.0 + lax.erf(pre_act * (0.5**0.5)))
        act_ref[block, :] = (pre_act * cdf).astype(BF16)
        slope = cdf + pre_act * (jnp.exp(-0.5 * pre_act * pre_act) * 0.3989422804014327)
        pre_low = (contract_cols(cot_ref[block, :], down_weight[...]) * slope).astype(BF16)
        pre_ref[block, :] = pre_low
        grad = contract_cols(pre_low, up_weight[...])
        send_parts(grad, index ^ rep, near_ref, far_ref, own_ref)

def down_grad_kernel(place_ref, act_ref, cot_a, cot_b, cot_c, cot_d, *refs):
    grad_refs, (grad_ref, cot_ref) = refs[:-2], refs[-2:]
    rows = cot_a.shape[0]
    for at, ref in enumerate((cot_a, cot_b, cot_c, cot_d)):
        start = pl.multiple_of((place_ref[0] ^ at) * rows, rows)
        cot_ref[pl.ds(start, rows), :] = ref[...]
    units = act_ref.shape[1]
    step = units // 3
    for first in range(0, units, step):
        grad_ref[first : first + step, :] = contract_rows(
            act_ref[:, first : first + step], cot_ref[...]
        ).astype(BF16)
    if len(grad_refs) == 2:
        split_halves(place_ref, grad_ref, *grad_refs)
    else:
        grad_refs[0][...] = grad_ref[...]


def third_kernel(place_ref, act_ref, hidden_ref, pre_ref, wide_ref, *refs):
    grad_refs, (near_ref, far_ref, own_ref, sum_ref, grad_ref) = refs[:-5], refs[-5:]
    rep = place_ref[0]
    total, width = hidden_ref.shape
    rows = total // SPAN
    step = width // 3
    for first in range(0, width, step):
        grad_ref[first : first + step, :] = contract_rows(
            hidden_ref[:, first : first + step], pre_ref[...]
        ).astype(BF16)
    sum_ref[...] = jnp.broadcast_to(
        jnp.sum(pre_ref[...].astype(F32), axis=0, keepdims=True), sum_ref.shape
    )

    @pl.loop(0, SPAN)
    def _(index):
        block = pl.ds(pl.multiple_of(index * rows, rows), rows)
        send_parts(
            dot(act_ref[block, :], wide_ref[...]), index ^ rep, near_ref, far_ref, own_ref
        )

    if len(grad_refs) == 2:
        split_halves(place_ref, grad_ref, *grad_refs)
    else:
        grad_refs[0][...] = grad_ref[...]


def fourth_kernel(
    place_ref,
    own_ref,
    near_ref,
    far_ref,
    residual_ref,
    cotangent_ref,
    small_ref,
    resid_grad_ref,
    branch_ref,
    sums_ref,
):
    grad = own_ref[...] + near_ref[own_ref.shape[0] :, :].astype(F32) + far_ref[...].astype(F32)
    normalized, inverse = norm_parts(residual_ref[...])
    cotangent = cotangent_ref[...].astype(F32)
    resid_grad = cotangent + norm_back(normalized, inverse, small_ref[5:6, :], grad)
    branch = resid_grad.astype(BF16)
    resid_grad_ref[...] = resid_grad
    branch_ref[...] = branch
    sums_ref[...] = jnp.zeros_like(sums_ref)
    sums_ref[4:5, :] = jnp.sum(branch.astype(F32), axis=0, keepdims=True)
    sums_ref[5:6, :] = jnp.sum(grad * normalized, axis=0, keepdims=True)
    sums_ref[6:7, :] = jnp.sum(grad, axis=0, keepdims=True)
    sums_ref[7:8, :] = jnp.sum(cotangent, axis=0, keepdims=True)


def fifth_kernel(
    place_ref,
    branch_a,
    branch_b,
    branch_c,
    branch_d,
    attended_a,
    attended_b,
    attended_c,
    attended_d,
    out_weight,
    qkv_weight,
    q_ref,
    k_ref,
    v_ref,
    lse_ref,
    seg_col_ref,
    seg_row_ref,
    all_ref,
    small_ref,
    sums_ref,
    unit_sums_ref,
    *refs,
):
    grad_refs, refs = refs[:-11], refs[-11:]
    (
        near_ref,
        far_ref,
        own_ref,
        branch_ref,
        back_ref,
        proj_ref,
        dk_ref,
        dv_ref,
        small_grads,
        grad_ref,
        hidden_ref,
    ) = refs
    rep = place_ref[0]
    total, width = all_ref.shape
    rows = total // SPAN
    part = q_ref.shape[1]
    for at, ref in enumerate((branch_a, branch_b, branch_c, branch_d)):
        start = pl.multiple_of((rep ^ at) * rows, rows)
        branch_ref[pl.ds(start, rows), :] = ref[...]
    back_ref[...] = contract_cols(branch_ref[...], out_weight[...]).astype(BF16)
    attend_back(
        q_ref,
        k_ref,
        v_ref,
        back_ref,
        lse_ref,
        seg_col_ref,
        seg_row_ref,
        proj_ref,
        dk_ref,
        dv_ref,
    )
    gain = small_ref[0:1, :]
    small_grads[...] = jnp.zeros_like(small_grads)
    small_grads[0:8, :] = sums_ref[...]
    small_grads[8:16, :] = unit_sums_ref[...]

    @pl.loop(0, SPAN)
    def _(index):
        block = pl.ds(pl.multiple_of(index * rows, rows), rows)
        grad = contract_cols(proj_ref[block, :], qkv_weight[...])
        normalized = norm_parts(all_ref[block, :].astype(F32))[0]
        hidden_ref[block, :] = (normalized * gain + small_ref[1:2, :]).astype(BF16)
        small_grads[0:1, :] += jnp.sum(grad * normalized, axis=0, keepdims=True)
        small_grads[1:2, :] += jnp.sum(grad, axis=0, keepdims=True)
        send_parts(grad, index ^ rep, near_ref, far_ref, own_ref)

    lane = lax.broadcasted_iota(jnp.int32, (1, width), 1)
    mine = (lane >= rep * part) & (lane < (rep + 1) * part)
    for row, first in ((2, 0), (3, 2 * part)):
        column_sum = jnp.sum(
            proj_ref[:, first : first + part].astype(F32), axis=0, keepdims=True
        )
        small_grads[row : row + 1, :] = jnp.where(
            mine, jnp.concatenate([column_sum] * SPAN, axis=1), 0.0
        )
    step = width // 3
    for first in range(0, width, step):
        grad_ref[first : first + step, : 3 * part] = contract_rows(
            hidden_ref[:, first : first + step], proj_ref[...]
        ).astype(BF16)
    branch_part = chosen(
        [branch_ref[:, r * part : (r + 1) * part] for r in range(SPAN)], rep
    )
    for at, ref in enumerate((attended_a, attended_b, attended_c, attended_d)):
        from_rows = pl.ds(pl.multiple_of((rep ^ at) * part, part), part)
        grad_ref[from_rows, 3 * part : 4 * part] = contract_rows(ref[...], branch_part).astype(
            BF16
        )
    grad_ref[:, 4 * part :] = small_grads[...].T.astype(BF16)
    if len(grad_refs) == 2:
        split_halves(place_ref, grad_ref, *grad_refs)
    else:
        grad_refs[0][...] = grad_ref[...]


def sixth_kernel(
    place_ref, own_ref, near_ref, far_ref, tokens_ref, resid_grad_ref, small_ref, out_ref
):
    grad = own_ref[...] + near_ref[own_ref.shape[0] :, :].astype(F32) + far_ref[...].astype(F32)
    normalized, inverse = norm_parts(tokens_ref[...].astype(F32))
    out_ref[...] = resid_grad_ref[...] + norm_back(normalized, inverse, small_ref[0:1, :], grad)


def rep_order(refs, rep):
    blocks = [ref[...].astype(F32) for ref in refs]
    odd, high = (rep & 1) == 1, (rep & 2) == 2
    pairs = []
    for first in (0, 2):
        lower, upper = blocks[first], blocks[first + 1]
        pairs.append((jnp.where(odd, upper, lower), jnp.where(odd, lower, upper)))
    low = [jnp.where(high, b, a) for a, b in zip(*pairs)]
    return low + [jnp.where(high, a, b) for a, b in zip(*pairs)]


def adam_kernel(place_ref, *refs):
    blocks = rep_order(refs[:SPAN], place_ref[0])
    small_refs, refs = refs[SPAN : 2 * SPAN], refs[2 * SPAN :]
    ins, outs = refs[:9], refs[9:]
    part = ins[3].shape[1] // SPAN
    qkv = [b[:, c * part : (c + 1) * part] for c in range(3) for b in blocks]
    out = [b[:, 3 * part : 4 * part] for b in blocks]

    def update(at, gradient, rate):
        weight, first, second = (ref[...] for ref in ins[3 * at : 3 * at + 3])
        results = adam_update(weight, gradient, first, second, rate)
        for ref, value in zip(outs[3 * at : 3 * at + 3], results):
            ref[...] = value

    update(0, jnp.concatenate(qkv, axis=1), RATE_MATRIX)
    update(1, jnp.concatenate(out, axis=1), RATE_MATRIX)

    @pl.when(pl.program_id(0) == 0)
    def _():
        small = small_refs[0][...].astype(F32)
        for ref in small_refs[1:]:
            small = small + ref[...].astype(F32)
        update(2, small.T[: ins[6].shape[0], :], RATE_SMALL)


def last_adam(place, blocks, arrays):
    steps = 3
    rows, columns = arrays[0].shape
    width = arrays[3].shape[1]

    def row_block(count):
        return pl.BlockSpec((rows // steps, count), lambda i: (i, 0))

    whole = pl.BlockSpec(arrays[6].shape, lambda i: (0, 0))
    specs = [row_block(columns)] * 3 + [row_block(width)] * 3 + [whole] * 3
    small = pl.BlockSpec((rows, 128), lambda i: (0, width // 128))
    return pl.pallas_call(
        adam_kernel,
        grid=(steps,),
        out_shape=[shape(*a.shape, dtype=F32) for a in arrays],
        in_specs=[pl.BlockSpec(memory_space=pltpu.SMEM)]
        + [row_block(width)] * SPAN
        + [small] * SPAN
        + specs,
        out_specs=specs,
        compiler_params=pltpu.CompilerParams(vmem_limit_bytes=16 * 2**20),
    )(place, *blocks, *blocks, *arrays)


def up_adam_kernel(place_ref, *refs):
    blocks = rep_order(refs[:SPAN], place_ref[0])
    weight, first, second, *outs = refs[SPAN:]
    width = weight.shape[1] // SPAN
    units = width // FEW
    pieces = [b[:, at * units : (at + 1) * units] for at in range(FEW) for b in blocks]
    results = adam_update(
        weight[...], jnp.concatenate(pieces, axis=1), first[...], second[...], RATE_MATRIX
    )
    for ref, value in zip(outs, results):
        ref[...] = value


def down_adam_kernel(place_ref, *refs):
    at = pl.program_id(0) ^ place_ref[0]
    gradient = chosen([ref[...] for ref in refs[:SPAN]], at).astype(F32)
    weight, first, second, *outs = refs[SPAN:]
    results = adam_update(weight[...], gradient, first[...], second[...], RATE_MATRIX)
    for ref, value in zip(outs, results):
        ref[...] = value


def grid_adam(kernel, steps, place, blocks, block_spec, arrays):
    rows, columns = arrays[0].shape
    spec = pl.BlockSpec((rows // steps, columns), lambda i: (i, 0))
    return list(pl.pallas_call(
        kernel,
        grid=(steps,),
        out_shape=[shape(rows, columns, dtype=F32)] * 3,
        in_specs=[pl.BlockSpec(memory_space=pltpu.SMEM)]
        + [block_spec] * SPAN
        + [spec] * 3,
        out_specs=[spec] * 3,
        compiler_params=pltpu.CompilerParams(vmem_limit_bytes=16 * 2**20),
        cost_estimate=pl.CostEstimate(
            flops=0, bytes_accessed=0, transcendentals=0
        ),
    )(place, *blocks, *arrays))


def in_order(blocks, rep):
    odd = (rep & 1) == 1
    high = (rep & 2) == 2
    low_pair = (jnp.where(odd, blocks[1], blocks[0]), jnp.where(odd, blocks[0], blocks[1]))
    high_pair = (jnp.where(odd, blocks[3], blocks[2]), jnp.where(odd, blocks[2], blocks[3]))
    return (
        jnp.where(high, high_pair[0], low_pair[0]),
        jnp.where(high, high_pair[1], low_pair[1]),
        jnp.where(high, low_pair[0], high_pair[0]),
        jnp.where(high, low_pair[1], high_pair[1]),
    )


def local(
    tokens,
    cotangent,
    segments,
    qkv_weight,
    out_weight,
    up_weight,
    down_weight,
    small_weights,
    qkv_first,
    out_first,
    up_first,
    down_first,
    small_first,
    qkv_second,
    out_second,
    up_second,
    down_second,
    small_second,
):
    rep = lax.axis_index("rep")
    shards = lax.axis_size("shard")
    place = jnp.stack([rep, lax.axis_index("shard")]).astype(jnp.int32)
    rows, width = tokens.shape
    total = SPAN * rows
    part = width // SPAN
    owned = qkv_weight.shape[0]
    ff = up_weight.shape[1]
    ff_part = ff // SPAN
    units = down_weight.shape[0] // SPAN

    def rep_part(block, size, axis):
        return lax.dynamic_slice_in_dim(block, rep * size, size, axis)

    few = shards == FEW
    half = width // 2
    if few:
        first_send, second_send, third_send = call(
            prep_kernel,
            [
                shape(owned, 3 * part + 64),
                shape(owned, half + ff_part),
                shape(units, width),
            ],
            [pltpu.VMEM((128, 128), F32)],
            owned * width,
            56,
            place,
            qkv_weight,
            small_weights,
            out_weight,
            up_weight,
            down_weight,
        )
    else:
        low_small = small_weights.astype(BF16).T
        low_qkv = rep_part(qkv_weight.astype(BF16).reshape(owned, 3, SPAN, part), 1, 2)
        low_qkv = low_qkv.reshape(owned, 3 * part)
        pad = 64 - low_small.shape[1]
        first_send = jnp.concatenate([low_qkv, jnp.pad(low_small, ((0, 0), (0, pad)))], axis=1)
        low_up = rep_part(up_weight.astype(BF16).reshape(owned, shards, SPAN, units), 1, 2)
        low_down = rep_part(down_weight, units, 0).astype(BF16)
        low_out = lax.dynamic_slice_in_dim(out_weight, (rep & 1) * half, half, 1).astype(BF16)
        second_send = jnp.concatenate([low_out, low_up.reshape(owned, -1)], axis=1)
        third_send = low_down
    crossed = [swap_shard(block, 1) for block in (first_send, second_send)]
    first_blocks = shard_sends(first_send, crossed, None)
    first_pieces = shard_gather(first_blocks, crossed[:2])
    second_blocks = shard_sends(second_send, crossed[1:2], first_blocks[2:])

    seg_block = jnp.pad(segments.astype(BF16)[None, :], ((0, 15), (0, width - rows)))
    with_seg = jnp.concatenate([tokens, seg_block], axis=0)
    token_blocks = rep_blocks(with_seg)
    cot_blocks = rep_blocks(after(cotangent, token_blocks[2]))

    (
        all_tokens,
        qkv_part,
        small,
        queries,
        keys,
        values,
        seg_col,
        seg_row,
        attended,
        log_total,
    ) = call(
        lambda *refs: first_kernel(first_pieces, *refs),
        [
            shape(total, width),
            shape(width, 3 * part),
            shape(16, width, dtype=F32),
            shape(total, part),
            shape(total, part),
            shape(total, part),
            shape(total, 128, dtype=F32),
            shape(8, total, dtype=F32),
            shape(total, part),
            shape(8, total, dtype=F32),
        ],
        [pltpu.VMEM((width, 128), BF16)],
        12 * total * width * width + 24 * total * total * part,
        56,
        place,
        *token_blocks,
        *first_pieces.arrays,
    )
    second_pieces = shard_gather(second_blocks, attended)
    third_blocks = shard_sends(third_send, [], attended)
    up_bias = rep_part(small[8:12].reshape(shards, SPAN, units), 1, 1).reshape(1, -1)
    attended_blocks = rep_blocks(attended)
    third_pieces = shard_gather(third_blocks, attended_blocks[2])
    half_pieces = second_pieces.swapped_columns(half, third_blocks[2:])
    (
        out_own,
        down_full,
        hidden_two,
        act_low,
        pre_low,
        residual,
        near_send,
        far_part,
        own,
    ) = call(
        lambda *refs: second_kernel(second_pieces, half_pieces, third_pieces, *refs),
        [
            shape(part, width),
            shape(ff_part, width),
            shape(total, width),
            shape(total, ff_part),
            shape(total, ff_part),
            shape(rows, width, dtype=F32),
            shape(2 * rows, width),
            shape(rows, width, dtype=F32),
            shape(rows, width, dtype=F32),
        ],
        [
            pltpu.VMEM((width, ff_part), BF16),
            pltpu.VMEM((width, width), BF16),
            pltpu.VMEM((total, width), BF16),
        ],
        32 * total * width * width,
        56,
        place,
        *attended_blocks,
        *cot_blocks,
        *second_pieces.arrays,
        *half_pieces.arrays,
        *third_pieces.arrays,
        all_tokens,
        small,
        up_bias,
    )
    near, far, far_send = rep_sum(near_send, far_part)
    hidden_two_terms = own, near, far
    down_grad = call(
        down_grad_kernel,
        [shape(ff_part // 2, width)] * 2 * few + [shape(ff_part, width)] * (not few),
        [pltpu.VMEM((ff_part, width), BF16), pltpu.VMEM((total, width), BF16)],
        6 * total * width * width,
        56,
        place,
        after(act_low, far_send),
        *cot_blocks,
    )
    *up_grad, mixed_near, mixed_far, mixed_own, unit_sums = call(
        third_kernel,
        [shape(width // 2, ff_part)] * 2 * few
        + [shape(width, ff_part)] * (not few)
        + [
            shape(2 * rows, width),
            shape(rows, width, dtype=F32),
            shape(rows, width, dtype=F32),
            shape(8, ff_part, dtype=F32),
        ],
        [pltpu.VMEM((width, ff_part), BF16)],
        12 * total * width * width,
        56,
        place,
        after(act_low, down_grad[0]),
        hidden_two,
        pre_low,
        down_full,
    )
    if few:
        down_received = swap_shard(down_grad[1], 1)
    near, unit_sums = lax.optimization_barrier((near, unit_sums))
    hidden_two_terms = own, near, far
    resid_grad, branch, sums = call(
        fourth_kernel,
        [
            shape(rows, width, dtype=F32),
            shape(rows, width),
            shape(8, width, dtype=F32),
        ],
        [],
        10 * rows * width,
        56,
        place,
        *hidden_two_terms,
        residual,
        cotangent,
        small,
    )
    branch_blocks = rep_blocks(branch, None, down_received if few else None)
    if few:
        down_own, down_received = scatter_high(place, after(down_grad[0], branch), down_received)
        branch_blocks = (after(branch, down_own),) + branch_blocks[1:]
        up_received = swap_shard(up_grad[1], 1)
    unit_rows = lax.dynamic_update_slice(
        jnp.zeros((shards, SPAN, units), F32), unit_sums[0].reshape(shards, 1, units), (0, rep, 0)
    ).reshape(ff // width, width)
    unit_rows = jnp.pad(unit_rows, ((0, 8 - ff // width), (0, 0)))
    *last_grad, near_send, far_part, own = call(
        fifth_kernel,
        [shape(width // 2, 4 * part + 128)] * 2 * few
        + [shape(width, 4 * part + 128)] * (not few)
        + [
            shape(2 * rows, width),
            shape(rows, width, dtype=F32),
            shape(rows, width, dtype=F32),
        ],
        [
            pltpu.VMEM((total, width), BF16),
            pltpu.VMEM((total, part), BF16),
            pltpu.VMEM((total, 3 * part), BF16),
            pltpu.VMEM((total, part), F32),
            pltpu.VMEM((total, part), F32),
            pltpu.VMEM((128, width), F32),
            pltpu.VMEM((width, 4 * part + 128), BF16),
            pltpu.VMEM((total, width), BF16),
        ],
        12 * total * width * width + 72 * total * total * part,
        56,
        place,
        *branch_blocks,
        *attended_blocks,
        out_own,
        qkv_part,
        queries,
        keys,
        values,
        log_total,
        seg_col,
        seg_row,
        all_tokens,
        small,
        sums,
        unit_rows,
    )
    if few:
        last_kept, last_sent = last_grad
        last_sent, near_send, down_received, up_received = lax.optimization_barrier(
            (last_sent, near_send, down_received, up_received)
        )
    near, far, _ = rep_sum(near_send, far_part)
    near_mixed, far_mixed, _ = rep_sum(mixed_near, mixed_far, far)
    if few:
        last_kept, far = lax.optimization_barrier((last_kept, far))
        last_own, last_received = scatter_middle(place, last_kept, last_sent)
        far_mixed = after(far_mixed, last_own)
        up_own, up_received = scatter_high(
            place, after(up_grad[0], (last_grad[0], down_received)), up_received
        )
        down_own, up_received = after((down_own, up_received), last_own)
        wide_total = jnp.concatenate(
            [scatter_end(down_own, down_received), scatter_end(up_own, up_received)], axis=1
        )
        wide_blocks = rep_blocks(wide_total, last_received)
    else:
        last_total, down_total, up_total = (
            lax.psum_scatter(grad, "shard", scatter_dimension=0, tiled=True)
            for grad in (last_grad[0], down_grad[0], up_grad[0])
        )
    mixed = residual + (
        mixed_own + near_mixed[rows:].astype(F32) + far_mixed.astype(F32) + small[7]
    )
    mixed = mixed.astype(BF16)
    input_grad = call(
        sixth_kernel,
        [shape(rows, width, dtype=F32)],
        [],
        10 * rows * width,
        56,
        place,
        own,
        near,
        far,
        tokens,
        resid_grad,
        small,
    )[0]
    if few:
        up_res = grid_adam(
            up_adam_kernel,
            3,
            place,
            wide_blocks,
            pl.BlockSpec((owned // 3, width), lambda i: (i, 1)),
            (up_weight, up_first, up_second),
        )
        down_res = grid_adam(
            down_adam_kernel,
            SPAN,
            place,
            wide_blocks,
            pl.BlockSpec((units, width), lambda i: (0, 0)),
            (down_weight, down_first, down_second),
        )
        last_received, input_grad, mixed = lax.optimization_barrier(
            (last_received, input_grad, mixed)
        )
        last_total = scatter_end(last_own, last_received)
        last_blocks = rep_blocks(last_total, (up_res[0], down_res[0]))
        results = last_adam(
            place,
            last_blocks,
            (
                qkv_weight,
                qkv_first,
                qkv_second,
                out_weight,
                out_first,
                out_second,
                small_weights,
                small_first,
                small_second,
            ),
        )
        qkv_res, out_res, small_res = results[:3], results[3:6], results[6:]
    else:
        down_own = jnp.concatenate(in_order(rep_blocks(down_total), rep), axis=0).astype(F32)
        up_own = in_order(rep_blocks(up_total), rep)
        up_own = [g.reshape(owned, shards, units) for g in up_own]
        up_own = jnp.stack(up_own, axis=2).reshape(owned, ff).astype(F32)
        up_res = adam_update(up_weight, up_own, up_first, up_second, RATE_MATRIX)
        down_res = adam_update(down_weight, down_own, down_first, down_second, RATE_MATRIX)
        last_own = in_order(rep_blocks(last_total), rep)
        out_own = jnp.concatenate([g[:, 3 * part : 4 * part] for g in last_own], axis=1)
        qkv_own = [g[:, : 3 * part].reshape(owned, 3, part) for g in last_own]
        qkv_own = jnp.stack(qkv_own, axis=2).reshape(owned, 3 * width).astype(F32)
        small_own = sum(g[:, 4 * part : 4 * part + 12].astype(F32) for g in last_own).T
        qkv_res = adam_update(qkv_weight, qkv_own, qkv_first, qkv_second, RATE_MATRIX)
        out_res = adam_update(
            out_weight, out_own.astype(F32), out_first, out_second, RATE_MATRIX
        )
        small_res = adam_update(
            small_weights, small_own, small_first, small_second, RATE_SMALL
        )
    return (
        mixed,
        input_grad,
        qkv_res[0],
        out_res[0],
        up_res[0],
        down_res[0],
        small_res[0],
        qkv_res[1],
        out_res[1],
        up_res[1],
        down_res[1],
        small_res[1],
        qkv_res[2],
        out_res[2],
        up_res[2],
        down_res[2],
        small_res[2],
    )


def solution(mesh):
    tokens_spec = P(("rep", "shard"), None)
    rows = P("shard", None)
    columns = P(None, "shard")
    weights = (rows, rows, rows, rows, columns)
    return jax.shard_map(
        local,
        mesh=mesh,
        in_specs=(tokens_spec, tokens_spec, P(("rep", "shard"))) + weights * 3,
        out_specs=(tokens_spec, tokens_spec) + weights * 3,
        check_vma=False,
    )
```
